32 devices in a mesh: dp: 8 (over y, x, core), seq: 4 (over z).
Axes of the slice: x: 2, y: 2, z: 4, core: 2. Of those that a mesh axis runs over, the one named last changes fastest.
Arguments:
- tokens: bfloat16 [24, 1280, 640], P('dp', 'seq'), may hold values from -6 to 6
- cotangent: bfloat16 [24, 1280, 640], P('dp', 'seq'), may hold values from -6 to 6
- segments: int32 [24, 1280], P('dp'), may hold values from 0 to 1, as said below
- positions: int32 [24, 1280], P('dp', 'seq'), may hold values from 0 to 2558, as said below
- query_weight: float32 [1024, 640], P('dp'), may hold values from -0.25 to 0.25
- key_weight: float32 [256, 640], P('dp'), may hold values from -0.25 to 0.25
- value_weight: float32 [256, 640], P('dp'), may hold values from -0.25 to 0.25
- output_weight: float32 [640, 1024], P('dp'), may hold values from -0.75 to 0.75
- gate_weight: float32 [2048, 640], P('dp'), may hold values from -0.25 to 0.25
- up_weight: float32 [2048, 640], P('dp'), may hold values from -0.25 to 0.25
- down_weight: float32 [640, 2048], P('dp'), may hold values from -0.125 to 0.125
- norm_gains: float32 [3072], P('dp'), may hold values from -0.4 to 0.4
- query_first: float32 [1024, 640], P('dp'), may hold values from -112 to 112
- key_first: float32 [256, 640], P('dp'), may hold values from -112 to 112
- value_first: float32 [256, 640], P('dp'), may hold values from -112 to 112
- output_first: float32 [640, 1024], P('dp'), may hold values from -56 to 56
- gate_first: float32 [2048, 640], P('dp'), may hold values from -112 to 112
- up_first: float32 [2048, 640], P('dp'), may hold values from -112 to 112
- down_first: float32 [640, 2048], P('dp'), may hold values from -112 to 112
- gains_first: float32 [3072], P('dp'), may hold values from -160 to 160
- query_second: float32 [1024, 640], P('dp'), may hold values from 921.6 to 7680
- key_second: float32 [256, 640], P('dp'), may hold values from 921.6 to 7680
- value_second: float32 [256, 640], P('dp'), may hold values from 921.6 to 7680
- output_second: float32 [640, 1024], P('dp'), may hold values from 153.6 to 1228.8
- gate_second: float32 [2048, 640], P('dp'), may hold values from 921.6 to 7680
- up_second: float32 [2048, 640], P('dp'), may hold values from 921.6 to 7680
- down_second: float32 [640, 2048], P('dp'), may hold values from 921.6 to 7680
- gains_second: float32 [3072], P('dp'), may hold values from 1843.2 to 15360
Outputs:
- layer_output: bfloat16 [24, 1280, 640], P('dp', 'seq')
- input_grad: float32 [24, 1280, 640], P('dp', 'seq')
- query_momentum: float32 [1024, 640], P('dp')
- key_momentum: float32 [256, 640], P('dp')
- value_momentum: float32 [256, 640], P('dp')
- output_momentum: float32 [640, 1024], P('dp')
- gate_momentum: float32 [2048, 640], P('dp')
- up_momentum: float32 [2048, 640], P('dp')
- down_momentum: float32 [640, 2048], P('dp')
- gains_momentum: float32 [3072], P('dp')
- query_variance: float32 [1024, 640], P('dp')
- key_variance: float32 [256, 640], P('dp')
- value_variance: float32 [256, 640], P('dp')
- output_variance: float32 [640, 1024], P('dp')
- gate_variance: float32 [2048, 640], P('dp')
- up_variance: float32 [2048, 640], P('dp')
- down_variance: float32 [640, 2048], P('dp')
- gains_variance: float32 [3072], P('dp')
- query_updated: float32 [1024, 640], P('dp')
- key_updated: float32 [256, 640], P('dp')
- value_updated: float32 [256, 640], P('dp')
- output_updated: float32 [640, 1024], P('dp')
- gate_updated: float32 [2048, 640], P('dp')
- up_updated: float32 [2048, 640], P('dp')
- down_updated: float32 [640, 2048], P('dp')
- gains_updated: float32 [3072], P('dp')
The draws below stay inside these ranges and needn't reach their ends.
Inputs may be any that keep to these rules, and one draw needn't show every extreme that they name: `segments`: along each sequence the ids start at 0 and rise by one at the first token of each document. Of the 3 sequences on one index of dp, one, drawn from the seed, is a single document; each of the others holds exactly 2 documents of varying lengths. `positions`: at the first token of a document the position is 0; within a document it rises by 1 or 2 from one token to the next, and by 2 throughout in the sequences that are a single document.
All inputs are finite; a program needn't handle non-finite values.
Results may differ from the reference program's by a relative error of at most 0.025.
Values may be sent and summed in bfloat16 or wider, within the bound.
No kernel may reach another device: no remote copies, remote signals or barrier semaphores. Data moves between devices by JAX's collectives and lax.ppermute only.
A program may use at most 192 MiB of HBM per device.

```python
import math
import jax
import jax.numpy as jnp
from jax import lax

D = 640
H = 4
HD = 256
FF = 2048
WINDOW = 512
SEQS_DEV = 3
STEP = 10
SEQS = 24
LENGTH = 1280
DOCS = 2
TOKENS = 30720
GAINS = 3072


def document_layout(key):
    start_key, whole_key, step_key = jax.random.split(key, 3)
    columns = jnp.arange(LENGTH)[None, :]
    row_keys = jax.random.split(start_key, SEQS)
    cut_points = jax.vmap(lambda row_key: jax.random.permutation(row_key, LENGTH - 1)[:DOCS - 1] + 1)(row_keys)
    cut_begins = jnp.any(columns[:, None, :] == cut_points[:, :, None], axis=1)
    chosen = jax.random.randint(whole_key, (SEQS // SEQS_DEV,), 0, SEQS_DEV)
    single = jnp.arange(SEQS) % SEQS_DEV == jnp.repeat(chosen, SEQS_DEV)
    begins = cut_begins & jnp.logical_not(single)[:, None] | (columns == 0)
    segment_ids = jnp.cumsum(begins.astype(jnp.int32), axis=1) - 1
    increments = jax.random.randint(step_key, (SEQS, LENGTH), 1, 3)
    increments = jnp.where(single[:, None], 2, increments)
    before = jnp.cumsum(increments, axis=1) - increments
    anchor = lax.cummax(jnp.where(begins, before, 0), axis=1)
    return (segment_ids.astype(jnp.int32), (before - anchor).astype(jnp.int32))


def draw_segments(key, part):
    return document_layout(key)[0]


def draw_positions(key, part):
    return document_layout(key)[1]


def level_of(rng, dims, cuts, least, top_value):
    def one(position, shards_of):
        draws = jax.random.uniform(jax.random.fold_in(jax.random.fold_in(rng, 6), position), (shards_of,), jnp.float32, least / len(cuts), top_value / len(cuts))
        return jnp.repeat(jnp.exp(draws), dims[position] // shards_of).reshape((-1,) + (1,) * (len(dims) - position - 1))

    factor_of = one(*cuts[0])
    for cut in cuts[1:]:
        factor_of = factor_of * one(*cut)
    return factor_of


def bell_draw(rng, extent, spread, reach, pieces=(), kind=jnp.bfloat16):
    entries = spread * jax.random.normal(rng, extent, jnp.float32)
    if pieces:
        entries = entries * level_of(rng, extent, pieces, -0.22, 0.18)
    return jnp.clip(entries, -reach, reach).astype(kind)


def setup_inputs(seed: int = 0) -> dict:
    keys = jax.random.split(jax.random.key(seed), 29)
    tokens = bell_draw(keys[0], (SEQS, LENGTH, D), 1.0, 6.0, ((0, 8), (1, 4)))
    cotangent = bell_draw(keys[1], (SEQS, LENGTH, D), 1.0, 6.0, ((0, 8), (1, 4)))
    segments = draw_segments(jax.random.fold_in(keys[28], 71), 0)
    positions = draw_positions(jax.random.fold_in(keys[28], 71), 0)
    query_weight = bell_draw(keys[4], (H * HD, D), D ** -0.5, 0.25, ((0, 8),), jnp.float32)
    key_weight = bell_draw(keys[5], (HD, D), D ** -0.5, 0.25, ((0, 8),), jnp.float32)
    value_weight = bell_draw(keys[6], (HD, D), D ** -0.5, 0.25, ((0, 8),), jnp.float32)
    output_weight = bell_draw(keys[7], (D, H * HD), (H * HD // 16) ** -0.5, 0.75, ((0, 8),), jnp.float32)
    gate_weight = bell_draw(keys[8], (FF, D), D ** -0.5, 0.25, ((0, 8),), jnp.float32)
    up_weight = bell_draw(keys[9], (FF, D), D ** -0.5, 0.25, ((0, 8),), jnp.float32)
    down_weight = bell_draw(keys[10], (D, FF), FF ** -0.5, 0.125, ((0, 8),), jnp.float32)
    norm_gains = bell_draw(keys[11], (GAINS,), 0.1, 0.4, ((0, 8),), jnp.float32)
    query_first = bell_draw(keys[12], (H * HD, D), (0.11 * TOKENS ** 0.5), 112.0, ((0, 8),), jnp.float32)
    key_first = bell_draw(keys[13], (HD, D), (0.11 * TOKENS ** 0.5), 112.0, ((0, 8),), jnp.float32)
    value_first = bell_draw(keys[14], (HD, D), (0.11 * TOKENS ** 0.5), 112.0, ((0, 8),), jnp.float32)
    output_first = bell_draw(keys[15], (D, H * HD), (0.05 * TOKENS ** 0.5), 56.0, ((0, 8),), jnp.float32)
    gate_first = bell_draw(keys[16], (FF, D), (0.11 * TOKENS ** 0.5), 112.0, ((0, 8),), jnp.float32)
    up_first = bell_draw(keys[17], (FF, D), (0.11 * TOKENS ** 0.5), 112.0, ((0, 8),), jnp.float32)
    down_first = bell_draw(keys[18], (D, FF), (0.11 * TOKENS ** 0.5), 112.0, ((0, 8),), jnp.float32)
    gains_first = bell_draw(keys[19], (GAINS,), (0.15 * TOKENS ** 0.5), 160.0, ((0, 8),), jnp.float32)
    query_second = jnp.clip(jnp.exp(math.log(7680.0) - 2.1202636 * jax.random.uniform(keys[20], (H * HD, D), jnp.float32) ** level_of(keys[20], (H * HD, D), ((0, 8),), -0.2, 0.2)), 921.6, 7680.0)
    key_second = jnp.clip(jnp.exp(math.log(7680.0) - 2.1202636 * jax.random.uniform(keys[21], (HD, D), jnp.float32) ** level_of(keys[21], (HD, D), ((0, 8),), -0.2, 0.2)), 921.6, 7680.0)
    value_second = jnp.clip(jnp.exp(math.log(7680.0) - 2.1202636 * jax.random.uniform(keys[22], (HD, D), jnp.float32) ** level_of(keys[22], (HD, D), ((0, 8),), -0.2, 0.2)), 921.6, 7680.0)
    output_second = jnp.clip(jnp.exp(math.log(1228.8) - 2.0794415 * jax.random.uniform(keys[23], (D, H * HD), jnp.float32) ** level_of(keys[23], (D, H * HD), ((0, 8),), -0.2, 0.2)), 153.6, 1228.8)
    gate_second = jnp.clip(jnp.exp(math.log(7680.0) - 2.1202636 * jax.random.uniform(keys[24], (FF, D), jnp.float32) ** level_of(keys[24], (FF, D), ((0, 8),), -0.2, 0.2)), 921.6, 7680.0)
    up_second = jnp.clip(jnp.exp(math.log(7680.0) - 2.1202636 * jax.random.uniform(keys[25], (FF, D), jnp.float32) ** level_of(keys[25], (FF, D), ((0, 8),), -0.2, 0.2)), 921.6, 7680.0)
    down_second = jnp.clip(jnp.exp(math.log(7680.0) - 2.1202636 * jax.random.uniform(keys[26], (D, FF), jnp.float32) ** level_of(keys[26], (D, FF), ((0, 8),), -0.2, 0.2)), 921.6, 7680.0)
    gains_second = jnp.clip(jnp.exp(math.log(15360.0) - 2.1202636 * jax.random.uniform(keys[27], (GAINS,), jnp.float32) ** level_of(keys[27], (GAINS,), ((0, 8),), -0.2, 0.2)), 1843.2, 15360.0)
    return {"tokens": tokens, "cotangent": cotangent, "segments": segments, "positions": positions, "query_weight": query_weight, "key_weight": key_weight, "value_weight": value_weight, "output_weight": output_weight, "gate_weight": gate_weight, "up_weight": up_weight, "down_weight": down_weight, "norm_gains": norm_gains, "query_first": query_first, "key_first": key_first, "value_first": value_first, "output_first": output_first, "gate_first": gate_first, "up_first": up_first, "down_first": down_first, "gains_first": gains_first, "query_second": query_second, "key_second": key_second, "value_second": value_second, "output_second": output_second, "gate_second": gate_second, "up_second": up_second, "down_second": down_second, "gains_second": gains_second}


NORM_EPSILON = 1e-06
ROPE_BASE = 10000.0
LEARN_RATE = 0.08
BETA_FIRST = 0.9
BETA_SECOND = 0.95
ADAM_EPSILON = 1e-08
WEIGHT_DECAY = 0.01
MASKED_SCORE = -1000000000.0

@jax.custom_vjp
def low(v):
    return lax.optimization_barrier(v.astype(jnp.bfloat16)).astype(jnp.float32)

@jax.custom_vjp
def low_back(v):
    return v

def low_keep(v):
    return (low(v), None)

def low_pass(kept, grad):
    return (grad,)

def back_keep(v):
    return (v, None)

def back_low(kept, grad):
    return (low(grad),)
low.defvjp(low_keep, low_pass)
low_back.defvjp(back_keep, back_low)

def rms_scale(values, gain_vector):
    mean_square = lax.optimization_barrier(jnp.mean(values * values, axis=-1, keepdims=True))
    return values * lax.rsqrt(mean_square + NORM_EPSILON) * (1.0 + gain_vector)

def rotate(values, angles):
    midpoint = values.shape[-1] // 2
    leading = values[..., :midpoint]
    trailing = values[..., midpoint:]
    cosine = jnp.cos(angles)
    sine_part = jnp.sin(angles)
    return jnp.concatenate([leading * cosine - trailing * sine_part, trailing * cosine + leading * sine_part], axis=-1)

def frequencies(size):
    return ROPE_BASE ** (-2.0 * jnp.arange(size // 2).astype(jnp.float32) / size)

def project(inputs, weight):
    return jnp.dot(inputs, weight.T, precision=lax.Precision.HIGHEST, preferred_element_type=jnp.float32)

def gated_gelu(gate_values, up_values):
    return jax.nn.gelu(gate_values, approximate=True) * up_values

def sequence_forward(params, inputs):
    w_query, w_key, w_value, w_output, w_gate, w_up, w_down, gains_all = params
    token_rows, seq_ids, seq_positions = inputs
    g_input = gains_all[0:D]
    g_attn = gains_all[D:2 * D]
    g_pre = gains_all[2 * D:3 * D]
    g_ffn = gains_all[3 * D:4 * D]
    g_query = gains_all[4 * D:4 * D + HD]
    g_key = gains_all[4 * D + HD:4 * D + 2 * HD]
    normed = low(rms_scale(token_rows, g_input))
    query_raw = low_back(project(normed, w_query)).reshape(LENGTH, H, HD)
    key_raw = low_back(project(normed, w_key))
    value_vectors = low_back(low(project(normed, w_value)))
    angles = seq_positions.astype(jnp.float32)[:, None] * frequencies(HD)[None, :]
    query_vectors = low(rotate(rms_scale(query_raw, g_query), angles[:, None, :]))
    key_vectors = low(rotate(rms_scale(key_raw, g_key), angles))
    scores = jnp.einsum('qhd,kd->hqk', query_vectors, key_vectors, precision=lax.Precision.HIGHEST) * HD ** (-0.5)
    scores = low_back(scores)
    token_index = jnp.arange(LENGTH)
    allowed = (seq_ids[:, None] == seq_ids[None, :]) & (token_index[None, :] <= token_index[:, None]) & (token_index[:, None] - token_index[None, :] < WINDOW)
    masked = jnp.where(allowed[None], scores, MASKED_SCORE)
    row_peak = lax.optimization_barrier(jnp.max(masked, axis=-1, keepdims=True))
    exponent = jnp.exp(masked - row_peak)
    soft_weights = low(exponent / lax.optimization_barrier(jnp.sum(exponent, axis=-1, keepdims=True)))
    mixed = jnp.einsum('hqk,kd->qhd', soft_weights, value_vectors, precision=lax.Precision.HIGHEST).reshape(LENGTH, H * HD)
    mixed = low_back(low(mixed))
    attended = low_back(project(mixed, w_output))
    hidden = token_rows + rms_scale(attended, g_attn)
    pre_normed = low(rms_scale(hidden, g_pre))
    gate_values = low_back(project(pre_normed, w_gate))
    up_values = low_back(project(pre_normed, w_up))
    product = low(gated_gelu(gate_values, up_values))
    down_values = low_back(project(product, w_down))
    return hidden + rms_scale(down_values, g_ffn)

def adam_step(weight, first_moment, second_moment, gradient, decay_rate):
    momentum = BETA_FIRST * first_moment + (1.0 - BETA_FIRST) * gradient
    variance = BETA_SECOND * second_moment + (1.0 - BETA_SECOND) * gradient * gradient
    corrected = momentum / (1.0 - BETA_FIRST ** STEP)
    scaled = variance / (1.0 - BETA_SECOND ** STEP)
    updated = weight - LEARN_RATE * (corrected / (jnp.sqrt(scaled) + ADAM_EPSILON) + decay_rate * weight)
    return (momentum, variance, updated)

def reference(tokens, cotangent, segments, positions, query_weight, key_weight, value_weight, output_weight, gate_weight, up_weight, down_weight, norm_gains, query_first, key_first, value_first, output_first, gate_first, up_first, down_first, gains_first, query_second, key_second, value_second, output_second, gate_second, up_second, down_second, gains_second):
    masters = (query_weight, key_weight, value_weight, output_weight, gate_weight, up_weight, down_weight, norm_gains)
    firsts = (query_first, key_first, value_first, output_first, gate_first, up_first, down_first, gains_first)
    seconds = (query_second, key_second, value_second, output_second, gate_second, up_second, down_second, gains_second)
    params = tuple((lax.optimization_barrier(master.astype(jnp.bfloat16)).astype(jnp.float32) for master in masters))

    def forward(layer_params, token_rows):

        def one_sequence(inputs):
            return sequence_forward(layer_params, inputs)
        return lax.map(jax.checkpoint(one_sequence), (token_rows, segments, positions))
    outputs, pullback = jax.vjp(forward, params, tokens.astype(jnp.float32))
    gradients, input_grad = pullback(cotangent.astype(jnp.float32))
    results = [adam_step(masters[member], firsts[member], seconds[member], gradients[member], WEIGHT_DECAY if member < 7 else 0.0) for member in range(8)]
    query_momentum, query_variance, query_updated = results[0]
    key_momentum, key_variance, key_updated = results[1]
    value_momentum, value_variance, value_updated = results[2]
    output_momentum, output_variance, output_updated = results[3]
    gate_momentum, gate_variance, gate_updated = results[4]
    up_momentum, up_variance, up_updated = results[5]
    down_momentum, down_variance, down_updated = results[6]
    gains_momentum, gains_variance, gains_updated = results[7]
    return (outputs.astype(jnp.bfloat16), input_grad, query_momentum, key_momentum, value_momentum, output_momentum, gate_momentum, up_momentum, down_momentum, gains_momentum, query_variance, key_variance, value_variance, output_variance, gate_variance, up_variance, down_variance, gains_variance, query_updated, key_updated, value_updated, output_updated, gate_updated, up_updated, down_updated, gains_updated)
```

```python
import jax
import jax.numpy as jnp
from jax import lax
from jax.sharding import PartitionSpec as P

WINDOW = 512
STEP = 10


NORM_EPSILON = 1e-06
ROPE_BASE = 10000.0
LEARN_RATE = 0.08
BETA_FIRST = 0.9
BETA_SECOND = 0.95
ADAM_EPSILON = 1e-08
WEIGHT_DECAY = 0.01
MASKED_SCORE = -1000000000.0


def rms_scale(values, gain_vector):
    mean_square = jnp.mean(values * values, axis=-1, keepdims=True)
    return values * lax.rsqrt(mean_square + NORM_EPSILON) * (1.0 + gain_vector)


def rotate(values, angles):
    midpoint = values.shape[-1] // 2
    leading = values[..., :midpoint]
    trailing = values[..., midpoint:]
    cosine = jnp.cos(angles)
    sine_part = jnp.sin(angles)
    return jnp.concatenate(
        [leading * cosine - trailing * sine_part, trailing * cosine + leading * sine_part], axis=-1
    )


def frequencies(size):
    return ROPE_BASE ** (-2.0 * jnp.arange(size // 2).astype(jnp.float32) / size)


def project(inputs, weight):
    return lax.dot_general(
        inputs, weight, (((1,), (1,)), ((), ())), preferred_element_type=jnp.float32
    )


def backward_input(gradients, weight):
    return jnp.dot(gradients, weight, preferred_element_type=jnp.float32)


def weight_grad(gradients, inputs):
    return lax.dot_general(
        gradients, inputs, (((0,), (0,)), ((), ())), preferred_element_type=jnp.float32
    )


def gated_gelu(gate_values, up_values):
    return jax.nn.gelu(gate_values, approximate=True) * up_values


def adam_step(weight, first_moment, second_moment, gradient, decay_rate):
    momentum = BETA_FIRST * first_moment + (1.0 - BETA_FIRST) * gradient
    variance = BETA_SECOND * second_moment + (1.0 - BETA_SECOND) * gradient * gradient
    corrected = momentum / (1.0 - BETA_FIRST**STEP)
    scaled = variance / (1.0 - BETA_SECOND**STEP)
    updated = weight - LEARN_RATE * (
        corrected / (jnp.sqrt(scaled) + ADAM_EPSILON) + decay_rate * weight
    )
    return (momentum, variance, updated)


def dp_bits():
    return (lax.axis_size("dp") - 1).bit_length()


def gather_rows(shard, order):
    count = lax.axis_size("dp")
    index = lax.axis_index("dp")
    current = shard
    for bit in order:
        received = lax.ppermute(current, "dp", [(i, i ^ (1 << bit)) for i in range(count)])
        upper = ((index >> bit) & 1) == 1
        current = jnp.stack(
            [jnp.where(upper, received, current), jnp.where(upper, current, received)]
        )
    done = list(reversed(order))
    lead = [done.index(bit) for bit in sorted(done, reverse=True)]
    current = current.transpose(lead + [len(done), len(done) + 1])
    return current.reshape((count,) + shard.shape)


def scatter_rows(total, order):
    count = lax.axis_size("dp")
    index = lax.axis_index("dp")
    bits = len(order)
    rows = total.shape[0] // count
    current = total.astype(jnp.bfloat16).reshape((2,) * bits + (rows, total.shape[1]))
    left = list(range(bits - 1, -1, -1))
    for bit in order:
        axis = left.index(bit)
        left.remove(bit)
        mine = (index >> bit) & 1
        keep = lax.dynamic_index_in_dim(current, mine, axis, keepdims=False)
        send = lax.dynamic_index_in_dim(current, 1 - mine, axis, keepdims=False)
        received = lax.ppermute(send, "dp", [(i, i ^ (1 << bit)) for i in range(count)])
        current = (keep.astype(jnp.float32) + received.astype(jnp.float32)).astype(jnp.bfloat16)
    return current


def seq_sum(part):
    count = lax.axis_size("seq")
    index = lax.axis_index("seq")
    half = count // 2
    current = part

    def add(received):
        return (current.astype(jnp.float32) + received.astype(jnp.float32)).astype(jnp.bfloat16)

    for t in range(half - 1):
        pairs = [(t, t + 1), (count - 1 - t, count - 2 - t)]
        current = add(lax.ppermute(current, "seq", pairs))
    current = add(lax.ppermute(current, "seq", [(half - 1, half), (half, half - 1)]))
    for t in range(half - 2, -1, -1):
        pairs = [(t + 1, t), (count - 2 - t, count - 1 - t)]
        received = lax.ppermute(current, "seq", pairs)
        outer = (index == t) | (index == count - 1 - t)
        current = jnp.where(outer, received, current)
    return current.astype(jnp.float32)


def body(
    tokens,
    cotangent,
    segments,
    positions,
    query_weight,
    key_weight,
    value_weight,
    output_weight,
    gate_weight,
    up_weight,
    down_weight,
    norm_gains,
    query_first,
    key_first,
    value_first,
    output_first,
    gate_first,
    up_first,
    down_first,
    gains_first,
    query_second,
    key_second,
    value_second,
    output_second,
    gate_second,
    up_second,
    down_second,
    gains_second,
):
    bits = dp_bits()
    order_a = list(range(1, bits)) + [0]
    order_b = list(range(bits - 1, 0, -1)) + [0]
    key_rows = key_weight.shape[0]
    gain_rows = norm_gains.shape[0]
    low = jnp.bfloat16
    width = tokens.shape[2]
    pad_rows = 16
    gain_block = jnp.pad(norm_gains.astype(low)[None], ((0, pad_rows - 1), (0, width - gain_rows)))
    key_value_gain = jnp.concatenate([key_weight.astype(low), value_weight.astype(low), gain_block])
    w_query = gather_rows(query_weight.astype(low), order_a).reshape(-1, width)
    kvg = gather_rows(key_value_gain, order_b)
    w_key = kvg[:, :key_rows].reshape(-1, width)
    w_value = kvg[:, key_rows : 2 * key_rows].reshape(-1, width)
    gains_all = kvg[:, 2 * key_rows, :gain_rows].reshape(-1)
    w_output = gather_rows(output_weight.astype(low), order_a).reshape(-1, output_weight.shape[1])
    w_gate = gather_rows(gate_weight.astype(low), order_a).reshape(-1, width)
    w_up = gather_rows(up_weight.astype(low), order_b).reshape(-1, width)
    w_down = gather_rows(down_weight.astype(low), order_b).reshape(-1, down_weight.shape[1])
    seq_count, seq_rows, model_width = tokens.shape
    head_size = w_key.shape[0]
    head_count = w_query.shape[0] // head_size
    halo_rows = WINDOW
    far_rows = WINDOW - seq_rows
    shards = lax.axis_size("seq")
    window_rows = halo_rows + seq_rows
    score_scale = head_size ** (-0.5)
    gains_float = gains_all.astype(jnp.float32)
    g_input = gains_float[0:model_width]
    g_attn = gains_float[model_width : 2 * model_width]
    g_pre = gains_float[2 * model_width : 3 * model_width]
    g_ffn = gains_float[3 * model_width : 4 * model_width]
    g_query = gains_float[4 * model_width : 4 * model_width + head_size]
    g_key = gains_float[4 * model_width + head_size : 4 * model_width + 2 * head_size]
    first_row = lax.axis_index("seq") * seq_rows
    token_rows = tokens.reshape(seq_count * seq_rows, model_width).astype(jnp.float32)
    normed_low = rms_scale(token_rows, g_input).astype(jnp.bfloat16)
    query_raw = project(normed_low, w_query).reshape(-1, head_count, head_size)
    key_raw = project(normed_low, w_key)
    value_low = project(normed_low, w_value).astype(jnp.bfloat16)
    angles = positions.reshape(-1).astype(jnp.float32)[:, None] * frequencies(head_size)[None, :]

    def query_finish(raw_values, gain_vector):
        return rotate(rms_scale(raw_values, gain_vector), angles[:, None, :])

    def key_finish(raw_values, gain_vector):
        return rotate(rms_scale(raw_values, gain_vector), angles)

    query_low = (
        query_finish(query_raw, g_query)
        .astype(jnp.bfloat16)
        .reshape(seq_count, seq_rows, head_count, head_size)
    )
    key_own = (
        key_finish(key_raw, g_key).astype(jnp.bfloat16).reshape(seq_count, seq_rows, head_size)
    )
    value_own = value_low.reshape(seq_count, seq_rows, head_size)
    pair_own = jnp.concatenate([key_own, value_own], axis=-1)
    upward = [(i, i + 1) for i in range(shards - 1)]
    pair_near = lax.ppermute(pair_own, "seq", upward)
    pair_far = lax.ppermute(pair_near[:, seq_rows - far_rows :], "seq", upward[1:])
    pair_window = jnp.concatenate([pair_far, pair_near, pair_own], axis=1)
    key_window = pair_window[..., :head_size]
    value_window = pair_window[..., head_size:]
    padded_ids = jnp.concatenate(
        [jnp.full((seq_count, halo_rows), -1, jnp.int32), segments], axis=1
    )
    key_ids = lax.dynamic_slice_in_dim(padded_ids, first_row, window_rows, 1)
    query_ids = lax.dynamic_slice_in_dim(segments, first_row, seq_rows, 1)
    row_index = jnp.arange(seq_rows)[:, None]
    column_index = jnp.arange(window_rows)[None, :]
    band = (column_index > row_index) & (column_index <= row_index + halo_rows)
    allowed = (query_ids[:, :, None] == key_ids[:, None, :]) & band[None]

    def scores_of(query_block, key_block, allowed_block):
        scores = (
            jnp.einsum("shd,kd->hsk", query_block, key_block, preferred_element_type=jnp.float32)
            * score_scale
        )
        return jnp.where(allowed_block[None], scores, MASKED_SCORE)

    def attend(operands):
        query_block, key_block, value_block, allowed_block = operands
        scores = scores_of(query_block, key_block, allowed_block)
        row_peak = jnp.max(scores, axis=-1, keepdims=True)
        exponent = jnp.exp(scores - row_peak)
        row_total = jnp.sum(exponent, axis=-1, keepdims=True)
        soft_low = (exponent / row_total).astype(jnp.bfloat16)
        mixed_block = jnp.einsum(
            "hsk,kd->shd", soft_low, value_block, preferred_element_type=jnp.float32
        )
        return (mixed_block, (row_peak + jnp.log(row_total))[..., 0])

    mixed_all, log_totals = lax.map(attend, (query_low, key_window, value_window, allowed))
    mixed_low = mixed_all.reshape(-1, head_count * head_size).astype(jnp.bfloat16)
    attended = project(mixed_low, w_output)
    hidden = token_rows + rms_scale(attended, g_attn)
    pre_low = rms_scale(hidden, g_pre).astype(jnp.bfloat16)
    gate_values = project(pre_low, w_gate)
    up_values = project(pre_low, w_up)
    product_low = gated_gelu(gate_values, up_values).astype(jnp.bfloat16)
    down_values = project(product_low, w_down)
    layer_output = (
        (hidden + rms_scale(down_values, g_ffn)).astype(jnp.bfloat16).reshape(tokens.shape)
    )
    grad_out = cotangent.reshape(-1, model_width).astype(jnp.float32)
    _, final_back = jax.vjp(rms_scale, down_values, g_ffn)
    grad_down, grad_g_ffn = final_back(grad_out)
    grad_down_low = grad_down.astype(jnp.bfloat16)
    grad_w_down = weight_grad(grad_down_low, product_low)
    grad_product = backward_input(grad_down_low, w_down)
    _, gelu_back = jax.vjp(gated_gelu, gate_values, up_values)
    grad_gate, grad_up = gelu_back(grad_product)
    grad_gate_low = grad_gate.astype(jnp.bfloat16)
    grad_up_low = grad_up.astype(jnp.bfloat16)
    grad_w_gate = weight_grad(grad_gate_low, pre_low)
    grad_w_up = weight_grad(grad_up_low, pre_low)
    grad_pre = backward_input(grad_gate_low, w_gate) + backward_input(grad_up_low, w_up)
    _, pre_back = jax.vjp(rms_scale, hidden, g_pre)
    grad_hidden_part, grad_g_pre = pre_back(grad_pre)
    grad_hidden = grad_out + grad_hidden_part
    _, post_back = jax.vjp(rms_scale, attended, g_attn)
    grad_attended, grad_g_attn = post_back(grad_hidden)
    grad_attended_low = grad_attended.astype(jnp.bfloat16)
    grad_w_output = weight_grad(grad_attended_low, mixed_low)
    grad_mixed_low = (
        backward_input(grad_attended_low, w_output)
        .astype(jnp.bfloat16)
        .reshape(seq_count, seq_rows, head_count, head_size)
    )

    def attend_back(operands):
        query_block, key_block, value_block, allowed_block, log_block, grad_block = operands
        scores = scores_of(query_block, key_block, allowed_block)
        soft_weights = jnp.exp(scores - log_block[..., None])
        soft_low = soft_weights.astype(jnp.bfloat16)
        grad_soft = jnp.einsum(
            "shd,kd->hsk", grad_block, value_block, preferred_element_type=jnp.float32
        )
        row_dot = jnp.sum(soft_weights * grad_soft, axis=-1, keepdims=True)
        grad_scores = (soft_weights * (grad_soft - row_dot)).astype(jnp.bfloat16)
        grad_query = (
            jnp.einsum("hsk,kd->shd", grad_scores, key_block, preferred_element_type=jnp.float32)
            * score_scale
        )
        grad_key = (
            jnp.einsum("hsk,shd->kd", grad_scores, query_block, preferred_element_type=jnp.float32)
            * score_scale
        )
        grad_value = jnp.einsum(
            "hsk,shd->kd", soft_low, grad_block, preferred_element_type=jnp.float32
        )
        return (grad_query, grad_key, grad_value)

    grad_query_all, grad_key_window, grad_value_window = lax.map(
        attend_back, (query_low, key_window, value_window, allowed, log_totals, grad_mixed_low)
    )
    pair_grad = jnp.concatenate([grad_key_window, grad_value_window], axis=-1)
    downward = [(i + 1, i) for i in range(shards - 1)]
    from_far = lax.ppermute(pair_grad[:, :far_rows].astype(low), "seq", downward[1:])
    near_sum = pair_grad[:, far_rows:halo_rows] + jnp.pad(
        from_far.astype(jnp.float32), ((0, 0), (seq_rows - far_rows, 0), (0, 0))
    )
    from_near = lax.ppermute(near_sum.astype(low), "seq", downward)
    pair_total = pair_grad[:, halo_rows:] + from_near.astype(jnp.float32)
    key_grad_own = pair_total[..., :head_size]
    value_grad_own = pair_total[..., head_size:]
    _, query_back = jax.vjp(query_finish, query_raw, g_query)
    grad_query_raw, grad_g_query = query_back(grad_query_all.reshape(-1, head_count, head_size))
    _, key_back = jax.vjp(key_finish, key_raw, g_key)
    grad_key_raw, grad_g_key = key_back(key_grad_own.reshape(-1, head_size))
    grad_query_low = grad_query_raw.reshape(-1, head_count * head_size).astype(jnp.bfloat16)
    grad_key_low = grad_key_raw.astype(jnp.bfloat16)
    grad_value_low = value_grad_own.reshape(-1, head_size).astype(jnp.bfloat16)
    grad_w_query = weight_grad(grad_query_low, normed_low)
    grad_w_key = weight_grad(grad_key_low, normed_low)
    grad_w_value = weight_grad(grad_value_low, normed_low)
    grad_normed = (
        backward_input(grad_query_low, w_query)
        + backward_input(grad_key_low, w_key)
        + backward_input(grad_value_low, w_value)
    )
    _, input_back = jax.vjp(rms_scale, token_rows, g_input)
    grad_rows_part, grad_g_input = input_back(grad_normed)
    input_grad = (grad_hidden + grad_rows_part).reshape(tokens.shape)
    grad_gains = jnp.concatenate(
        [grad_g_input, grad_g_attn, grad_g_pre, grad_g_ffn, grad_g_query, grad_g_key]
    )
    count = lax.axis_size("dp")
    back_a = [0] + order_a[:-1]
    back_b = [0] + order_b[:-1]
    gate_total = seq_sum(scatter_rows(grad_w_gate, back_a))
    up_total = seq_sum(scatter_rows(grad_w_up, back_b))
    down_total = seq_sum(scatter_rows(grad_w_down, back_b))
    output_total = seq_sum(scatter_rows(grad_w_output, back_a))
    query_total = seq_sum(scatter_rows(grad_w_query, back_a))
    gain_grad_block = jnp.pad(
        grad_gains.astype(low).reshape(count, 1, gain_rows),
        ((0, 0), (0, pad_rows - 1), (0, width - gain_rows)),
    )
    kvg_grad = jnp.concatenate(
        [
            grad_w_key.astype(low).reshape(count, key_rows, width),
            grad_w_value.astype(low).reshape(count, key_rows, width),
            gain_grad_block,
        ],
        axis=1,
    ).reshape(-1, width)
    kvg_total = seq_sum(scatter_rows(kvg_grad, back_b))
    key_total = kvg_total[:key_rows]
    value_total = kvg_total[key_rows : 2 * key_rows]
    gains_total = kvg_total[2 * key_rows, :gain_rows]
    query_momentum, query_variance, query_updated = adam_step(
        query_weight, query_first, query_second, query_total, WEIGHT_DECAY
    )
    key_momentum, key_variance, key_updated = adam_step(
        key_weight, key_first, key_second, key_total, WEIGHT_DECAY
    )
    value_momentum, value_variance, value_updated = adam_step(
        value_weight, value_first, value_second, value_total, WEIGHT_DECAY
    )
    output_momentum, output_variance, output_updated = adam_step(
        output_weight, output_first, output_second, output_total, WEIGHT_DECAY
    )
    gate_momentum, gate_variance, gate_updated = adam_step(
        gate_weight, gate_first, gate_second, gate_total, WEIGHT_DECAY
    )
    up_momentum, up_variance, up_updated = adam_step(
        up_weight, up_first, up_second, up_total, WEIGHT_DECAY
    )
    down_momentum, down_variance, down_updated = adam_step(
        down_weight, down_first, down_second, down_total, WEIGHT_DECAY
    )
    gains_momentum, gains_variance, gains_updated = adam_step(
        norm_gains, gains_first, gains_second, gains_total, 0.0
    )
    return (
        layer_output,
        input_grad,
        query_momentum,
        key_momentum,
        value_momentum,
        output_momentum,
        gate_momentum,
        up_momentum,
        down_momentum,
        gains_momentum,
        query_variance,
        key_variance,
        value_variance,
        output_variance,
        gate_variance,
        up_variance,
        down_variance,
        gains_variance,
        query_updated,
        key_updated,
        value_updated,
        output_updated,
        gate_updated,
        up_updated,
        down_updated,
        gains_updated,
    )


def solution(mesh):
    return jax.shard_map(
        body,
        mesh=mesh,
        in_specs=(
            P("dp", "seq", None),
            P("dp", "seq", None),
            P("dp", None),
            P("dp", "seq"),
            P("dp", None),
            P("dp", None),
            P("dp", None),
            P("dp", None),
            P("dp", None),
            P("dp", None),
            P("dp", None),
            P("dp"),
            P("dp", None),
            P("dp", None),
            P("dp", None),
            P("dp", None),
            P("dp", None),
            P("dp", None),
            P("dp", None),
            P("dp"),
            P("dp", None),
            P("dp", None),
            P("dp", None),
            P("dp", None),
            P("dp", None),
            P("dp", None),
            P("dp", None),
            P("dp"),
        ),
        out_specs=(
            P("dp", "seq", None),
            P("dp", "seq", None),
            P("dp", None),
            P("dp", None),
            P("dp", None),
            P("dp", None),
            P("dp", None),
            P("dp", None),
            P("dp", None),
            P("dp"),
            P("dp", None),
            P("dp", None),
            P("dp", None),
            P("dp", None),
            P("dp", None),
            P("dp", None),
            P("dp", None),
            P("dp"),
            P("dp", None),
            P("dp", None),
            P("dp", None),
            P("dp", None),
            P("dp", None),
            P("dp", None),
            P("dp", None),
            P("dp"),
        ),
        check_vma=False,
    )
```

```python
import functools
import math

import jax
import jax.numpy as jnp
from jax import lax
from jax.experimental import pallas as pl
from jax.experimental.pallas import tpu as pltpu
from jax.sharding import PartitionSpec as P

WINDOW = 512
STEP = 10


NORM_EPSILON = 1e-06
ROPE_BASE = 10000.0
LEARN_RATE = 0.08
BETA_FIRST = 0.9
BETA_SECOND = 0.95
ADAM_EPSILON = 1e-08
WEIGHT_DECAY = 0.01
MASKED_SCORE = -1000000000.0


def frequencies(size):
    return ROPE_BASE ** (-2.0 * jnp.arange(size // 2).astype(jnp.float32) / size)


def weight_grad(gradients, inputs):
    return lax.dot_general(
        gradients, inputs, (((0,), (0,)), ((), ())), preferred_element_type=jnp.float32
    )


def adam_step(weight, first_moment, second_moment, gradient, decay_rate):
    momentum = BETA_FIRST * first_moment + (1.0 - BETA_FIRST) * gradient
    variance = BETA_SECOND * second_moment + (1.0 - BETA_SECOND) * gradient * gradient
    corrected = momentum / (1.0 - BETA_FIRST**STEP)
    scaled = variance / (1.0 - BETA_SECOND**STEP)
    updated = weight - LEARN_RATE * (
        corrected / (jnp.sqrt(scaled) + ADAM_EPSILON) + decay_rate * weight
    )
    return (momentum, variance, updated)


VMEM_BYTES = 56 * 1024 * 1024


def kernel_params():
    return pltpu.CompilerParams(
        dimension_semantics=("arbitrary",), vmem_limit_bytes=VMEM_BYTES
    )


def per_seq(*tail):
    return pl.BlockSpec((1,) + tail, lambda s: (s,) + (0,) * len(tail))


def whole(*shape):
    return pl.BlockSpec(shape, lambda s: (0,) * len(shape), pipeline_mode=pl.Buffered(1))


def dot_nt(a, b):
    return lax.dot_general(a, b, (((1,), (1,)), ((), ())), preferred_element_type=jnp.float32)


def dot_nn(a, b):
    return lax.dot_general(a, b, (((1,), (0,)), ((), ())), preferred_element_type=jnp.float32)


def dot_tn(a, b):
    return lax.dot_general(a, b, (((0,), (0,)), ((), ())), preferred_element_type=jnp.float32)


def inverse_rms(values):
    return lax.rsqrt(jnp.mean(values * values, axis=-1, keepdims=True) + NORM_EPSILON)


def rms_back(values, gain, grad):
    inverse = inverse_rms(values)
    unit = values * inverse
    scaled = grad * (1.0 + gain)
    return (
        inverse * (scaled - unit * jnp.mean(unit * scaled, axis=-1, keepdims=True)),
        jnp.sum(grad * unit, axis=0, keepdims=True),
    )


def turn(values, cosine, sine):
    half = values.shape[-1] // 2
    first, second = values[:, :half], values[:, half:]
    return jnp.concatenate(
        [first * cosine - second * sine, second * cosine + first * sine], axis=-1
    )


def stack_heads(values, heads):
    return jnp.concatenate([values] * heads, axis=0)


def project_kernel(
    heads, x_ref, cos_ref, sin_ref, wq_ref, wk_ref, wv_ref, gi_ref, gq_ref, gk_ref,
    normed_ref, q_ref, qraw_ref, kv_ref, kraw_ref,
):
    x = x_ref[0].astype(jnp.float32)
    size = wk_ref.shape[0]
    rows = x.shape[0]
    part = rows // 2
    normed = (x * inverse_rms(x) * (1.0 + gi_ref[...])).astype(jnp.bfloat16)
    normed_ref[0] = normed
    cosine, sine = cos_ref[0], sin_ref[0]
    k_raw = dot_nt(normed, wk_ref[...])
    kraw_ref[0] = k_raw.astype(jnp.bfloat16)
    key = turn(k_raw * inverse_rms(k_raw) * (1.0 + gk_ref[...]), cosine, sine)
    kv_ref[0, :, :size] = key.astype(jnp.bfloat16)
    kv_ref[0, :, size:] = dot_nt(normed, wv_ref[...]).astype(jnp.bfloat16)
    for head in range(heads):
        raw = dot_nt(normed, wq_ref[head * size : (head + 1) * size, :])
        query = turn(raw * inverse_rms(raw) * (1.0 + gq_ref[...]), cosine, sine)
        query = (query * size ** (-0.5)).astype(jnp.bfloat16)
        raw = raw.astype(jnp.bfloat16)
        for t in range(2):
            span = slice(head * part, (head + 1) * part)
            q_ref[0, t, span, :] = query[t * part : (t + 1) * part]
            qraw_ref[0, t, span, :] = raw[t * part : (t + 1) * part]


def load_window(far_ref, near_ref, own_ref, win_ref):
    far, near = far_ref.shape[1], near_ref.shape[1]
    win_ref[:far, :] = far_ref[0]
    win_ref[far : far + near, :] = near_ref[0]
    win_ref[far + near :, :] = own_ref[0]


def mask_bias(qid_ref, kid_ref, t, part, span):
    ids = qid_ref[0, t * part : (t + 1) * part, :] == kid_ref[0, t]
    row = lax.broadcasted_iota(jnp.int32, (part, span), 0)
    column = lax.broadcasted_iota(jnp.int32, (part, span), 1)
    ok = ids & (column > row) & (column <= row + WINDOW)
    return jnp.where(ok, 0.0, MASKED_SCORE)


def attend_kernel(heads, q_ref, far_ref, near_ref, own_ref, qid_ref, kid_ref, mixed_ref, win_ref):
    size = q_ref.shape[-1]
    part = q_ref.shape[2] // heads
    span = part + WINDOW
    load_window(far_ref, near_ref, own_ref, win_ref)
    for t in range(2):
        bias = mask_bias(qid_ref, kid_ref, t, part, span)
        keys = win_ref[t * part : t * part + span, :size]
        values = win_ref[t * part : t * part + span, size:]
        for head in range(heads):
            scores = dot_nt(q_ref[0, t, head * part : (head + 1) * part, :], keys)
            weights = jnp.exp(scores + bias)
            total = jnp.sum(weights, axis=-1, keepdims=True)
            mixed = dot_nn(weights.astype(jnp.bfloat16), values) / total
            mixed_ref[0, t * part : (t + 1) * part, head * size : (head + 1) * size] = (
                mixed.astype(jnp.bfloat16)
            )


def middle_kernel(
    heads, chunk, mixed_ref, x_ref, cot_ref, wo_ref, wg_ref, wu_ref, wd_ref, ga_ref, gp_ref, gf_ref,
    out_ref, pre_ref, product_ref, ddown_ref, dgate_ref, dup_ref, datt_ref, dhid_ref, dmix_ref, dg_ref,
    act_ref, slope_ref,
):
    units = wg_ref.shape[0]
    size = dmix_ref.shape[-1]
    part = dmix_ref.shape[2] // heads
    x = x_ref[0].astype(jnp.float32)
    attended = dot_nt(mixed_ref[0], wo_ref[...])
    hidden = x + attended * inverse_rms(attended) * (1.0 + ga_ref[...])
    pre = (hidden * inverse_rms(hidden) * (1.0 + gp_ref[...])).astype(jnp.bfloat16)
    pre_ref[0] = pre
    down = jnp.zeros(x.shape, jnp.float32)
    root = (2.0 / math.pi) ** 0.5
    for start in range(0, units, chunk):
        span = slice(start, start + chunk)
        gate = dot_nt(pre, wg_ref[span, :])
        up = dot_nt(pre, wu_ref[span, :])
        square = gate * gate
        bend = jnp.tanh(gate * (root + (root * 0.044715) * square))
        half = 0.5 + 0.5 * bend
        act = gate * half
        slope = half + act * (1.0 - bend) * (root + (3.0 * root * 0.044715) * square)
        act_ref[:, span] = act
        slope_ref[:, span] = up * slope
        product = (act * up).astype(jnp.bfloat16)
        product_ref[0, :, span] = product
        down += dot_nt(product, wd_ref[:, span])
    out_ref[0] = (hidden + down * inverse_rms(down) * (1.0 + gf_ref[...])).astype(jnp.bfloat16)
    dy = cot_ref[0].astype(jnp.float32)
    d_down, dg_ffn = rms_back(down, gf_ref[...], dy)
    d_down = d_down.astype(jnp.bfloat16)
    ddown_ref[0] = d_down
    d_pre = jnp.zeros(x.shape, jnp.float32)
    for start in range(0, units, chunk):
        span = slice(start, start + chunk)
        d_product = dot_nn(d_down, wd_ref[:, span])
        d_gate = (d_product * slope_ref[:, span]).astype(jnp.bfloat16)
        d_up = (d_product * act_ref[:, span]).astype(jnp.bfloat16)
        dgate_ref[0, :, span] = d_gate
        dup_ref[0, :, span] = d_up
        d_pre += dot_nn(d_gate, wg_ref[span, :]) + dot_nn(d_up, wu_ref[span, :])
    d_hidden, dg_pre = rms_back(hidden, gp_ref[...], d_pre)
    d_hidden = dy + d_hidden
    dhid_ref[0] = d_hidden
    d_att, dg_attn = rms_back(attended, ga_ref[...], d_hidden)
    d_att = d_att.astype(jnp.bfloat16)
    datt_ref[0] = d_att
    dg_ref[0] = jnp.concatenate([dg_attn, dg_pre, dg_ffn], axis=0)
    for head in range(heads):
        d_mixed = dot_nn(d_att, wo_ref[:, head * size : (head + 1) * size]).astype(jnp.bfloat16)
        for t in range(2):
            dmix_ref[0, t, head * part : (head + 1) * part, :] = d_mixed[t * part : (t + 1) * part]


def attend_back_kernel(
    heads, q_ref, qraw_ref, far_ref, near_ref, own_ref, qid_ref, kid_ref, mixed_ref, dmix_ref,
    cos_ref, sin_ref, gq_ref,
    dfar_ref, dnear_ref, down_ref, dqraw_ref, dg_ref,
    win_ref, grad_ref,
):
    size = q_ref.shape[-1]
    part = q_ref.shape[2] // heads
    span = part + WINDOW
    far, near = far_ref.shape[1], near_ref.shape[1]
    load_window(far_ref, near_ref, own_ref, win_ref)
    grad_ref[...] = jnp.zeros_like(grad_ref)
    dg = jnp.zeros((1, size), jnp.float32)
    for t in range(2):
        rows = slice(t * part, (t + 1) * part)
        window = slice(t * part, t * part + span)
        bias = mask_bias(qid_ref, kid_ref, t, part, span)
        keys = win_ref[window, :size]
        values = win_ref[window, size:]
        cosine, sine = cos_ref[0, rows, :], sin_ref[0, rows, :]
        for head in range(heads):
            line = slice(head * part, (head + 1) * part)
            lanes = slice(head * size, (head + 1) * size)
            query = q_ref[0, t, line, :]
            d_out = dmix_ref[0, t, line, :]
            weights = jnp.exp(dot_nt(query, keys) + bias)
            weights = weights * (1.0 / jnp.sum(weights, axis=-1, keepdims=True))
            delta = jnp.sum(
                d_out.astype(jnp.float32) * mixed_ref[0, rows, lanes].astype(jnp.float32),
                axis=-1,
                keepdims=True,
            )
            d_scores = (weights * (dot_nt(d_out, values) - delta)).astype(jnp.bfloat16)
            weights = weights.astype(jnp.bfloat16)
            grad_ref[window, :size] += dot_tn(d_scores, query)
            grad_ref[window, size:] += dot_tn(weights, d_out)
            d_query = dot_nn(d_scores, keys) * size ** (-0.5)
            d_raw, part_g = rms_back(
                qraw_ref[0, t, line, :].astype(jnp.float32),
                gq_ref[...],
                turn(d_query, cosine, -sine),
            )
            dqraw_ref[0, rows, lanes] = d_raw.astype(jnp.bfloat16)
            dg += part_g
    dg_ref[0] = dg
    dfar_ref[0] = grad_ref[:far, :].astype(jnp.bfloat16)
    dnear_ref[0] = grad_ref[far : far + near, :]
    down_ref[0] = grad_ref[far + near :, :]


def input_back_kernel(
    own_ref, recv_ref, kraw_ref, cos_ref, sin_ref, wk_ref, wv_ref, dnq_ref, x_ref, dhid_ref,
    normed_ref, gi_ref, gk_ref,
    grad_ref, gkv_ref, dgi_ref, dgk_ref,
    total_ref,
):
    step = pl.program_id(0)
    size = wk_ref.shape[0]
    total = own_ref[0] + recv_ref[0].astype(jnp.float32)
    d_key = turn(total[:, :size], cos_ref[0], -sin_ref[0])
    d_raw, dg_key = rms_back(kraw_ref[0].astype(jnp.float32), gk_ref[...], d_key)
    d_raw = d_raw.astype(jnp.bfloat16)
    d_value = total[:, size:].astype(jnp.bfloat16)
    d_normed = dnq_ref[0] + dot_nn(d_raw, wk_ref[...]) + dot_nn(d_value, wv_ref[...])
    d_x, dg_input = rms_back(x_ref[0].astype(jnp.float32), gi_ref[...], d_normed)
    grad_ref[0] = dhid_ref[0] + d_x
    dgi_ref[0] = dg_input
    dgk_ref[0] = dg_key

    @pl.when(step == 0)
    def _():
        total_ref[...] = jnp.zeros_like(total_ref)

    total_ref[:size, :] += dot_tn(d_raw, normed_ref[0])
    total_ref[size:, :] += dot_tn(d_value, normed_ref[0])

    @pl.when(step == pl.num_programs(0) - 1)
    def _():
        gkv_ref[...] = total_ref[...].astype(jnp.bfloat16)


def dp_bits():
    return (lax.axis_size("dp") - 1).bit_length()


def gather_rows(shard, order):
    count = lax.axis_size("dp")
    index = lax.axis_index("dp")
    current = shard
    for bit in order:
        received = lax.ppermute(current, "dp", [(i, i ^ (1 << bit)) for i in range(count)])
        upper = ((index >> bit) & 1) == 1
        current = jnp.stack(
            [jnp.where(upper, received, current), jnp.where(upper, current, received)]
        )
    done = list(reversed(order))
    lead = [done.index(bit) for bit in sorted(done, reverse=True)]
    current = current.transpose(lead + [len(done), len(done) + 1])
    return current.reshape((count,) + shard.shape)


def scatter_rows(total, order):
    count = lax.axis_size("dp")
    index = lax.axis_index("dp")
    bits = len(order)
    rows = total.shape[0] // count
    current = total.astype(jnp.bfloat16).reshape((2,) * bits + (rows, total.shape[1]))
    left = list(range(bits - 1, -1, -1))
    for bit in order:
        axis = left.index(bit)
        left.remove(bit)
        mine = (index >> bit) & 1
        keep = lax.dynamic_index_in_dim(current, mine, axis, keepdims=False)
        send = lax.dynamic_index_in_dim(current, 1 - mine, axis, keepdims=False)
        received = lax.ppermute(send, "dp", [(i, i ^ (1 << bit)) for i in range(count)])
        current = (keep.astype(jnp.float32) + received.astype(jnp.float32)).astype(jnp.bfloat16)
    return current


def seq_sum(part):
    count = lax.axis_size("seq")
    index = lax.axis_index("seq")
    half = count // 2
    current = part

    def add(received):
        return (current.astype(jnp.float32) + received.astype(jnp.float32)).astype(jnp.bfloat16)

    for t in range(half - 1):
        pairs = [(t, t + 1), (count - 1 - t, count - 2 - t)]
        current = add(lax.ppermute(current, "seq", pairs))
    current = add(lax.ppermute(current, "seq", [(half - 1, half), (half, half - 1)]))
    for t in range(half - 2, -1, -1):
        pairs = [(t + 1, t), (count - 2 - t, count - 1 - t)]
        received = lax.ppermute(current, "seq", pairs)
        outer = (index == t) | (index == count - 1 - t)
        current = jnp.where(outer, received, current)
    return current.astype(jnp.float32)


def body(
    tokens,
    cotangent,
    segments,
    positions,
    query_weight,
    key_weight,
    value_weight,
    output_weight,
    gate_weight,
    up_weight,
    down_weight,
    norm_gains,
    query_first,
    key_first,
    value_first,
    output_first,
    gate_first,
    up_first,
    down_first,
    gains_first,
    query_second,
    key_second,
    value_second,
    output_second,
    gate_second,
    up_second,
    down_second,
    gains_second,
):
    bits = dp_bits()
    order_a = list(range(1, bits)) + [0]
    order_b = list(range(bits - 1, 0, -1)) + [0]
    key_rows = key_weight.shape[0]
    gain_rows = norm_gains.shape[0]
    low = jnp.bfloat16
    width = tokens.shape[2]
    pad_rows = 16
    gain_block = jnp.pad(norm_gains.astype(low)[None], ((0, pad_rows - 1), (0, width - gain_rows)))
    key_value_gain = jnp.concatenate([key_weight.astype(low), value_weight.astype(low), gain_block])
    w_query = gather_rows(query_weight.astype(low), order_a).reshape(-1, width)
    kvg = gather_rows(key_value_gain, order_b)
    w_key = kvg[:, :key_rows].reshape(-1, width)
    w_value = kvg[:, key_rows : 2 * key_rows].reshape(-1, width)
    gains_all = kvg[:, 2 * key_rows, :gain_rows].reshape(-1)
    w_output = gather_rows(output_weight.astype(low), order_a).reshape(-1, output_weight.shape[1])
    w_gate = gather_rows(gate_weight.astype(low), order_a).reshape(-1, width)
    w_up = gather_rows(up_weight.astype(low), order_b).reshape(-1, width)
    w_down = gather_rows(down_weight.astype(low), order_b).reshape(-1, down_weight.shape[1])
    seqs, rows, _ = tokens.shape
    size = w_key.shape[0]
    heads = w_query.shape[0] // size
    units = w_gate.shape[0]
    shards = lax.axis_size("seq")
    far = WINDOW - rows
    part = rows // 2
    span = part + WINDOW
    gains_float = gains_all.astype(jnp.float32)[None]
    g_input, g_attn, g_pre, g_ffn = (
        gains_float[:, i * width : (i + 1) * width] for i in range(4)
    )
    g_query = gains_float[:, 4 * width : 4 * width + size]
    g_key = gains_float[:, 4 * width + size : 4 * width + 2 * size]
    angles = positions.astype(jnp.float32)[..., None] * frequencies(size)
    cosine, sine = jnp.cos(angles), jnp.sin(angles)
    first_row = lax.axis_index("seq") * rows
    padded = jnp.concatenate([jnp.full((seqs, WINDOW), -1, jnp.int32), segments], axis=1)
    window_ids = lax.dynamic_slice_in_dim(padded, first_row, WINDOW + rows, 1)
    query_ids = window_ids[:, WINDOW:, None]
    key_ids = jnp.stack([window_ids[:, :span], window_ids[:, part:]], axis=1)[:, :, None, :]

    f32 = jnp.float32

    def array(shape, kind):
        return jax.ShapeDtypeStruct(shape, kind)

    def call(kernel, outs, out_specs, in_specs, scratch, flops, moved):
        return pl.pallas_call(
            kernel,
            grid=(seqs,),
            out_shape=outs,
            in_specs=in_specs,
            out_specs=out_specs,
            scratch_shapes=scratch,
            compiler_params=kernel_params(),
            cost_estimate=pl.CostEstimate(flops=flops, bytes_accessed=moved, transcendentals=0),
        )

    tokens_all = seqs * rows
    head_block = per_seq(2, heads * part, size)
    q_shape = (seqs, 2, heads * part, size)
    normed, query, query_raw, pair_own, key_raw = call(
        functools.partial(project_kernel, heads),
        [
            array((seqs, rows, width), low),
            array(q_shape, low),
            array(q_shape, low),
            array((seqs, rows, 2 * size), low),
            array((seqs, rows, size), low),
        ],
        [per_seq(rows, width), head_block, head_block, per_seq(rows, 2 * size), per_seq(rows, size)],
        [
            per_seq(rows, width),
            per_seq(rows, size // 2),
            per_seq(rows, size // 2),
            whole(*w_query.shape),
            whole(*w_key.shape),
            whole(*w_value.shape),
            whole(1, width),
            whole(1, size),
            whole(1, size),
        ],
        [],
        4 * tokens_all * width * (heads + 2) * size,
        16_000_000,
    )(tokens, cosine, sine, w_query, w_key, w_value, g_input, g_query, g_key)

    upward = [(i, i + 1) for i in range(shards - 1)]
    pair_near = lax.ppermute(pair_own, "seq", upward)
    pair_far = lax.ppermute(pair_near[:, rows - far :], "seq", upward[1:])

    window_specs = [
        per_seq(far, 2 * size),
        per_seq(rows, 2 * size),
        per_seq(rows, 2 * size),
        per_seq(rows, 1),
        per_seq(2, 1, span),
    ]
    attend_flops = 8 * tokens_all * heads * span * size
    mixed = call(
        functools.partial(attend_kernel, heads),
        array((seqs, rows, heads * size), low),
        per_seq(rows, heads * size),
        [head_block] + window_specs,
        [pltpu.VMEM((WINDOW + rows, 2 * size), low)],
        attend_flops,
        16_000_000,
    )(query, pair_far, pair_near, pair_own, query_ids, key_ids)

    (
        layer_output,
        pre_low,
        product_low,
        grad_down_low,
        grad_gate_low,
        grad_up_low,
        grad_attended_low,
        grad_hidden,
        grad_mixed,
        grad_gains_middle,
    ) = call(
        functools.partial(middle_kernel, heads, 512),
        [
            array((seqs, rows, width), low),
            array((seqs, rows, width), low),
            array((seqs, rows, units), low),
            array((seqs, rows, width), low),
            array((seqs, rows, units), low),
            array((seqs, rows, units), low),
            array((seqs, rows, width), low),
            array((seqs, rows, width), f32),
            array(q_shape, low),
            array((seqs, 3, width), f32),
        ],
        [
            per_seq(rows, width),
            per_seq(rows, width),
            per_seq(rows, units),
            per_seq(rows, width),
            per_seq(rows, units),
            per_seq(rows, units),
            per_seq(rows, width),
            per_seq(rows, width),
            head_block,
            per_seq(3, width),
        ],
        [
            per_seq(rows, heads * size),
            per_seq(rows, width),
            per_seq(rows, width),
            whole(*w_output.shape),
            whole(*w_gate.shape),
            whole(*w_up.shape),
            whole(*w_down.shape),
            whole(1, width),
            whole(1, width),
            whole(1, width),
        ],
        [pltpu.VMEM((rows, units), f32), pltpu.VMEM((rows, units), f32)],
        4 * tokens_all * width * (heads * size + 3 * units),
        40_000_000,
    )(mixed, tokens, cotangent, w_output, w_gate, w_up, w_down, g_attn, g_pre, g_ffn)

    def flat(values):
        return values.reshape(tokens_all, values.shape[-1])

    grad_w_gate = weight_grad(flat(grad_gate_low), flat(pre_low)).astype(low)
    grad_w_up = weight_grad(flat(grad_up_low), flat(pre_low)).astype(low)
    grad_w_down = weight_grad(flat(grad_down_low), flat(product_low)).astype(low)
    grad_w_output = weight_grad(flat(grad_attended_low), flat(mixed)).astype(low)

    grad_far, grad_near, grad_own, grad_query_low, grad_g_query = call(
        functools.partial(attend_back_kernel, heads),
        [
            array((seqs, far, 2 * size), low),
            array((seqs, rows, 2 * size), f32),
            array((seqs, rows, 2 * size), f32),
            array((seqs, rows, heads * size), low),
            array((seqs, 1, size), f32),
        ],
        [
            per_seq(far, 2 * size),
            per_seq(rows, 2 * size),
            per_seq(rows, 2 * size),
            per_seq(rows, heads * size),
            per_seq(1, size),
        ],
        [head_block, head_block]
        + window_specs
        + [
            per_seq(rows, heads * size),
            head_block,
            per_seq(rows, size // 2),
            per_seq(rows, size // 2),
            whole(1, size),
        ],
        [
            pltpu.VMEM((WINDOW + rows, 2 * size), low),
            pltpu.VMEM((WINDOW + rows, 2 * size), f32),
        ],
        attend_flops * 3,
        25_000_000,
    )(
        query, query_raw, pair_far, pair_near, pair_own, query_ids, key_ids, mixed, grad_mixed,
        cosine, sine, g_query,
    )

    downward = [(i + 1, i) for i in range(shards - 1)]
    from_far = lax.ppermute(grad_far, "seq", downward[1:])
    near_sum = grad_near + jnp.pad(
        from_far.astype(f32), ((0, 0), (rows - far, 0), (0, 0))
    )
    from_near = lax.ppermute(near_sum.astype(low), "seq", downward)
    grad_w_query = weight_grad(flat(grad_query_low), flat(normed)).astype(low)
    grad_normed_query = jnp.dot(
        flat(grad_query_low), w_query, preferred_element_type=f32
    ).reshape(tokens.shape)
    input_grad, grad_w_pair, grad_g_input, grad_g_key = call(
        input_back_kernel,
        [
            array((seqs, rows, width), f32),
            array((2 * size, width), low),
            array((seqs, 1, width), f32),
            array((seqs, 1, size), f32),
        ],
        [per_seq(rows, width), whole(2 * size, width), per_seq(1, width), per_seq(1, size)],
        [
            per_seq(rows, 2 * size),
            per_seq(rows, 2 * size),
            per_seq(rows, size),
            per_seq(rows, size // 2),
            per_seq(rows, size // 2),
            whole(*w_key.shape),
            whole(*w_value.shape),
            per_seq(rows, width),
            per_seq(rows, width),
            per_seq(rows, width),
            per_seq(rows, width),
            whole(1, width),
            whole(1, size),
        ],
        [pltpu.VMEM((2 * size, width), f32)],
        8 * tokens_all * width * size * 2,
        20_000_000,
    )(
        grad_own, from_near, key_raw, cosine, sine, w_key, w_value, grad_normed_query, tokens,
        grad_hidden, normed, g_input, g_key,
    )
    gains_middle = jnp.sum(grad_gains_middle, axis=0).reshape(-1)
    grad_gains = jnp.concatenate(
        [
            jnp.sum(grad_g_input, axis=(0, 1)),
            gains_middle,
            jnp.sum(grad_g_query, axis=(0, 1)),
            jnp.sum(grad_g_key, axis=(0, 1)),
        ]
    )
    count = lax.axis_size("dp")
    back_a = [0] + order_a[:-1]
    back_b = [0] + order_b[:-1]
    gate_total = seq_sum(scatter_rows(grad_w_gate, back_a))
    up_total = seq_sum(scatter_rows(grad_w_up, back_b))
    down_total = seq_sum(scatter_rows(grad_w_down, back_b))
    output_total = seq_sum(scatter_rows(grad_w_output, back_a))
    query_total = seq_sum(scatter_rows(grad_w_query, back_a))
    gain_grad_block = jnp.pad(
        grad_gains.astype(low).reshape(count, 1, gain_rows),
        ((0, 0), (0, pad_rows - 1), (0, width - gain_rows)),
    )
    kvg_grad = jnp.concatenate(
        [
            grad_w_pair[:size].reshape(count, key_rows, width),
            grad_w_pair[size:].reshape(count, key_rows, width),
            gain_grad_block,
        ],
        axis=1,
    ).reshape(-1, width)
    kvg_total = seq_sum(scatter_rows(kvg_grad, back_b))
    key_total = kvg_total[:key_rows]
    value_total = kvg_total[key_rows : 2 * key_rows]
    gains_total = kvg_total[2 * key_rows, :gain_rows]
    query_momentum, query_variance, query_updated = adam_step(
        query_weight, query_first, query_second, query_total, WEIGHT_DECAY
    )
    key_momentum, key_variance, key_updated = adam_step(
        key_weight, key_first, key_second, key_total, WEIGHT_DECAY
    )
    value_momentum, value_variance, value_updated = adam_step(
        value_weight, value_first, value_second, value_total, WEIGHT_DECAY
    )
    output_momentum, output_variance, output_updated = adam_step(
        output_weight, output_first, output_second, output_total, WEIGHT_DECAY
    )
    gate_momentum, gate_variance, gate_updated = adam_step(
        gate_weight, gate_first, gate_second, gate_total, WEIGHT_DECAY
    )
    up_momentum, up_variance, up_updated = adam_step(
        up_weight, up_first, up_second, up_total, WEIGHT_DECAY
    )
    down_momentum, down_variance, down_updated = adam_step(
        down_weight, down_first, down_second, down_total, WEIGHT_DECAY
    )
    gains_momentum, gains_variance, gains_updated = adam_step(
        norm_gains, gains_first, gains_second, gains_total, 0.0
    )
    return (
        layer_output,
        input_grad,
        query_momentum,
        key_momentum,
        value_momentum,
        output_momentum,
        gate_momentum,
        up_momentum,
        down_momentum,
        gains_momentum,
        query_variance,
        key_variance,
        value_variance,
        output_variance,
        gate_variance,
        up_variance,
        down_variance,
        gains_variance,
        query_updated,
        key_updated,
        value_updated,
        output_updated,
        gate_updated,
        up_updated,
        down_updated,
        gains_updated,
    )


def solution(mesh):
    return jax.shard_map(
        body,
        mesh=mesh,
        in_specs=(
            P("dp", "seq", None),
            P("dp", "seq", None),
            P("dp", None),
            P("dp", "seq"),
            P("dp", None),
            P("dp", None),
            P("dp", None),
            P("dp", None),
            P("dp", None),
            P("dp", None),
            P("dp", None),
            P("dp"),
            P("dp", None),
            P("dp", None),
            P("dp", None),
            P("dp", None),
            P("dp", None),
            P("dp", None),
            P("dp", None),
            P("dp"),
            P("dp", None),
            P("dp", None),
            P("dp", None),
            P("dp", None),
            P("dp", None),
            P("dp", None),
            P("dp", None),
            P("dp"),
        ),
        out_specs=(
            P("dp", "seq", None),
            P("dp", "seq", None),
            P("dp", None),
            P("dp", None),
            P("dp", None),
            P("dp", None),
            P("dp", None),
            P("dp", None),
            P("dp", None),
            P("dp"),
            P("dp", None),
            P("dp", None),
            P("dp", None),
            P("dp", None),
            P("dp", None),
            P("dp", None),
            P("dp", None),
            P("dp"),
            P("dp", None),
            P("dp", None),
            P("dp", None),
            P("dp", None),
            P("dp", None),
            P("dp", None),
            P("dp", None),
            P("dp"),
        ),
        check_vma=False,
    )
```

```python
import functools
import math

import jax
import jax.numpy as jnp
from jax import lax
from jax.experimental import pallas as pl
from jax.experimental.pallas import tpu as pltpu
from jax.sharding import PartitionSpec as P

WINDOW = 512
STEP = 10


NORM_EPSILON = 1e-06
ROPE_BASE = 10000.0
LEARN_RATE = 0.08
BETA_FIRST = 0.9
BETA_SECOND = 0.95
ADAM_EPSILON = 1e-08
WEIGHT_DECAY = 0.01
MASKED_SCORE = -1000000000.0


def frequencies(size):
    return ROPE_BASE ** (-2.0 * jnp.arange(size // 2).astype(jnp.float32) / size)


def weight_grad(gradients, inputs):
    return lax.dot_general(
        gradients, inputs, (((0,), (0,)), ((), ())), preferred_element_type=jnp.float32
    )


def adam_step(weight, first_moment, second_moment, gradient, decay_rate):
    momentum = BETA_FIRST * first_moment + (1.0 - BETA_FIRST) * gradient
    variance = BETA_SECOND * second_moment + (1.0 - BETA_SECOND) * gradient * gradient
    corrected = momentum / (1.0 - BETA_FIRST**STEP)
    scaled = variance / (1.0 - BETA_SECOND**STEP)
    updated = weight - LEARN_RATE * (
        corrected / (jnp.sqrt(scaled) + ADAM_EPSILON) + decay_rate * weight
    )
    return (momentum, variance, updated)


VMEM_BYTES = 56 * 1024 * 1024


def kernel_params():
    return pltpu.CompilerParams(
        dimension_semantics=("arbitrary",), vmem_limit_bytes=VMEM_BYTES
    )


def per_seq(*tail):
    return pl.BlockSpec((1,) + tail, lambda s: (s,) + (0,) * len(tail))


def whole(*shape):
    return pl.BlockSpec(shape, lambda s: (0,) * len(shape), pipeline_mode=pl.Buffered(1))


def dot_nt(a, b):
    return lax.dot_general(a, b, (((1,), (1,)), ((), ())), preferred_element_type=jnp.float32)


def dot_nn(a, b):
    return lax.dot_general(a, b, (((1,), (0,)), ((), ())), preferred_element_type=jnp.float32)


def dot_tn(a, b):
    return lax.dot_general(a, b, (((0,), (0,)), ((), ())), preferred_element_type=jnp.float32)


def inverse_rms(values):
    return lax.rsqrt(jnp.mean(values * values, axis=-1, keepdims=True) + NORM_EPSILON)


def rms_back(values, gain, grad):
    inverse = inverse_rms(values)
    unit = values * inverse
    scaled = grad * (1.0 + gain)
    return (
        inverse * (scaled - unit * jnp.mean(unit * scaled, axis=-1, keepdims=True)),
        jnp.sum(grad * unit, axis=0, keepdims=True),
    )


def turn(values, cosine, sine):
    half = values.shape[-1] // 2
    first, second = values[:, :half], values[:, half:]
    return jnp.concatenate(
        [first * cosine - second * sine, second * cosine + first * sine], axis=-1
    )


def stack_heads(values, heads):
    return jnp.concatenate([values] * heads, axis=0)


def cast_first_kernel(wq_ref, wk_ref, wv_ref, gain_ref, q_ref, rest_ref):
    q_ref[...] = wq_ref[...].astype(jnp.bfloat16)
    width = wq_ref.shape[1]
    gains = gain_ref[...]
    tail = width - gains.shape[1]
    block = jnp.broadcast_to(gains, (16, gains.shape[1]))
    if tail:
        block = jnp.concatenate([block, jnp.zeros((16, tail), jnp.float32)], axis=1)
    rest_ref[...] = jnp.concatenate([wk_ref[...], wv_ref[...], block], axis=0).astype(jnp.bfloat16)


def cast_rest_kernel(waits, wg_ref, wu_ref, wd_ref, wo_ref, *refs):
    gate_ref, up_ref, pair_ref = refs[waits:]
    units = wd_ref.shape[1]
    gate_ref[...] = wg_ref[...].astype(jnp.bfloat16)
    up_ref[...] = wu_ref[...].astype(jnp.bfloat16)
    pair_ref[:, :units] = wd_ref[...].astype(jnp.bfloat16)
    pair_ref[:, units:] = wo_ref[...].astype(jnp.bfloat16)


def project_kernel(
    heads, x_ref, cos_ref, sin_ref, wq_ref, wk_ref, wv_ref, gi_ref, gq_ref, gk_ref,
    normed_ref, q_ref, qraw_ref, kv_ref, kraw_ref,
):
    x = x_ref[0].astype(jnp.float32)
    size = wk_ref.shape[0]
    rows = x.shape[0]
    part = rows // 2
    normed = (x * inverse_rms(x) * (1.0 + gi_ref[...])).astype(jnp.bfloat16)
    normed_ref[0] = normed
    cosine, sine = cos_ref[0], sin_ref[0]
    k_raw = dot_nt(normed, wk_ref[...])
    kraw_ref[0] = k_raw.astype(jnp.bfloat16)
    key = turn(k_raw * inverse_rms(k_raw) * (1.0 + gk_ref[...]), cosine, sine)
    kv_ref[0, :, :size] = key.astype(jnp.bfloat16)
    kv_ref[0, :, size:] = dot_nt(normed, wv_ref[...]).astype(jnp.bfloat16)
    for head in range(heads):
        raw = dot_nt(normed, wq_ref[head * size : (head + 1) * size, :])
        query = turn(raw * inverse_rms(raw) * (1.0 + gq_ref[...]), cosine, sine)
        query = (query * size ** (-0.5)).astype(jnp.bfloat16)
        raw = raw.astype(jnp.bfloat16)
        for t in range(2):
            span = slice(head * part, (head + 1) * part)
            q_ref[0, t, span, :] = query[t * part : (t + 1) * part]
            qraw_ref[0, t, span, :] = raw[t * part : (t + 1) * part]


def load_window(far_ref, near_ref, own_ref, win_ref):
    far, near = far_ref.shape[1], near_ref.shape[1]
    win_ref[:far, :] = far_ref[0]
    win_ref[far : far + near, :] = near_ref[0]
    win_ref[far + near :, :] = own_ref[0]


def mask_bias(qid_ref, kid_ref, t, part, span):
    ids = qid_ref[0, t * part : (t + 1) * part, :] == kid_ref[0, t]
    row = lax.broadcasted_iota(jnp.int32, (part, span), 0)
    column = lax.broadcasted_iota(jnp.int32, (part, span), 1)
    ok = ids & (column > row) & (column <= row + WINDOW)
    return jnp.where(ok, 0.0, MASKED_SCORE)


def attend_kernel(heads, q_ref, far_ref, near_ref, own_ref, qid_ref, kid_ref, mixed_ref, win_ref):
    size = q_ref.shape[-1]
    part = q_ref.shape[2] // heads
    span = part + WINDOW
    load_window(far_ref, near_ref, own_ref, win_ref)
    for t in range(2):
        bias = mask_bias(qid_ref, kid_ref, t, part, span)
        keys = win_ref[t * part : t * part + span, :size]
        values = win_ref[t * part : t * part + span, size:]
        for head in range(heads):
            scores = dot_nt(q_ref[0, t, head * part : (head + 1) * part, :], keys)
            weights = jnp.exp(scores + bias)
            total = jnp.sum(weights, axis=-1, keepdims=True)
            mixed = dot_nn(weights.astype(jnp.bfloat16), values) / total
            mixed_ref[0, t * part : (t + 1) * part, head * size : (head + 1) * size] = (
                mixed.astype(jnp.bfloat16)
            )


def middle_kernel(
    heads, chunk, mixed_ref, x_ref, cot_ref, wg_ref, wu_ref, wdo_ref, ga_ref, gp_ref, gf_ref,
    out_ref, pre_ref, product_ref, ddown_ref, dgate_ref, dup_ref, datt_ref, dhid_ref, dmix_ref, dg_ref,
    act_ref, slope_ref,
):
    units = wg_ref.shape[0]
    size = dmix_ref.shape[-1]
    part = dmix_ref.shape[2] // heads
    x = x_ref[0].astype(jnp.float32)
    attended = dot_nt(mixed_ref[0], wdo_ref[:, units:])
    hidden = x + attended * inverse_rms(attended) * (1.0 + ga_ref[...])
    pre = (hidden * inverse_rms(hidden) * (1.0 + gp_ref[...])).astype(jnp.bfloat16)
    pre_ref[0] = pre
    down = jnp.zeros(x.shape, jnp.float32)
    root = (2.0 / math.pi) ** 0.5
    for start in range(0, units, chunk):
        span = slice(start, start + chunk)
        gate = dot_nt(pre, wg_ref[span, :])
        up = dot_nt(pre, wu_ref[span, :])
        square = gate * gate
        bend = jnp.tanh(gate * (root + (root * 0.044715) * square))
        half = 0.5 + 0.5 * bend
        act = gate * half
        slope = half + act * (1.0 - bend) * (root + (3.0 * root * 0.044715) * square)
        act_ref[:, span] = act
        slope_ref[:, span] = up * slope
        product = (act * up).astype(jnp.bfloat16)
        product_ref[0, :, span] = product
        down += dot_nt(product, wdo_ref[:, span])
    out_ref[0] = (hidden + down * inverse_rms(down) * (1.0 + gf_ref[...])).astype(jnp.bfloat16)
    dy = cot_ref[0].astype(jnp.float32)
    d_down, dg_ffn = rms_back(down, gf_ref[...], dy)
    d_down = d_down.astype(jnp.bfloat16)
    ddown_ref[0] = d_down
    d_pre = jnp.zeros(x.shape, jnp.float32)
    for start in range(0, units, chunk):
        span = slice(start, start + chunk)
        d_product = dot_nn(d_down, wdo_ref[:, span])
        d_gate = (d_product * slope_ref[:, span]).astype(jnp.bfloat16)
        d_up = (d_product * act_ref[:, span]).astype(jnp.bfloat16)
        dgate_ref[0, :, span] = d_gate
        dup_ref[0, :, span] = d_up
        d_pre += dot_nn(d_gate, wg_ref[span, :]) + dot_nn(d_up, wu_ref[span, :])
    d_hidden, dg_pre = rms_back(hidden, gp_ref[...], d_pre)
    d_hidden = dy + d_hidden
    dhid_ref[0] = d_hidden
    d_att, dg_attn = rms_back(attended, ga_ref[...], d_hidden)
    d_att = d_att.astype(jnp.bfloat16)
    datt_ref[0] = d_att
    dg_ref[0] = jnp.concatenate([dg_attn, dg_pre, dg_ffn], axis=0)
    for head in range(heads):
        d_mixed = dot_nn(
            d_att, wdo_ref[:, units + head * size : units + (head + 1) * size]
        ).astype(jnp.bfloat16)
        for t in range(2):
            dmix_ref[0, t, head * part : (head + 1) * part, :] = d_mixed[t * part : (t + 1) * part]


def attend_back_kernel(
    heads, waits, q_ref, qraw_ref, far_ref, near_ref, own_ref, qid_ref, kid_ref, mixed_ref, dmix_ref,
    cos_ref, sin_ref, gq_ref, *refs
):
    dfar_ref, dnear_ref, down_ref, dqraw_ref, dg_ref, win_ref, grad_ref = refs[waits:]
    size = q_ref.shape[-1]
    part = q_ref.shape[2] // heads
    span = part + WINDOW
    far, near = far_ref.shape[1], near_ref.shape[1]
    load_window(far_ref, near_ref, own_ref, win_ref)
    grad_ref[...] = jnp.zeros_like(grad_ref)
    dg = jnp.zeros((1, size), jnp.float32)
    for t in range(2):
        rows = slice(t * part, (t + 1) * part)
        window = slice(t * part, t * part + span)
        bias = mask_bias(qid_ref, kid_ref, t, part, span)
        keys = win_ref[window, :size]
        values = win_ref[window, size:]
        cosine, sine = cos_ref[0, rows, :], sin_ref[0, rows, :]
        for head in range(heads):
            line = slice(head * part, (head + 1) * part)
            lanes = slice(head * size, (head + 1) * size)
            query = q_ref[0, t, line, :]
            d_out = dmix_ref[0, t, line, :]
            weights = jnp.exp(dot_nt(query, keys) + bias)
            weights = weights * (1.0 / jnp.sum(weights, axis=-1, keepdims=True))
            delta = jnp.sum(
                d_out.astype(jnp.float32) * mixed_ref[0, rows, lanes].astype(jnp.float32),
                axis=-1,
                keepdims=True,
            )
            d_scores = (weights * (dot_nt(d_out, values) - delta)).astype(jnp.bfloat16)
            weights = weights.astype(jnp.bfloat16)
            grad_ref[window, :size] += dot_tn(d_scores, query)
            grad_ref[window, size:] += dot_tn(weights, d_out)
            d_query = dot_nn(d_scores, keys) * size ** (-0.5)
            d_raw, part_g = rms_back(
                qraw_ref[0, t, line, :].astype(jnp.float32),
                gq_ref[...],
                turn(d_query, cosine, -sine),
            )
            dqraw_ref[0, rows, lanes] = d_raw.astype(jnp.bfloat16)
            dg += part_g
    dg_ref[0] = dg
    dfar_ref[0] = grad_ref[:far, :].astype(jnp.bfloat16)
    dnear_ref[0] = grad_ref[far : far + near, :]
    down_ref[0] = grad_ref[far + near :, :]


def input_back_kernel(
    waits, own_ref, recv_ref, kraw_ref, cos_ref, sin_ref, wk_ref, wv_ref, dnq_ref, x_ref, dhid_ref,
    gi_ref, gk_ref, *refs
):
    grad_ref, dpair_ref, dgi_ref, dgk_ref = refs[waits:]
    size = wk_ref.shape[0]
    total = own_ref[0] + recv_ref[0].astype(jnp.float32)
    d_key = turn(total[:, :size], cos_ref[0], -sin_ref[0])
    d_raw, dg_key = rms_back(kraw_ref[0].astype(jnp.float32), gk_ref[...], d_key)
    d_raw = d_raw.astype(jnp.bfloat16)
    d_value = total[:, size:].astype(jnp.bfloat16)
    dpair_ref[0, :, :size] = d_raw
    dpair_ref[0, :, size:] = d_value
    d_normed = dnq_ref[0] + dot_nn(d_raw, wk_ref[...]) + dot_nn(d_value, wv_ref[...])
    d_x, dg_input = rms_back(x_ref[0].astype(jnp.float32), gi_ref[...], d_normed)
    grad_ref[0] = dhid_ref[0] + d_x
    dgi_ref[0] = dg_input
    dgk_ref[0] = dg_key


def flips(bit):
    return [(i, i ^ (1 << bit)) for i in range(lax.axis_size("dp"))]


def side(bit):
    return (lax.axis_index("dp") >> bit) & 1


def gather_rows(shard, order):
    current, done, steps = shard, [], []
    for bit in order:
        received = lax.ppermute(current, "dp", flips(bit))
        steps.append(received)
        upper = side(bit) == 1
        axis = sum(1 for other in done if other > bit)
        current = jnp.stack(
            [jnp.where(upper, received, current), jnp.where(upper, current, received)], axis=axis
        )
        done.append(bit)
    return current.reshape((lax.axis_size("dp"),) + shard.shape), steps


class RowSum:
    def __init__(self, parts, order, axis):
        self.terms = [
            (part.reshape((2,) * len(order) + part.shape[1:]), list(range(len(order) - 1, -1, -1)))
            for part in parts
        ]
        self.join = axis
        self.order = order
        self.chosen = {}
        self.received = []

    def total(self, other=None):
        picks = dict(self.chosen)
        if other is not None:
            picks[other] = 1 - side(other)
        pieces = [self.pick(part, bits, picks) for part, bits in self.terms]
        value = jnp.concatenate(pieces, axis=self.join) if len(pieces) > 1 else pieces[0]
        value = value.astype(jnp.float32)
        for part, bits in self.received:
            value += self.pick(part, bits, picks).astype(jnp.float32)
        return value.astype(jnp.bfloat16)

    def pick(self, part, bits, picks):
        bits = list(bits)
        for bit, where in picks.items():
            if bit in bits:
                part = lax.dynamic_index_in_dim(part, where, bits.index(bit), keepdims=False)
                bits.remove(bit)
        return part

    def send(self, bit):
        self.sent = self.total(bit)
        return self.sent

    def step(self, bit):
        received = lax.ppermute(self.send(bit), "dp", flips(bit))
        self.chosen[bit] = side(bit)
        left = [b for b in range(len(self.order) - 1, -1, -1) if b not in self.chosen]
        self.received.append((received, left))
        return received


def seq_sum(part):
    count = lax.axis_size("seq")
    index = lax.axis_index("seq")
    half = count // 2
    terms = [part]

    def total():
        return sum(term.astype(jnp.float32) for term in terms)

    for t in range(half - 1):
        pairs = [(t, t + 1), (count - 1 - t, count - 2 - t)]
        terms.append(lax.ppermute(total().astype(jnp.bfloat16), "seq", pairs))
    middle = [(half - 1, half), (half, half - 1)]
    terms.append(lax.ppermute(total().astype(jnp.bfloat16), "seq", middle))
    result = total()
    for t in range(half - 2, -1, -1):
        pairs = [(t + 1, t), (count - 2 - t, count - 1 - t)]
        received = lax.ppermute(result.astype(jnp.bfloat16), "seq", pairs)
        outer = (index == t) | (index == count - 1 - t)
        result = jnp.where(outer, received.astype(jnp.float32), result)
    return result


def body(
    tokens,
    cotangent,
    segments,
    positions,
    query_weight,
    key_weight,
    value_weight,
    output_weight,
    gate_weight,
    up_weight,
    down_weight,
    norm_gains,
    query_first,
    key_first,
    value_first,
    output_first,
    gate_first,
    up_first,
    down_first,
    gains_first,
    query_second,
    key_second,
    value_second,
    output_second,
    gate_second,
    up_second,
    down_second,
    gains_second,
):
    count = lax.axis_size("dp")
    bits = (count - 1).bit_length()
    order_a = list(range(1, bits)) + [0]
    order_b = list(range(bits - 1, 0, -1)) + [0]
    low = jnp.bfloat16
    f32 = jnp.float32
    width = tokens.shape[2]
    key_rows = key_weight.shape[0]
    gain_rows = norm_gains.shape[0]
    rest_rows = 2 * key_rows + 16

    def array(shape, kind):
        return jax.ShapeDtypeStruct(shape, kind)

    query_shard, rest_shard = pl.pallas_call(
        cast_first_kernel,
        out_shape=[array(query_weight.shape, low), array((rest_rows, width), low)],
    )(query_weight, key_weight, value_weight, norm_gains[None])
    query_all, query_steps = gather_rows(query_shard, order_a)
    rest_all, rest_steps = gather_rows(rest_shard, order_b)
    w_query = query_all.reshape(-1, width)
    w_key = rest_all[:, :key_rows].reshape(-1, width)
    w_value = rest_all[:, key_rows : 2 * key_rows].reshape(-1, width)
    gains_all = rest_all[:, 2 * key_rows, :gain_rows].reshape(-1)
    block = pl.BlockSpec(memory_space=pltpu.VMEM)
    anywhere = pl.BlockSpec(memory_space=pl.ANY)
    arrived = [query_steps[-2], rest_steps[-2]]
    gate_shard, up_shard, pair_shard = pl.pallas_call(
        functools.partial(cast_rest_kernel, len(arrived)),
        out_shape=[
            array(gate_weight.shape, low),
            array(up_weight.shape, low),
            array((down_weight.shape[0], down_weight.shape[1] + output_weight.shape[1]), low),
        ],
        in_specs=[block] * 4 + [anywhere] * len(arrived),
    )(gate_weight, up_weight, down_weight, output_weight, *arrived)
    w_gate = gather_rows(gate_shard, order_a)[0].reshape(-1, width)
    w_up = gather_rows(up_shard, order_b)[0].reshape(-1, width)
    w_pair = gather_rows(pair_shard, order_b)[0].reshape(-1, pair_shard.shape[1])
    seqs, rows, _ = tokens.shape
    size = w_key.shape[0]
    heads = w_query.shape[0] // size
    units = w_gate.shape[0]
    shards = lax.axis_size("seq")
    far = WINDOW - rows
    part = rows // 2
    span = part + WINDOW
    gains_float = gains_all.astype(jnp.float32)[None]
    g_input, g_attn, g_pre, g_ffn = (
        gains_float[:, i * width : (i + 1) * width] for i in range(4)
    )
    g_query = gains_float[:, 4 * width : 4 * width + size]
    g_key = gains_float[:, 4 * width + size : 4 * width + 2 * size]
    angles = positions.astype(jnp.float32)[..., None] * frequencies(size)
    cosine, sine = jnp.cos(angles), jnp.sin(angles)
    first_row = lax.axis_index("seq") * rows
    padded = jnp.concatenate([jnp.full((seqs, WINDOW), -1, jnp.int32), segments], axis=1)
    window_ids = lax.dynamic_slice_in_dim(padded, first_row, WINDOW + rows, 1)
    query_ids = window_ids[:, WINDOW:, None]
    key_ids = jnp.stack([window_ids[:, :span], window_ids[:, part:]], axis=1)[:, :, None, :]

    def call(kernel, outs, out_specs, in_specs, scratch, flops, moved):
        return pl.pallas_call(
            kernel,
            grid=(seqs,),
            out_shape=outs,
            in_specs=in_specs,
            out_specs=out_specs,
            scratch_shapes=scratch,
            compiler_params=kernel_params(),
            cost_estimate=pl.CostEstimate(flops=flops, bytes_accessed=moved, transcendentals=0),
        )

    tokens_all = seqs * rows
    head_block = per_seq(2, heads * part, size)
    q_shape = (seqs, 2, heads * part, size)
    normed, query, query_raw, pair_own, key_raw = call(
        functools.partial(project_kernel, heads),
        [
            array((seqs, rows, width), low),
            array(q_shape, low),
            array(q_shape, low),
            array((seqs, rows, 2 * size), low),
            array((seqs, rows, size), low),
        ],
        [per_seq(rows, width), head_block, head_block, per_seq(rows, 2 * size), per_seq(rows, size)],
        [
            per_seq(rows, width),
            per_seq(rows, size // 2),
            per_seq(rows, size // 2),
            whole(*w_query.shape),
            whole(*w_key.shape),
            whole(*w_value.shape),
            whole(1, width),
            whole(1, size),
            whole(1, size),
        ],
        [],
        4 * tokens_all * width * (heads + 2) * size,
        16_000_000,
    )(tokens, cosine, sine, w_query, w_key, w_value, g_input, g_query, g_key)

    upward = [(i, i + 1) for i in range(shards - 1)]
    pair_near = lax.ppermute(pair_own, "seq", upward)
    pair_far = lax.ppermute(pair_near[:, rows - far :], "seq", upward[1:])

    window_specs = [
        per_seq(far, 2 * size),
        per_seq(rows, 2 * size),
        per_seq(rows, 2 * size),
        per_seq(rows, 1),
        per_seq(2, 1, span),
    ]
    attend_flops = 8 * tokens_all * heads * span * size
    mixed = call(
        functools.partial(attend_kernel, heads),
        array((seqs, rows, heads * size), low),
        per_seq(rows, heads * size),
        [head_block] + window_specs,
        [pltpu.VMEM((WINDOW + rows, 2 * size), low)],
        attend_flops,
        16_000_000,
    )(query, pair_far, pair_near, pair_own, query_ids, key_ids)

    (
        layer_output,
        pre_low,
        product_low,
        grad_down_low,
        grad_gate_low,
        grad_up_low,
        grad_attended_low,
        grad_hidden,
        grad_mixed,
        grad_gains_middle,
    ) = call(
        functools.partial(middle_kernel, heads, 512),
        [
            array((seqs, rows, width), low),
            array((seqs, rows, width), low),
            array((seqs, rows, units), low),
            array((seqs, rows, width), low),
            array((seqs, rows, units), low),
            array((seqs, rows, units), low),
            array((seqs, rows, width), low),
            array((seqs, rows, width), f32),
            array(q_shape, low),
            array((seqs, 3, width), f32),
        ],
        [
            per_seq(rows, width),
            per_seq(rows, width),
            per_seq(rows, units),
            per_seq(rows, width),
            per_seq(rows, units),
            per_seq(rows, units),
            per_seq(rows, width),
            per_seq(rows, width),
            head_block,
            per_seq(3, width),
        ],
        [
            per_seq(rows, heads * size),
            per_seq(rows, width),
            per_seq(rows, width),
            whole(*w_gate.shape),
            whole(*w_up.shape),
            whole(*w_pair.shape),
            whole(1, width),
            whole(1, width),
            whole(1, width),
        ],
        [pltpu.VMEM((rows, units), f32), pltpu.VMEM((rows, units), f32)],
        4 * tokens_all * width * (heads * size + 3 * units),
        40_000_000,
    )(mixed, tokens, cotangent, w_gate, w_up, w_pair, g_attn, g_pre, g_ffn)

    def flat(values):
        return values.reshape(tokens_all, values.shape[-1])

    def grad_blocks(gradient, inputs):
        product = weight_grad(flat(gradient), flat(inputs)).astype(low)
        return product.reshape(count, -1, product.shape[1])

    back_a = [0] + order_a[:-1]
    back_b = [0] + order_b[:-1]
    gate_up_sum = RowSum(
        [grad_blocks(grad_gate_low, pre_low), grad_blocks(grad_up_low, pre_low)], back_a, -2
    )
    gate_up_core = gate_up_sum.step(back_a[0])
    down_out_sum = RowSum(
        [
            grad_blocks(grad_down_low, product_low),
            grad_blocks(grad_attended_low, mixed),
        ],
        back_b,
        -1,
    )
    down_out_core = down_out_sum.step(back_b[0])

    def at_seq(s, *tail):
        return pl.BlockSpec((1,) + tail, lambda g: (s,) + (0,) * len(tail))

    def seq_call(kernel, outs, out_specs, in_specs, operands, scratch, alias, flops):
        return pl.pallas_call(
            kernel,
            grid=(1,),
            out_shape=outs,
            in_specs=in_specs,
            out_specs=out_specs,
            scratch_shapes=scratch,
            input_output_aliases=alias,
            compiler_params=kernel_params(),
            cost_estimate=pl.CostEstimate(
                flops=flops, bytes_accessed=8_000_000, transcendentals=0
            ),
        )(*operands)

    def attend_back(s, buffer, arrived):
        kinds = [
            array((1, far, 2 * size), low),
            array((1, rows, 2 * size), f32),
            array((1, rows, 2 * size), f32),
            array((seqs, rows, heads * size), low),
            array((1, 1, size), f32),
        ]
        specs = [
            at_seq(0, far, 2 * size),
            at_seq(0, rows, 2 * size),
            at_seq(0, rows, 2 * size),
            at_seq(s, rows, heads * size),
            at_seq(0, 1, size),
        ]
        in_specs = [
            at_seq(s, 2, heads * part, size),
            at_seq(s, 2, heads * part, size),
            at_seq(s, far, 2 * size),
            at_seq(s, rows, 2 * size),
            at_seq(s, rows, 2 * size),
            at_seq(s, rows, 1),
            at_seq(s, 2, 1, span),
            at_seq(s, rows, heads * size),
            at_seq(s, 2, heads * part, size),
            at_seq(s, rows, size // 2),
            at_seq(s, rows, size // 2),
            whole(1, size),
        ]
        operands = [
            query, query_raw, pair_far, pair_near, pair_own, query_ids, key_ids, mixed, grad_mixed,
            cosine, sine, g_query,
        ]
        alias = {}
        extra = list(arrived)
        if buffer is not None:
            alias = {len(operands): 3}
            extra = [buffer] + extra
        return seq_call(
            functools.partial(attend_back_kernel, heads, len(extra)),
            kinds,
            specs,
            in_specs + [anywhere] * len(extra),
            operands + extra,
            [
                pltpu.VMEM((WINDOW + rows, 2 * size), low),
                pltpu.VMEM((WINDOW + rows, 2 * size), f32),
            ],
            alias,
            attend_flops * 3 // seqs,
        )

    downward = [(i + 1, i) for i in range(shards - 1)]
    grad_query_low = None
    arrived = [gate_up_sum.sent]
    far_parts, near_parts, own_parts, query_gains = [], [], [], []
    for s in range(seqs):
        grad_far, grad_near, grad_own, grad_query_low, g_part = attend_back(
            s, grad_query_low, arrived
        )
        from_far = lax.ppermute(grad_far, "seq", downward[1:])
        far_parts.append(from_far)
        near_parts.append(grad_near)
        own_parts.append(grad_own)
        query_gains.append(g_part)
        if s == 0:
            arrived = [gate_up_core, down_out_sum.sent]
        elif s == 1:
            arrived = [down_out_core, far_parts[0]]
    from_near = []
    for s in range(seqs):
        near_sum = near_parts[s] + jnp.pad(
            far_parts[s].astype(f32), ((0, 0), (rows - far, 0), (0, 0))
        )
        from_near.append(lax.ppermute(near_sum.astype(low), "seq", downward))

    gate_up_steps = [gate_up_sum.step(bit) for bit in back_a[1:]]
    down_out_steps = [down_out_sum.step(bit) for bit in back_b[1:]]
    query_sum = RowSum([grad_blocks(grad_query_low, normed)], back_a, -2)
    query_core = query_sum.step(back_a[0])
    grad_normed_query = jnp.dot(
        flat(grad_query_low), w_query, preferred_element_type=f32
    ).reshape(tokens.shape)

    def input_back(s, buffers, arrived):
        kinds = [
            array((seqs, rows, width), f32),
            array((seqs, rows, 2 * size), low),
            array((1, 1, width), f32),
            array((1, 1, size), f32),
        ]
        specs = [
            at_seq(s, rows, width),
            at_seq(s, rows, 2 * size),
            at_seq(0, 1, width),
            at_seq(0, 1, size),
        ]
        in_specs = [
            at_seq(0, rows, 2 * size),
            at_seq(0, rows, 2 * size),
            at_seq(s, rows, size),
            at_seq(s, rows, size // 2),
            at_seq(s, rows, size // 2),
            whole(*w_key.shape),
            whole(*w_value.shape),
            at_seq(s, rows, width),
            at_seq(s, rows, width),
            at_seq(s, rows, width),
            whole(1, width),
            whole(1, size),
        ]
        operands = [
            own_parts[s], from_near[s], key_raw, cosine, sine, w_key, w_value, grad_normed_query,
            tokens, grad_hidden, g_input, g_key,
        ]
        alias = {}
        extra = list(arrived)
        if buffers:
            alias = {len(operands): 0, len(operands) + 1: 1}
            extra = list(buffers) + extra
        return seq_call(
            functools.partial(input_back_kernel, len(extra)),
            kinds,
            specs,
            in_specs + [anywhere] * len(extra),
            operands + extra,
            [],
            alias,
            6 * rows * width * size * 2,
        )

    buffers = []
    input_gains, key_gains = [], []
    waits = [[gate_up_steps[0], query_core], [down_out_steps[0]], [gate_up_steps[-1]]]
    for s in range(seqs):
        *buffers, g_part, g_key_part = input_back(s, buffers, waits[s])
        input_gains.append(g_part)
        key_gains.append(g_key_part)
    input_grad, grad_pair_low = buffers
    pair_blocks = grad_blocks(grad_pair_low, normed).reshape(2, count, key_rows, width)
    grad_gains = jnp.concatenate(
        [
            sum(input_gains).reshape(-1),
            jnp.sum(grad_gains_middle, axis=0).reshape(-1),
            sum(query_gains).reshape(-1),
            sum(key_gains).reshape(-1),
        ]
    )
    gain_block = jnp.pad(
        grad_gains.astype(low).reshape(count, 1, gain_rows),
        ((0, 0), (0, 15), (0, width - gain_rows)),
    )
    rest_sum = RowSum([pair_blocks[0], pair_blocks[1], gain_block], back_b, -2)
    for bit in back_b:
        rest_sum.step(bit)
    for bit in back_a[1:]:
        query_sum.step(bit)
    gate_up_total = seq_sum(gate_up_sum.total())
    down_out_total = seq_sum(down_out_sum.total())
    query_total = seq_sum(query_sum.total())
    rest_total = seq_sum(rest_sum.total())
    units_own = gate_weight.shape[0]
    gate_total = gate_up_total[:units_own]
    up_total = gate_up_total[units_own:]
    down_total = down_out_total[:, :units]
    output_total = down_out_total[:, units:]
    key_total = rest_total[:key_rows]
    value_total = rest_total[key_rows : 2 * key_rows]
    gains_total = rest_total[2 * key_rows, :gain_rows]
    query_momentum, query_variance, query_updated = adam_step(
        query_weight, query_first, query_second, query_total, WEIGHT_DECAY
    )
    key_momentum, key_variance, key_updated = adam_step(
        key_weight, key_first, key_second, key_total, WEIGHT_DECAY
    )
    value_momentum, value_variance, value_updated = adam_step(
        value_weight, value_first, value_second, value_total, WEIGHT_DECAY
    )
    output_momentum, output_variance, output_updated = adam_step(
        output_weight, output_first, output_second, output_total, WEIGHT_DECAY
    )
    gate_momentum, gate_variance, gate_updated = adam_step(
        gate_weight, gate_first, gate_second, gate_total, WEIGHT_DECAY
    )
    up_momentum, up_variance, up_updated = adam_step(
        up_weight, up_first, up_second, up_total, WEIGHT_DECAY
    )
    down_momentum, down_variance, down_updated = adam_step(
        down_weight, down_first, down_second, down_total, WEIGHT_DECAY
    )
    gains_momentum, gains_variance, gains_updated = adam_step(
        norm_gains, gains_first, gains_second, gains_total, 0.0
    )
    return (
        layer_output,
        input_grad,
        query_momentum,
        key_momentum,
        value_momentum,
        output_momentum,
        gate_momentum,
        up_momentum,
        down_momentum,
        gains_momentum,
        query_variance,
        key_variance,
        value_variance,
        output_variance,
        gate_variance,
        up_variance,
        down_variance,
        gains_variance,
        query_updated,
        key_updated,
        value_updated,
        output_updated,
        gate_updated,
        up_updated,
        down_updated,
        gains_updated,
    )


def solution(mesh):
    return jax.shard_map(
        body,
        mesh=mesh,
        in_specs=(
            P("dp", "seq", None),
            P("dp", "seq", None),
            P("dp", None),
            P("dp", "seq"),
            P("dp", None),
            P("dp", None),
            P("dp", None),
            P("dp", None),
            P("dp", None),
            P("dp", None),
            P("dp", None),
            P("dp"),
            P("dp", None),
            P("dp", None),
            P("dp", None),
            P("dp", None),
            P("dp", None),
            P("dp", None),
            P("dp", None),
            P("dp"),
            P("dp", None),
            P("dp", None),
            P("dp", None),
            P("dp", None),
            P("dp", None),
            P("dp", None),
            P("dp", None),
            P("dp"),
        ),
        out_specs=(
            P("dp", "seq", None),
            P("dp", "seq", None),
            P("dp", None),
            P("dp", None),
            P("dp", None),
            P("dp", None),
            P("dp", None),
            P("dp", None),
            P("dp", None),
            P("dp"),
            P("dp", None),
            P("dp", None),
            P("dp", None),
            P("dp", None),
            P("dp", None),
            P("dp", None),
            P("dp", None),
            P("dp"),
            P("dp", None),
            P("dp", None),
            P("dp", None),
            P("dp", None),
            P("dp", None),
            P("dp", None),
            P("dp", None),
            P("dp"),
        ),
        check_vma=False,
    )
```

```python
import functools
import math

import jax
import jax.numpy as jnp
from jax import lax
from jax.experimental import pallas as pl
from jax.experimental.pallas import tpu as pltpu
from jax.sharding import PartitionSpec as P

WINDOW = 512
STEP = 10


NORM_EPSILON = 1e-06
ROPE_BASE = 10000.0
LEARN_RATE = 0.08
BETA_FIRST = 0.9
BETA_SECOND = 0.95
ADAM_EPSILON = 1e-08
WEIGHT_DECAY = 0.01
MASKED_SCORE = -1000000000.0


def frequencies(size):
    return ROPE_BASE ** (-2.0 * jnp.arange(size // 2).astype(jnp.float32) / size)


def weight_grad(gradients, inputs):
    return lax.dot_general(
        gradients, inputs, (((0,), (0,)), ((), ())), preferred_element_type=jnp.float32
    )


def adam_step(weight, first_moment, second_moment, gradient, decay_rate):
    momentum = BETA_FIRST * first_moment + (1.0 - BETA_FIRST) * gradient
    variance = BETA_SECOND * second_moment + (1.0 - BETA_SECOND) * gradient * gradient
    corrected = momentum / (1.0 - BETA_FIRST**STEP)
    scaled = variance / (1.0 - BETA_SECOND**STEP)
    updated = weight - LEARN_RATE * (
        corrected / (jnp.sqrt(scaled) + ADAM_EPSILON) + decay_rate * weight
    )
    return (momentum, variance, updated)


VMEM_BYTES = 56 * 1024 * 1024


def kernel_params():
    return pltpu.CompilerParams(
        dimension_semantics=("arbitrary",), vmem_limit_bytes=VMEM_BYTES
    )


def per_seq(*tail):
    return pl.BlockSpec((1,) + tail, lambda s: (s,) + (0,) * len(tail))


def whole(*shape):
    return pl.BlockSpec(shape, lambda s: (0,) * len(shape), pipeline_mode=pl.Buffered(1))


def dot_nt(a, b):
    return lax.dot_general(a, b, (((1,), (1,)), ((), ())), preferred_element_type=jnp.float32)


def dot_nn(a, b):
    return lax.dot_general(a, b, (((1,), (0,)), ((), ())), preferred_element_type=jnp.float32)


def dot_tn(a, b):
    return lax.dot_general(a, b, (((0,), (0,)), ((), ())), preferred_element_type=jnp.float32)


def inverse_rms(values):
    return lax.rsqrt(jnp.mean(values * values, axis=-1, keepdims=True) + NORM_EPSILON)


def rms_back(values, gain, grad):
    inverse = inverse_rms(values)
    unit = values * inverse
    scaled = grad * (1.0 + gain)
    return (
        inverse * (scaled - unit * jnp.mean(unit * scaled, axis=-1, keepdims=True)),
        jnp.sum(grad * unit, axis=0, keepdims=True),
    )


def turn(values, cosine, sine):
    half = values.shape[-1] // 2
    first, second = values[:, :half], values[:, half:]
    return jnp.concatenate(
        [first * cosine - second * sine, second * cosine + first * sine], axis=-1
    )


def stack_heads(values, heads):
    return jnp.concatenate([values] * heads, axis=0)


def cast_first_kernel(wq_ref, wk_ref, wv_ref, gain_ref, q_ref, rest_ref):
    q_ref[...] = wq_ref[...].astype(jnp.bfloat16)
    width = wq_ref.shape[1]
    gains = gain_ref[...]
    tail = width - gains.shape[1]
    block = jnp.broadcast_to(gains, (16, gains.shape[1]))
    if tail:
        block = jnp.concatenate([block, jnp.zeros((16, tail), jnp.float32)], axis=1)
    rest_ref[...] = jnp.concatenate([wk_ref[...], wv_ref[...], block], axis=0).astype(jnp.bfloat16)


def cast_gate_up_kernel(wg_ref, wu_ref, out_ref):
    rows = wg_ref.shape[0]
    out_ref[:rows, :] = wg_ref[...].astype(jnp.bfloat16)
    out_ref[rows:, :] = wu_ref[...].astype(jnp.bfloat16)


def cast_pair_kernel(waits, wd_ref, wo_ref, *refs):
    pair_ref = refs[waits]
    units = wd_ref.shape[1]
    pair_ref[:, :units] = wd_ref[...].astype(jnp.bfloat16)
    pair_ref[:, units:] = wo_ref[...].astype(jnp.bfloat16)


def stack_kernel(waits, side_ref, own_ref, received_ref, *refs):
    out_ref = refs[waits]
    upper = side_ref[0]
    out_ref[:, upper] = own_ref[...]
    out_ref[:, 1 - upper] = received_ref[...]


def gate_up_grad_kernel(dgate_ref, dup_ref, pre_ref, out_ref):
    rows = dgate_ref.shape[1]
    out_ref[0, :rows, :] = dot_tn(dgate_ref[...], pre_ref[...]).astype(jnp.bfloat16)
    out_ref[0, rows:, :] = dot_tn(dup_ref[...], pre_ref[...]).astype(jnp.bfloat16)


def query_grad_kernel(waits, dq_ref, normed_ref, *refs):
    refs[waits][...] = dot_tn(dq_ref[...], normed_ref[...]).astype(jnp.bfloat16)


def project_kernel(
    heads, x_ref, cos_ref, sin_ref, wq_ref, wk_ref, wv_ref, gi_ref, gq_ref, gk_ref,
    normed_ref, q_ref, qraw_ref, kv_ref, kraw_ref,
):
    x = x_ref[0].astype(jnp.float32)
    size = wk_ref.shape[0]
    rows = x.shape[0]
    part = rows // 2
    normed = (x * inverse_rms(x) * (1.0 + gi_ref[...])).astype(jnp.bfloat16)
    normed_ref[0] = normed
    cosine, sine = cos_ref[0], sin_ref[0]
    k_raw = dot_nt(normed, wk_ref[...])
    kraw_ref[0] = k_raw.astype(jnp.bfloat16)
    key = turn(k_raw * inverse_rms(k_raw) * (1.0 + gk_ref[...]), cosine, sine)
    kv_ref[0, :, :size] = key.astype(jnp.bfloat16)
    kv_ref[0, :, size:] = dot_nt(normed, wv_ref[...]).astype(jnp.bfloat16)
    for head in range(heads):
        raw = dot_nt(normed, wq_ref[head * size : (head + 1) * size, :])
        query = turn(raw * inverse_rms(raw) * (1.0 + gq_ref[...]), cosine, sine)
        query = (query * size ** (-0.5)).astype(jnp.bfloat16)
        raw = raw.astype(jnp.bfloat16)
        for t in range(2):
            span = slice(head * part, (head + 1) * part)
            q_ref[0, t, span, :] = query[t * part : (t + 1) * part]
            qraw_ref[0, t, span, :] = raw[t * part : (t + 1) * part]


def load_window(far_ref, near_ref, own_ref, win_ref):
    far, near = far_ref.shape[1], near_ref.shape[1]
    win_ref[:far, :] = far_ref[0]
    win_ref[far : far + near, :] = near_ref[0]
    win_ref[far + near :, :] = own_ref[0]


def mask_bias(qid_ref, kid_ref, t, part, span):
    ids = qid_ref[0, t * part : (t + 1) * part, :] == kid_ref[0, t]
    row = lax.broadcasted_iota(jnp.int32, (part, span), 0)
    column = lax.broadcasted_iota(jnp.int32, (part, span), 1)
    ok = ids & (column > row) & (column <= row + WINDOW)
    return jnp.where(ok, 0.0, MASKED_SCORE)


def attend_kernel(heads, q_ref, far_ref, near_ref, own_ref, qid_ref, kid_ref, mixed_ref, win_ref):
    size = q_ref.shape[-1]
    part = q_ref.shape[2] // heads
    span = part + WINDOW
    load_window(far_ref, near_ref, own_ref, win_ref)
    for t in range(2):
        bias = mask_bias(qid_ref, kid_ref, t, part, span)
        keys = win_ref[t * part : t * part + span, :size]
        values = win_ref[t * part : t * part + span, size:]
        for head in range(heads):
            scores = dot_nt(q_ref[0, t, head * part : (head + 1) * part, :], keys)
            weights = jnp.exp(scores + bias)
            total = jnp.sum(weights, axis=-1, keepdims=True)
            mixed = dot_nn(weights.astype(jnp.bfloat16), values) / total
            mixed_ref[0, t * part : (t + 1) * part, head * size : (head + 1) * size] = (
                mixed.astype(jnp.bfloat16)
            )


def middle_kernel(
    heads, chunk, mixed_ref, x_ref, cot_ref, wgu_ref, wdo_ref, ga_ref, gp_ref, gf_ref,
    out_ref, pre_ref, product_ref, ddown_ref, dgate_ref, dup_ref, datt_ref, dhid_ref, dmix_ref, dg_ref,
    act_ref, slope_ref,
):
    shard = wgu_ref.shape[1] // 2
    units = wgu_ref.shape[0] * shard
    group = chunk // shard

    def gate_up_rows(start, which):
        first = start // shard
        picked = wgu_ref[first : first + group, which * shard : (which + 1) * shard, :]
        return picked.reshape(chunk, picked.shape[-1])

    size = dmix_ref.shape[-1]
    part = dmix_ref.shape[2] // heads
    x = x_ref[0].astype(jnp.float32)
    attended = dot_nt(mixed_ref[0], wdo_ref[:, units:])
    hidden = x + attended * inverse_rms(attended) * (1.0 + ga_ref[...])
    pre = (hidden * inverse_rms(hidden) * (1.0 + gp_ref[...])).astype(jnp.bfloat16)
    pre_ref[0] = pre
    down = jnp.zeros(x.shape, jnp.float32)
    root = (2.0 / math.pi) ** 0.5
    for start in range(0, units, chunk):
        span = slice(start, start + chunk)
        gate = dot_nt(pre, gate_up_rows(start, 0))
        up = dot_nt(pre, gate_up_rows(start, 1))
        square = gate * gate
        bend = jnp.tanh(gate * (root + (root * 0.044715) * square))
        half = 0.5 + 0.5 * bend
        act = gate * half
        slope = half + act * (1.0 - bend) * (root + (3.0 * root * 0.044715) * square)
        act_ref[:, span] = act
        slope_ref[:, span] = up * slope
        product = (act * up).astype(jnp.bfloat16)
        product_ref[0, :, span] = product
        down += dot_nt(product, wdo_ref[:, span])
    out_ref[0] = (hidden + down * inverse_rms(down) * (1.0 + gf_ref[...])).astype(jnp.bfloat16)
    dy = cot_ref[0].astype(jnp.float32)
    d_down, dg_ffn = rms_back(down, gf_ref[...], dy)
    d_down = d_down.astype(jnp.bfloat16)
    ddown_ref[0] = d_down
    d_pre = jnp.zeros(x.shape, jnp.float32)
    for start in range(0, units, chunk):
        span = slice(start, start + chunk)
        d_product = dot_nn(d_down, wdo_ref[:, span])
        d_gate = (d_product * slope_ref[:, span]).astype(jnp.bfloat16)
        d_up = (d_product * act_ref[:, span]).astype(jnp.bfloat16)
        dgate_ref[0, :, span] = d_gate
        dup_ref[0, :, span] = d_up
        d_pre += dot_nn(d_gate, gate_up_rows(start, 0)) + dot_nn(
            d_up, gate_up_rows(start, 1)
        )
    d_hidden, dg_pre = rms_back(hidden, gp_ref[...], d_pre)
    d_hidden = dy + d_hidden
    dhid_ref[0] = d_hidden
    d_att, dg_attn = rms_back(attended, ga_ref[...], d_hidden)
    d_att = d_att.astype(jnp.bfloat16)
    datt_ref[0] = d_att
    dg_ref[0] = jnp.concatenate([dg_attn, dg_pre, dg_ffn], axis=0)
    for head in range(heads):
        d_mixed = dot_nn(
            d_att, wdo_ref[:, units + head * size : units + (head + 1) * size]
        ).astype(jnp.bfloat16)
        for t in range(2):
            dmix_ref[0, t, head * part : (head + 1) * part, :] = d_mixed[t * part : (t + 1) * part]


def attend_back_kernel(
    heads, waits, q_ref, qraw_ref, far_ref, near_ref, own_ref, qid_ref, kid_ref, mixed_ref, dmix_ref,
    cos_ref, sin_ref, gq_ref, *refs
):
    dfar_ref, dnear_ref, down_ref, dqraw_ref, dg_ref, win_ref, grad_ref = refs[waits:]
    size = q_ref.shape[-1]
    part = q_ref.shape[2] // heads
    span = part + WINDOW
    far, near = far_ref.shape[1], near_ref.shape[1]
    load_window(far_ref, near_ref, own_ref, win_ref)
    grad_ref[...] = jnp.zeros_like(grad_ref)
    dg = jnp.zeros((1, size), jnp.float32)
    for t in range(2):
        rows = slice(t * part, (t + 1) * part)
        window = slice(t * part, t * part + span)
        bias = mask_bias(qid_ref, kid_ref, t, part, span)
        keys = win_ref[window, :size]
        values = win_ref[window, size:]
        cosine, sine = cos_ref[0, rows, :], sin_ref[0, rows, :]
        for head in range(heads):
            line = slice(head * part, (head + 1) * part)
            lanes = slice(head * size, (head + 1) * size)
            query = q_ref[0, t, line, :]
            d_out = dmix_ref[0, t, line, :]
            weights = jnp.exp(dot_nt(query, keys) + bias)
            weights = weights * (1.0 / jnp.sum(weights, axis=-1, keepdims=True))
            delta = jnp.sum(
                d_out.astype(jnp.float32) * mixed_ref[0, rows, lanes].astype(jnp.float32),
                axis=-1,
                keepdims=True,
            )
            d_scores = (weights * (dot_nt(d_out, values) - delta)).astype(jnp.bfloat16)
            weights = weights.astype(jnp.bfloat16)
            grad_ref[window, :size] += dot_tn(d_scores, query)
            grad_ref[window, size:] += dot_tn(weights, d_out)
            d_query = dot_nn(d_scores, keys) * size ** (-0.5)
            d_raw, part_g = rms_back(
                qraw_ref[0, t, line, :].astype(jnp.float32),
                gq_ref[...],
                turn(d_query, cosine, -sine),
            )
            dqraw_ref[0, rows, lanes] = d_raw.astype(jnp.bfloat16)
            dg += part_g
    dg_ref[0] = dg
    dfar_ref[0] = grad_ref[:far, :].astype(jnp.bfloat16)
    dnear_ref[0] = grad_ref[far : far + near, :]
    down_ref[0] = grad_ref[far + near :, :]


def input_back_kernel(
    waits, own_ref, recv_ref, kraw_ref, cos_ref, sin_ref, wk_ref, wv_ref, dq_ref, wq_ref, x_ref, dhid_ref,
    gi_ref, gk_ref, *refs
):
    grad_ref, dpair_ref, dgi_ref, dgk_ref = refs[waits:]
    size = wk_ref.shape[0]
    total = own_ref[0] + recv_ref[0].astype(jnp.float32)
    d_key = turn(total[:, :size], cos_ref[0], -sin_ref[0])
    d_raw, dg_key = rms_back(kraw_ref[0].astype(jnp.float32), gk_ref[...], d_key)
    d_raw = d_raw.astype(jnp.bfloat16)
    d_value = total[:, size:].astype(jnp.bfloat16)
    dpair_ref[0, :, :size] = d_raw
    dpair_ref[0, :, size:] = d_value
    d_normed = dot_nn(dq_ref[0], wq_ref[...])
    d_normed += dot_nn(d_raw, wk_ref[...]) + dot_nn(d_value, wv_ref[...])
    d_x, dg_input = rms_back(x_ref[0].astype(jnp.float32), gi_ref[...], d_normed)
    grad_ref[0] = dhid_ref[0] + d_x
    dgi_ref[0] = dg_input
    dgk_ref[0] = dg_key


def flips(bit):
    return [(i, i ^ (1 << bit)) for i in range(lax.axis_size("dp"))]


def side(bit):
    return (lax.axis_index("dp") >> bit) & 1


def gather_rows(shard, order):
    current, done, steps = shard, [], []
    for bit in order:
        received = lax.ppermute(current, "dp", flips(bit))
        steps.append(received)
        upper = side(bit) == 1
        axis = sum(1 for other in done if other > bit)
        current = jnp.stack(
            [jnp.where(upper, received, current), jnp.where(upper, current, received)], axis=axis
        )
        done.append(bit)
    return current.reshape((lax.axis_size("dp"),) + shard.shape), steps


class RowSum:
    def __init__(self, parts, order, axis):
        self.terms = [
            (part.reshape((2,) * len(order) + part.shape[1:]), list(range(len(order) - 1, -1, -1)))
            for part in parts
        ]
        self.join = axis
        self.order = order
        self.chosen = {}
        self.received = []

    def total(self, other=None):
        picks = dict(self.chosen)
        if other is not None:
            picks[other] = 1 - side(other)
        pieces = [self.pick(part, bits, picks) for part, bits in self.terms]
        value = jnp.concatenate(pieces, axis=self.join) if len(pieces) > 1 else pieces[0]
        value = value.astype(jnp.float32)
        for part, bits in self.received:
            value += self.pick(part, bits, picks).astype(jnp.float32)
        return value.astype(jnp.bfloat16)

    def pick(self, part, bits, picks):
        bits = list(bits)
        for bit, where in picks.items():
            if bit in bits:
                part = lax.dynamic_index_in_dim(part, where, bits.index(bit), keepdims=False)
                bits.remove(bit)
        return part

    def send(self, bit):
        self.sent = self.total(bit)
        return self.sent

    def step(self, bit):
        received = lax.ppermute(self.send(bit), "dp", flips(bit))
        self.chosen[bit] = side(bit)
        left = [b for b in range(len(self.order) - 1, -1, -1) if b not in self.chosen]
        self.received.append((received, left))
        return received


def seq_sum(part):
    count = lax.axis_size("seq")
    index = lax.axis_index("seq")
    half = count // 2
    terms = [part]

    def total():
        return sum(term.astype(jnp.float32) for term in terms)

    for t in range(half - 1):
        pairs = [(t, t + 1), (count - 1 - t, count - 2 - t)]
        terms.append(lax.ppermute(total().astype(jnp.bfloat16), "seq", pairs))
    middle = [(half - 1, half), (half, half - 1)]
    terms.append(lax.ppermute(total().astype(jnp.bfloat16), "seq", middle))
    result = total()
    for t in range(half - 2, -1, -1):
        pairs = [(t + 1, t), (count - 2 - t, count - 1 - t)]
        received = lax.ppermute(result.astype(jnp.bfloat16), "seq", pairs)
        outer = (index == t) | (index == count - 1 - t)
        result = jnp.where(outer, received.astype(jnp.float32), result)
    return result


def body(
    tokens,
    cotangent,
    segments,
    positions,
    query_weight,
    key_weight,
    value_weight,
    output_weight,
    gate_weight,
    up_weight,
    down_weight,
    norm_gains,
    query_first,
    key_first,
    value_first,
    output_first,
    gate_first,
    up_first,
    down_first,
    gains_first,
    query_second,
    key_second,
    value_second,
    output_second,
    gate_second,
    up_second,
    down_second,
    gains_second,
):
    count = lax.axis_size("dp")
    bits = (count - 1).bit_length()
    order_a = list(range(1, bits)) + [0]
    order_b = list(range(bits - 1, 0, -1)) + [0]
    low = jnp.bfloat16
    f32 = jnp.float32
    width = tokens.shape[2]
    key_rows = key_weight.shape[0]
    gain_rows = norm_gains.shape[0]
    rest_rows = 2 * key_rows + 16

    def array(shape, kind):
        return jax.ShapeDtypeStruct(shape, kind)

    query_shard, rest_shard = pl.pallas_call(
        cast_first_kernel,
        out_shape=[array(query_weight.shape, low), array((rest_rows, width), low)],
    )(query_weight, key_weight, value_weight, norm_gains[None])
    query_all, query_steps = gather_rows(query_shard, order_a)
    rest_all, rest_steps = gather_rows(rest_shard, order_b)
    w_query = query_all.reshape(-1, width)
    w_key = rest_all[:, :key_rows].reshape(-1, width)
    w_value = rest_all[:, key_rows : 2 * key_rows].reshape(-1, width)
    gains_all = rest_all[:, 2 * key_rows, :gain_rows].reshape(-1)
    block = pl.BlockSpec(memory_space=pltpu.VMEM)
    anywhere = pl.BlockSpec(memory_space=pl.ANY)
    gate_up_shard = pl.pallas_call(
        cast_gate_up_kernel,
        out_shape=array((2 * gate_weight.shape[0], width), low),
    )(gate_weight, up_weight)
    gate_up_all = lax.all_gather(gate_up_shard, "dp", axis=0)
    arrived = [query_steps[-2], rest_steps[-2]]
    pair_shard = pl.pallas_call(
        functools.partial(cast_pair_kernel, len(arrived)),
        out_shape=array(
            (down_weight.shape[0], down_weight.shape[1] + output_weight.shape[1]), low
        ),
        in_specs=[block] * 2 + [anywhere] * len(arrived),
    )(down_weight, output_weight, *arrived)

    def stack_pair(own, received, bit, arrived):
        shape = own.shape
        return pl.pallas_call(
            functools.partial(stack_kernel, len(arrived)),
            out_shape=array((shape[0], 2) + shape[1:], low),
            in_specs=[pl.BlockSpec(memory_space=pltpu.SMEM)]
            + [block] * 2
            + [anywhere] * len(arrived),
            compiler_params=pltpu.CompilerParams(vmem_limit_bytes=VMEM_BYTES),
        )(side(bit)[None].astype(jnp.int32), own, received, *arrived).reshape(
            (2 * shape[0],) + shape[1:]
        )

    seqs, rows, _ = tokens.shape
    size = w_key.shape[0]
    heads = w_query.shape[0] // size
    units = down_weight.shape[1]
    shards = lax.axis_size("seq")
    far = WINDOW - rows
    part = rows // 2
    span = part + WINDOW
    gains_float = gains_all.astype(jnp.float32)[None]
    g_input, g_attn, g_pre, g_ffn = (
        gains_float[:, i * width : (i + 1) * width] for i in range(4)
    )
    g_query = gains_float[:, 4 * width : 4 * width + size]
    g_key = gains_float[:, 4 * width + size : 4 * width + 2 * size]
    angles = positions.astype(jnp.float32)[..., None] * frequencies(size)
    cosine, sine = jnp.cos(angles), jnp.sin(angles)
    first_row = lax.axis_index("seq") * rows
    padded = jnp.concatenate([jnp.full((seqs, WINDOW), -1, jnp.int32), segments], axis=1)
    window_ids = lax.dynamic_slice_in_dim(padded, first_row, WINDOW + rows, 1)
    query_ids = window_ids[:, WINDOW:, None]
    key_ids = jnp.stack([window_ids[:, :span], window_ids[:, part:]], axis=1)[:, :, None, :]

    def call(kernel, outs, out_specs, in_specs, scratch, flops, moved):
        return pl.pallas_call(
            kernel,
            grid=(seqs,),
            out_shape=outs,
            in_specs=in_specs,
            out_specs=out_specs,
            scratch_shapes=scratch,
            compiler_params=kernel_params(),
            cost_estimate=pl.CostEstimate(flops=flops, bytes_accessed=moved, transcendentals=0),
        )

    tokens_all = seqs * rows
    head_block = per_seq(2, heads * part, size)
    q_shape = (seqs, 2, heads * part, size)
    normed, query, query_raw, pair_own, key_raw = call(
        functools.partial(project_kernel, heads),
        [
            array((seqs, rows, width), low),
            array(q_shape, low),
            array(q_shape, low),
            array((seqs, rows, 2 * size), low),
            array((seqs, rows, size), low),
        ],
        [per_seq(rows, width), head_block, head_block, per_seq(rows, 2 * size), per_seq(rows, size)],
        [
            per_seq(rows, width),
            per_seq(rows, size // 2),
            per_seq(rows, size // 2),
            whole(*w_query.shape),
            whole(*w_key.shape),
            whole(*w_value.shape),
            whole(1, width),
            whole(1, size),
            whole(1, size),
        ],
        [],
        4 * tokens_all * width * (heads + 2) * size,
        16_000_000,
    )(tokens, cosine, sine, w_query, w_key, w_value, g_input, g_query, g_key)

    upward = [(i, i + 1) for i in range(shards - 1)]
    pair_near = lax.ppermute(pair_own, "seq", upward)
    far_send = pair_near[:, rows - far :]
    pair_far = lax.ppermute(far_send, "seq", upward[1:])
    pair_stack = pair_shard[None]
    for bit in order_b:
        received = lax.ppermute(pair_stack, "dp", flips(bit))
        if bit == order_b[0]:
            waits = [pair_own]
        elif bit == order_b[-2]:
            waits = [far_send]
        else:
            waits = []
        pair_stack = stack_pair(pair_stack, received, bit, waits)
    w_pair = pair_stack.reshape(-1, pair_stack.shape[-1])

    window_specs = [
        per_seq(far, 2 * size),
        per_seq(rows, 2 * size),
        per_seq(rows, 2 * size),
        per_seq(rows, 1),
        per_seq(2, 1, span),
    ]
    attend_flops = 8 * tokens_all * heads * span * size
    mixed = call(
        functools.partial(attend_kernel, heads),
        array((seqs, rows, heads * size), low),
        per_seq(rows, heads * size),
        [head_block] + window_specs,
        [pltpu.VMEM((WINDOW + rows, 2 * size), low)],
        attend_flops,
        16_000_000,
    )(query, pair_far, pair_near, pair_own, query_ids, key_ids)

    (
        layer_output,
        pre_low,
        product_low,
        grad_down_low,
        grad_gate_low,
        grad_up_low,
        grad_attended_low,
        grad_hidden,
        grad_mixed,
        grad_gains_middle,
    ) = call(
        functools.partial(middle_kernel, heads, 512),
        [
            array((seqs, rows, width), low),
            array((seqs, rows, width), low),
            array((seqs, rows, units), low),
            array((seqs, rows, width), low),
            array((seqs, rows, units), low),
            array((seqs, rows, units), low),
            array((seqs, rows, width), low),
            array((seqs, rows, width), f32),
            array(q_shape, low),
            array((seqs, 3, width), f32),
        ],
        [
            per_seq(rows, width),
            per_seq(rows, width),
            per_seq(rows, units),
            per_seq(rows, width),
            per_seq(rows, units),
            per_seq(rows, units),
            per_seq(rows, width),
            per_seq(rows, width),
            head_block,
            per_seq(3, width),
        ],
        [
            per_seq(rows, heads * size),
            per_seq(rows, width),
            per_seq(rows, width),
            whole(*gate_up_all.shape),
            whole(*w_pair.shape),
            whole(1, width),
            whole(1, width),
            whole(1, width),
        ],
        [pltpu.VMEM((rows, units), f32), pltpu.VMEM((rows, units), f32)],
        4 * tokens_all * width * (heads * size + 3 * units),
        40_000_000,
    )(mixed, tokens, cotangent, gate_up_all, w_pair, g_attn, g_pre, g_ffn)

    def flat(values):
        return values.reshape(tokens_all, values.shape[-1])

    def grad_blocks(gradient, inputs):
        product = weight_grad(flat(gradient), flat(inputs)).astype(low)
        return product.reshape(count, -1, product.shape[1])

    back_a = [0] + order_a[:-1]
    back_b = [0] + order_b[:-1]
    shard_units = gate_weight.shape[0]
    if shard_units % 128 == 0:
        gate_up_blocks = pl.pallas_call(
            gate_up_grad_kernel,
            grid=(count,),
            out_shape=array((count, 2 * shard_units, width), low),
            in_specs=[
                pl.BlockSpec((tokens_all, shard_units), lambda i: (0, i)),
                pl.BlockSpec((tokens_all, shard_units), lambda i: (0, i)),
                whole(tokens_all, width),
            ],
            out_specs=pl.BlockSpec((1, 2 * shard_units, width), lambda i: (i, 0, 0)),
            compiler_params=kernel_params(),
            cost_estimate=pl.CostEstimate(
                flops=4 * tokens_all * width * units, bytes_accessed=14_000_000, transcendentals=0
            ),
        )(flat(grad_gate_low), flat(grad_up_low), flat(pre_low))
    else:
        gate_up_blocks = jnp.concatenate(
            [grad_blocks(grad_gate_low, pre_low), grad_blocks(grad_up_low, pre_low)], axis=1
        )
    gate_up_part = lax.psum_scatter(gate_up_blocks, "dp", scatter_dimension=0, tiled=False)
    down_out_sum = RowSum(
        [
            grad_blocks(grad_down_low, product_low),
            grad_blocks(grad_attended_low, mixed),
        ],
        back_b,
        -1,
    )
    down_out_core = down_out_sum.step(back_b[0])

    def at_seq(s, *tail):
        return pl.BlockSpec((1,) + tail, lambda g: (s,) + (0,) * len(tail))

    def seq_call(kernel, outs, out_specs, in_specs, operands, scratch, alias, flops):
        return pl.pallas_call(
            kernel,
            grid=(1,),
            out_shape=outs,
            in_specs=in_specs,
            out_specs=out_specs,
            scratch_shapes=scratch,
            input_output_aliases=alias,
            compiler_params=kernel_params(),
            cost_estimate=pl.CostEstimate(
                flops=flops, bytes_accessed=8_000_000, transcendentals=0
            ),
        )(*operands)

    def attend_back(s, buffer, arrived):
        kinds = [
            array((1, far, 2 * size), low),
            array((1, rows, 2 * size), f32),
            array((1, rows, 2 * size), f32),
            array((seqs, rows, heads * size), low),
            array((1, 1, size), f32),
        ]
        specs = [
            at_seq(0, far, 2 * size),
            at_seq(0, rows, 2 * size),
            at_seq(0, rows, 2 * size),
            at_seq(s, rows, heads * size),
            at_seq(0, 1, size),
        ]
        in_specs = [
            at_seq(s, 2, heads * part, size),
            at_seq(s, 2, heads * part, size),
            at_seq(s, far, 2 * size),
            at_seq(s, rows, 2 * size),
            at_seq(s, rows, 2 * size),
            at_seq(s, rows, 1),
            at_seq(s, 2, 1, span),
            at_seq(s, rows, heads * size),
            at_seq(s, 2, heads * part, size),
            at_seq(s, rows, size // 2),
            at_seq(s, rows, size // 2),
            whole(1, size),
        ]
        operands = [
            query, query_raw, pair_far, pair_near, pair_own, query_ids, key_ids, mixed, grad_mixed,
            cosine, sine, g_query,
        ]
        alias = {}
        extra = list(arrived)
        if buffer is not None:
            alias = {len(operands): 3}
            extra = [buffer] + extra
        return seq_call(
            functools.partial(attend_back_kernel, heads, len(extra)),
            kinds,
            specs,
            in_specs + [anywhere] * len(extra),
            operands + extra,
            [
                pltpu.VMEM((WINDOW + rows, 2 * size), low),
                pltpu.VMEM((WINDOW + rows, 2 * size), f32),
            ],
            alias,
            attend_flops * 3 // seqs,
        )

    downward = [(i + 1, i) for i in range(shards - 1)]
    grad_query_low = None
    arrived = [down_out_sum.sent]
    own_parts, query_gains, near_sums, from_near = [], [], [], []
    for s in range(seqs):
        grad_far, grad_near, grad_own, grad_query_low, g_part = attend_back(
            s, grad_query_low, arrived
        )
        from_far = lax.ppermute(grad_far, "seq", downward[1:])
        own_parts.append(grad_own)
        query_gains.append(g_part)
        near_sum = (
            grad_near
            + jnp.pad(from_far.astype(f32), ((0, 0), (rows - far, 0), (0, 0)))
        ).astype(low)
        near_sums.append(near_sum)
        from_near.append(lax.ppermute(near_sum, "seq", downward))
        if s == 0:
            down_out_sum.step(back_b[1])
            arrived = [down_out_sum.sent, near_sums[0]]
        elif s == 1:
            arrived = [from_near[0]]
    query_columns = heads * size
    grad_w_query = pl.pallas_call(
        functools.partial(query_grad_kernel, 1),
        grid=(heads,),
        out_shape=array((query_columns, width), low),
        in_specs=[
            pl.BlockSpec((tokens_all, size), lambda i: (0, i)),
            whole(tokens_all, width),
            anywhere,
        ],
        out_specs=pl.BlockSpec((size, width), lambda i: (i, 0)),
        compiler_params=kernel_params(),
        cost_estimate=pl.CostEstimate(
            flops=2 * tokens_all * width * query_columns, bytes_accessed=5_000_000, transcendentals=0
        ),
    )(flat(grad_query_low), flat(normed), near_sums[1])
    for bit in back_b[2:]:
        down_out_sum.step(bit)
    down_out_last = down_out_sum.received[-1][0]

    def input_back(s, buffers, arrived):
        kinds = [
            array((seqs, rows, width), f32),
            array((seqs, rows, 2 * size), low),
            array((1, 1, width), f32),
            array((1, 1, size), f32),
        ]
        specs = [
            at_seq(s, rows, width),
            at_seq(s, rows, 2 * size),
            at_seq(0, 1, width),
            at_seq(0, 1, size),
        ]
        in_specs = [
            at_seq(0, rows, 2 * size),
            at_seq(0, rows, 2 * size),
            at_seq(s, rows, size),
            at_seq(s, rows, size // 2),
            at_seq(s, rows, size // 2),
            whole(*w_key.shape),
            whole(*w_value.shape),
            at_seq(s, rows, heads * size),
            whole(*w_query.shape),
            at_seq(s, rows, width),
            at_seq(s, rows, width),
            whole(1, width),
            whole(1, size),
        ]
        operands = [
            own_parts[s], from_near[s], key_raw, cosine, sine, w_key, w_value, grad_query_low,
            w_query, tokens, grad_hidden, g_input, g_key,
        ]
        alias = {}
        extra = list(arrived)
        if buffers:
            alias = {len(operands): 0, len(operands) + 1: 1}
            extra = list(buffers) + extra
        return seq_call(
            functools.partial(input_back_kernel, len(extra)),
            kinds,
            specs,
            in_specs + [anywhere] * len(extra),
            operands + extra,
            [],
            alias,
            2 * rows * width * size * (heads + 2),
        )

    buffers = []
    input_gains, key_gains = [], []
    waits = [[grad_w_query, near_sums[-1]], [down_out_sum.sent], [down_out_last]]
    waits += [[]] * seqs
    for s in range(seqs):
        *buffers, g_part, g_key_part = input_back(s, buffers, waits[s])
        input_gains.append(g_part)
        key_gains.append(g_key_part)
    input_grad, grad_pair_low = buffers
    pair_blocks = grad_blocks(grad_pair_low, normed).reshape(2, count, key_rows, width)
    grad_gains = jnp.concatenate(
        [
            sum(input_gains).reshape(-1),
            jnp.sum(grad_gains_middle, axis=0).reshape(-1),
            sum(query_gains).reshape(-1),
            sum(key_gains).reshape(-1),
        ]
    )
    gain_block = jnp.pad(
        grad_gains.astype(low).reshape(count, 1, gain_rows),
        ((0, 0), (0, 15), (0, width - gain_rows)),
    )
    query_rows = query_weight.shape[0]
    rest_sum = RowSum(
        [grad_w_query.reshape(count, query_rows, width), pair_blocks[0], pair_blocks[1], gain_block],
        back_b,
        -2,
    )
    for bit in back_b:
        rest_sum.step(bit)
    down_out_total = seq_sum(down_out_sum.total())
    gate_total = seq_sum(gate_up_part[:shard_units])
    up_total = seq_sum(gate_up_part[shard_units:])
    rest_total = seq_sum(rest_sum.total())
    query_total = rest_total[:query_rows]
    rest_total = rest_total[query_rows:]
    down_total = down_out_total[:, :units]
    output_total = down_out_total[:, units:]
    key_total = rest_total[:key_rows]
    value_total = rest_total[key_rows : 2 * key_rows]
    gains_total = rest_total[2 * key_rows, :gain_rows]
    query_momentum, query_variance, query_updated = adam_step(
        query_weight, query_first, query_second, query_total, WEIGHT_DECAY
    )
    key_momentum, key_variance, key_updated = adam_step(
        key_weight, key_first, key_second, key_total, WEIGHT_DECAY
    )
    value_momentum, value_variance, value_updated = adam_step(
        value_weight, value_first, value_second, value_total, WEIGHT_DECAY
    )
    output_momentum, output_variance, output_updated = adam_step(
        output_weight, output_first, output_second, output_total, WEIGHT_DECAY
    )
    gate_momentum, gate_variance, gate_updated = adam_step(
        gate_weight, gate_first, gate_second, gate_total, WEIGHT_DECAY
    )
    up_momentum, up_variance, up_updated = adam_step(
        up_weight, up_first, up_second, up_total, WEIGHT_DECAY
    )
    down_momentum, down_variance, down_updated = adam_step(
        down_weight, down_first, down_second, down_total, WEIGHT_DECAY
    )
    gains_momentum, gains_variance, gains_updated = adam_step(
        norm_gains, gains_first, gains_second, gains_total, 0.0
    )
    return (
        layer_output,
        input_grad,
        query_momentum,
        key_momentum,
        value_momentum,
        output_momentum,
        gate_momentum,
        up_momentum,
        down_momentum,
        gains_momentum,
        query_variance,
        key_variance,
        value_variance,
        output_variance,
        gate_variance,
        up_variance,
        down_variance,
        gains_variance,
        query_updated,
        key_updated,
        value_updated,
        output_updated,
        gate_updated,
        up_updated,
        down_updated,
        gains_updated,
    )


def solution(mesh):
    return jax.shard_map(
        body,
        mesh=mesh,
        in_specs=(
            P("dp", "seq", None),
            P("dp", "seq", None),
            P("dp", None),
            P("dp", "seq"),
            P("dp", None),
            P("dp", None),
            P("dp", None),
            P("dp", None),
            P("dp", None),
            P("dp", None),
            P("dp", None),
            P("dp"),
            P("dp", None),
            P("dp", None),
            P("dp", None),
            P("dp", None),
            P("dp", None),
            P("dp", None),
            P("dp", None),
            P("dp"),
            P("dp", None),
            P("dp", None),
            P("dp", None),
            P("dp", None),
            P("dp", None),
            P("dp", None),
            P("dp", None),
            P("dp"),
        ),
        out_specs=(
            P("dp", "seq", None),
            P("dp", "seq", None),
            P("dp", None),
            P("dp", None),
            P("dp", None),
            P("dp", None),
            P("dp", None),
            P("dp", None),
            P("dp", None),
            P("dp"),
            P("dp", None),
            P("dp", None),
            P("dp", None),
            P("dp", None),
            P("dp", None),
            P("dp", None),
            P("dp", None),
            P("dp"),
            P("dp", None),
            P("dp", None),
            P("dp", None),
            P("dp", None),
            P("dp", None),
            P("dp", None),
            P("dp", None),
            P("dp"),
        ),
        check_vma=False,
    )
```

```python
import functools
import math

import jax
import jax.numpy as jnp
from jax import lax
from jax.experimental import pallas as pl
from jax.experimental.pallas import tpu as pltpu
from jax.sharding import PartitionSpec as P

WINDOW = 512
STEP = 10


NORM_EPSILON = 1e-06
ROPE_BASE = 10000.0
LEARN_RATE = 0.08
BETA_FIRST = 0.9
BETA_SECOND = 0.95
ADAM_EPSILON = 1e-08
WEIGHT_DECAY = 0.01
MASKED_SCORE = -1000000000.0


def frequencies(size):
    return ROPE_BASE ** (-2.0 * jnp.arange(size // 2).astype(jnp.float32) / size)


def weight_grad(gradients, inputs):
    return lax.dot_general(
        gradients, inputs, (((0,), (0,)), ((), ())), preferred_element_type=jnp.float32
    )


def adam_step(weight, first_moment, second_moment, gradient, decay_rate):
    momentum = BETA_FIRST * first_moment + (1.0 - BETA_FIRST) * gradient
    variance = BETA_SECOND * second_moment + (1.0 - BETA_SECOND) * gradient * gradient
    corrected = momentum / (1.0 - BETA_FIRST**STEP)
    scaled = variance / (1.0 - BETA_SECOND**STEP)
    updated = weight - LEARN_RATE * (
        corrected / (jnp.sqrt(scaled) + ADAM_EPSILON) + decay_rate * weight
    )
    return (momentum, variance, updated)


VMEM_BYTES = 56 * 1024 * 1024


def kernel_params():
    return pltpu.CompilerParams(
        dimension_semantics=("arbitrary",), vmem_limit_bytes=VMEM_BYTES
    )


def per_seq(*tail):
    return pl.BlockSpec((1,) + tail, lambda s: (s,) + (0,) * len(tail))


def whole(*shape):
    return pl.BlockSpec(shape, lambda s: (0,) * len(shape), pipeline_mode=pl.Buffered(1))


def dot_nt(a, b):
    return lax.dot_general(a, b, (((1,), (1,)), ((), ())), preferred_element_type=jnp.float32)


def dot_nn(a, b):
    return lax.dot_general(a, b, (((1,), (0,)), ((), ())), preferred_element_type=jnp.float32)


def dot_tn(a, b):
    return lax.dot_general(a, b, (((0,), (0,)), ((), ())), preferred_element_type=jnp.float32)


def inverse_rms(values):
    return lax.rsqrt(jnp.mean(values * values, axis=-1, keepdims=True) + NORM_EPSILON)


def rms_back(values, gain, grad):
    inverse = inverse_rms(values)
    unit = values * inverse
    scaled = grad * (1.0 + gain)
    return (
        inverse * (scaled - unit * jnp.mean(unit * scaled, axis=-1, keepdims=True)),
        jnp.sum(grad * unit, axis=0, keepdims=True),
    )


def turn(values, cosine, sine):
    half = values.shape[-1] // 2
    first, second = values[:, :half], values[:, half:]
    return jnp.concatenate(
        [first * cosine - second * sine, second * cosine + first * sine], axis=-1
    )


def stack_heads(values, heads):
    return jnp.concatenate([values] * heads, axis=0)


def cast_first_kernel(wq_ref, wk_ref, wv_ref, gain_ref, q_ref, rest_ref):
    q_ref[...] = wq_ref[...].astype(jnp.bfloat16)
    width = wq_ref.shape[1]
    gains = gain_ref[...]
    tail = width - gains.shape[1]
    block = jnp.broadcast_to(gains, (16, gains.shape[1]))
    if tail:
        block = jnp.concatenate([block, jnp.zeros((16, tail), jnp.float32)], axis=1)
    rest_ref[...] = jnp.concatenate([wk_ref[...], wv_ref[...], block], axis=0).astype(jnp.bfloat16)


def cast_rest_kernel(waits, wg_ref, wu_ref, wd_ref, wo_ref, *refs):
    out_ref, pair_ref = refs[waits:]
    rows = wg_ref.shape[0]
    units = wd_ref.shape[1]
    out_ref[:rows, :] = wg_ref[...].astype(jnp.bfloat16)
    out_ref[rows:, :] = wu_ref[...].astype(jnp.bfloat16)
    pair_ref[:, :units] = wd_ref[...].astype(jnp.bfloat16)
    pair_ref[:, units:] = wo_ref[...].astype(jnp.bfloat16)


def stack_kernel(axis, waits, side_ref, own_ref, received_ref, *refs):
    out_ref, sems = refs[waits:]
    upper = side_ref[0]
    lead = (slice(None),) * axis
    mine = pltpu.make_async_copy(own_ref, out_ref.at[lead + (upper,)], sems.at[0])
    other = pltpu.make_async_copy(received_ref, out_ref.at[lead + (1 - upper,)], sems.at[1])
    mine.start()
    other.start()
    mine.wait()
    other.wait()


def tail_rows_kernel(waits, near_ref, *refs):
    out_ref, sem = refs[waits:]
    rows = out_ref.shape[1]
    copy = pltpu.make_async_copy(near_ref.at[:, near_ref.shape[1] - rows :], out_ref, sem)
    copy.start()
    copy.wait()


def gate_up_grad_kernel(side_ref, dgate_ref, dup_ref, pre_ref, after_ref, send_ref, keep_ref, turned_ref):
    step = pl.program_id(0)
    half = pl.num_programs(0) // 2
    rows = dgate_ref.shape[1]

    @pl.when(step == 0)
    def _():
        turned_ref[...] = pre_ref[...].T

    gate = dot_nn(turned_ref[...], dgate_ref[...]).astype(jnp.bfloat16)
    up = dot_nn(turned_ref[...], dup_ref[...]).astype(jnp.bfloat16)

    @pl.when(step < half)
    def _():
        send_ref[0, :, :rows] = gate
        send_ref[0, :, rows:] = up

    @pl.when(step >= half)
    def _():
        keep_ref[0, :, :rows] = gate
        keep_ref[0, :, rows:] = up


def pair_grad_kernel(
    first, side_ref, product_ref, mixed_ref, ddown_ref, datt_ref, send_ref, keep_ref, turned_ref, total_ref
):
    step = pl.program_id(0)
    upper = side_ref[0]
    half, rows = send_ref.shape[0], send_ref.shape[1]

    @pl.when(step == 0)
    def _():
        turned_ref[...] = ddown_ref[...].T

    @pl.when(step == first)
    def _():
        turned_ref[...] = datt_ref[...].T

    @pl.when(step < first)
    def _():
        total_ref[...] = dot_nn(turned_ref[...], product_ref[...])

    @pl.when(step >= first)
    def _():
        total_ref[...] = dot_nn(turned_ref[...], mixed_ref[...])

    for i in range(half):
        mine = pl.multiple_of((2 * i + upper) * rows, rows)
        other = pl.multiple_of((2 * i + 1 - upper) * rows, rows)
        keep_ref[i] = total_ref[pl.ds(mine, rows), :].astype(jnp.bfloat16)
        send_ref[i] = total_ref[pl.ds(other, rows), :].astype(jnp.bfloat16)


def query_grad_kernel(waits, dq_ref, normed_ref, *refs):
    refs[waits][...] = dot_tn(dq_ref[...], normed_ref[...]).astype(jnp.bfloat16)


def project_pair_kernel(
    waits, x_ref, cos_ref, sin_ref, wk_ref, wv_ref, gi_ref, gk_ref, *refs
):
    normed_ref, kv_ref, kraw_ref = refs[waits:]
    x = x_ref[0].astype(jnp.float32)
    size = wk_ref.shape[0]
    normed = (x * inverse_rms(x) * (1.0 + gi_ref[...])).astype(jnp.bfloat16)
    normed_ref[0] = normed
    k_raw = dot_nt(normed, wk_ref[...])
    kraw_ref[0] = k_raw.astype(jnp.bfloat16)
    key = turn(k_raw * inverse_rms(k_raw) * (1.0 + gk_ref[...]), cos_ref[0], sin_ref[0])
    kv_ref[0, :, :size] = key.astype(jnp.bfloat16)
    kv_ref[0, :, size:] = dot_nt(normed, wv_ref[...]).astype(jnp.bfloat16)


def project_query_kernel(
    heads, waits, normed_ref, cos_ref, sin_ref, wq_ref, gq_ref, *refs
):
    q_ref, qraw_ref = refs[waits:]
    size = gq_ref.shape[-1]
    part = normed_ref.shape[1] // 2
    normed = normed_ref[0]
    cosine, sine = cos_ref[0], sin_ref[0]
    for head in range(heads):
        raw = dot_nt(normed, wq_ref[head * size : (head + 1) * size, :])
        query = turn(raw * inverse_rms(raw) * (1.0 + gq_ref[...]), cosine, sine)
        query = (query * size ** (-0.5)).astype(jnp.bfloat16)
        raw = raw.astype(jnp.bfloat16)
        for t in range(2):
            span = slice(head * part, (head + 1) * part)
            q_ref[0, t, span, :] = query[t * part : (t + 1) * part]
            qraw_ref[0, t, span, :] = raw[t * part : (t + 1) * part]


def load_window(far_ref, near_ref, own_ref, win_ref):
    far, near = far_ref.shape[1], near_ref.shape[1]
    win_ref[:far, :] = far_ref[0]
    win_ref[far : far + near, :] = near_ref[0]
    win_ref[far + near :, :] = own_ref[0]


def mask_bias(qid_ref, kid_ref, t, part, span):
    ids = qid_ref[0, t * part : (t + 1) * part, :] == kid_ref[0, t]
    row = lax.broadcasted_iota(jnp.int32, (part, span), 0)
    column = lax.broadcasted_iota(jnp.int32, (part, span), 1)
    ok = ids & (column > row) & (column <= row + WINDOW)
    return jnp.where(ok, 0.0, MASKED_SCORE)


def attend_kernel(heads, q_ref, far_ref, near_ref, own_ref, qid_ref, kid_ref, mixed_ref, win_ref):
    size = q_ref.shape[-1]
    part = q_ref.shape[2] // heads
    span = part + WINDOW
    load_window(far_ref, near_ref, own_ref, win_ref)
    for t in range(2):
        bias = mask_bias(qid_ref, kid_ref, t, part, span)
        keys = win_ref[t * part : t * part + span, :size]
        values = win_ref[t * part : t * part + span, size:]
        for head in range(heads):
            scores = dot_nt(q_ref[0, t, head * part : (head + 1) * part, :], keys)
            weights = jnp.exp(scores + bias)
            total = jnp.sum(weights, axis=-1, keepdims=True)
            mixed = dot_nn(weights.astype(jnp.bfloat16), values) / total
            mixed_ref[0, t * part : (t + 1) * part, head * size : (head + 1) * size] = (
                mixed.astype(jnp.bfloat16)
            )


def middle_kernel(
    heads, chunk, side_ref, mixed_ref, x_ref, cot_ref, gu_own_ref, gu_got_ref, do_own_ref, do_got_ref, ga_ref, gp_ref, gf_ref,
    out_ref, pre_ref, product_ref, ddown_ref, dgate_ref, dup_ref, datt_ref, dhid_ref, dmix_ref, dg_ref,
    act_ref, slope_ref, wgu_ref, wdo_blocks_ref, sems,
):
    @pl.when(pl.program_id(0) == 0)
    def _():
        upper = side_ref[0]
        copies = []
        for i, (source, target) in enumerate(
            [(do_own_ref, wdo_blocks_ref), (do_got_ref, wdo_blocks_ref), (gu_own_ref, wgu_ref), (gu_got_ref, wgu_ref)]
        ):
            place = upper if i % 2 == 0 else 1 - upper
            copies.append(pltpu.make_async_copy(source, target.at[:, place], sems.at[i]))
        for copy in copies:
            copy.start()
        for copy in copies:
            copy.wait()

    def pair_columns(start, stop):
        picked = wdo_blocks_ref[:, :, :, start:stop]
        return picked.reshape(-1, stop - start)

    shard = wgu_ref.shape[2] // 2
    units = 2 * wgu_ref.shape[0] * shard
    group = chunk // shard

    def gate_up_rows(start, which):
        first = start // shard // 2
        picked = wgu_ref[first : first + group // 2, :, which * shard : (which + 1) * shard, :]
        return picked.reshape(chunk, picked.shape[-1])

    size = dmix_ref.shape[-1]
    part = dmix_ref.shape[2] // heads
    x = x_ref[0].astype(jnp.float32)
    attended = dot_nt(mixed_ref[0], pair_columns(units, units + heads * size))
    hidden = x + attended * inverse_rms(attended) * (1.0 + ga_ref[...])
    pre = (hidden * inverse_rms(hidden) * (1.0 + gp_ref[...])).astype(jnp.bfloat16)
    pre_ref[0] = pre
    down = jnp.zeros(x.shape, jnp.float32)
    root = (2.0 / math.pi) ** 0.5
    for start in range(0, units, chunk):
        span = slice(start, start + chunk)
        gate = dot_nt(pre, gate_up_rows(start, 0))
        up = dot_nt(pre, gate_up_rows(start, 1))
        square = gate * gate
        bend = jnp.tanh(gate * (root + (root * 0.044715) * square))
        half = 0.5 + 0.5 * bend
        act = gate * half
        slope = half + act * (1.0 - bend) * (root + (3.0 * root * 0.044715) * square)
        act_ref[:, span] = act
        slope_ref[:, span] = up * slope
        product = (act * up).astype(jnp.bfloat16)
        product_ref[0, :, span] = product
        down += dot_nt(product, pair_columns(start, start + chunk))
    out_ref[0] = (hidden + down * inverse_rms(down) * (1.0 + gf_ref[...])).astype(jnp.bfloat16)
    dy = cot_ref[0].astype(jnp.float32)
    d_down, dg_ffn = rms_back(down, gf_ref[...], dy)
    d_down = d_down.astype(jnp.bfloat16)
    ddown_ref[0] = d_down
    d_pre = jnp.zeros(x.shape, jnp.float32)
    for start in range(0, units, chunk):
        span = slice(start, start + chunk)
        d_product = dot_nn(d_down, pair_columns(start, start + chunk))
        d_gate = (d_product * slope_ref[:, span]).astype(jnp.bfloat16)
        d_up = (d_product * act_ref[:, span]).astype(jnp.bfloat16)
        dgate_ref[0, :, span] = d_gate
        dup_ref[0, :, span] = d_up
        d_pre += dot_nn(d_gate, gate_up_rows(start, 0)) + dot_nn(
            d_up, gate_up_rows(start, 1)
        )
    d_hidden, dg_pre = rms_back(hidden, gp_ref[...], d_pre)
    d_hidden = dy + d_hidden
    dhid_ref[0] = d_hidden
    d_att, dg_attn = rms_back(attended, ga_ref[...], d_hidden)
    d_att = d_att.astype(jnp.bfloat16)
    datt_ref[0] = d_att
    dg_ref[0] = jnp.concatenate([dg_attn, dg_pre, dg_ffn], axis=0)
    for head in range(heads):
        d_mixed = dot_nn(
            d_att, pair_columns(units + head * size, units + (head + 1) * size)
        ).astype(jnp.bfloat16)
        for t in range(2):
            dmix_ref[0, t, head * part : (head + 1) * part, :] = d_mixed[t * part : (t + 1) * part]


def attend_back_kernel(
    heads, waits, q_ref, qraw_ref, far_ref, near_ref, own_ref, qid_ref, kid_ref, mixed_ref, dmix_ref,
    cos_ref, sin_ref, gq_ref, *refs
):
    dfar_ref, dnear_ref, down_ref, dqraw_ref, dg_ref, win_ref, grad_ref = refs[waits:]
    size = q_ref.shape[-1]
    part = q_ref.shape[2] // heads
    span = part + WINDOW
    far, near = far_ref.shape[1], near_ref.shape[1]
    load_window(far_ref, near_ref, own_ref, win_ref)
    grad_ref[...] = jnp.zeros_like(grad_ref)
    dg = jnp.zeros((1, size), jnp.float32)
    for t in range(2):
        rows = slice(t * part, (t + 1) * part)
        window = slice(t * part, t * part + span)
        bias = mask_bias(qid_ref, kid_ref, t, part, span)
        keys = win_ref[window, :size]
        values = win_ref[window, size:]
        cosine, sine = cos_ref[0, rows, :], sin_ref[0, rows, :]
        for head in range(heads):
            line = slice(head * part, (head + 1) * part)
            lanes = slice(head * size, (head + 1) * size)
            query = q_ref[0, t, line, :]
            d_out = dmix_ref[0, t, line, :]
            weights = jnp.exp(dot_nt(query, keys) + bias)
            weights = weights * (1.0 / jnp.sum(weights, axis=-1, keepdims=True))
            delta = jnp.sum(
                d_out.astype(jnp.float32) * mixed_ref[0, rows, lanes].astype(jnp.float32),
                axis=-1,
                keepdims=True,
            )
            d_scores = (weights * (dot_nt(d_out, values) - delta)).astype(jnp.bfloat16)
            weights = weights.astype(jnp.bfloat16)
            grad_ref[window, :size] += dot_tn(d_scores, query)
            grad_ref[window, size:] += dot_tn(weights, d_out)
            d_query = dot_nn(d_scores, keys) * size ** (-0.5)
            d_raw, part_g = rms_back(
                qraw_ref[0, t, line, :].astype(jnp.float32),
                gq_ref[...],
                turn(d_query, cosine, -sine),
            )
            dqraw_ref[0, rows, lanes] = d_raw.astype(jnp.bfloat16)
            dg += part_g
    dg_ref[0] = dg
    dfar_ref[0] = grad_ref[:far, :].astype(jnp.bfloat16)
    dnear_ref[0] = grad_ref[far : far + near, :]
    down_ref[0] = grad_ref[far + near :, :]


def input_back_kernel(
    waits, own_ref, recv_ref, kraw_ref, cos_ref, sin_ref, wk_ref, wv_ref, dq_ref, wq_ref, x_ref, dhid_ref,
    gi_ref, gk_ref, *refs
):
    grad_ref, dpair_ref, dgi_ref, dgk_ref = refs[waits:]
    size = wk_ref.shape[0]
    total = own_ref[0] + recv_ref[0].astype(jnp.float32)
    d_key = turn(total[:, :size], cos_ref[0], -sin_ref[0])
    d_raw, dg_key = rms_back(kraw_ref[0].astype(jnp.float32), gk_ref[...], d_key)
    d_raw = d_raw.astype(jnp.bfloat16)
    d_value = total[:, size:].astype(jnp.bfloat16)
    dpair_ref[0, :, :size] = d_raw
    dpair_ref[0, :, size:] = d_value
    d_normed = dot_nn(dq_ref[0], wq_ref[...])
    d_normed += dot_nn(d_raw, wk_ref[...]) + dot_nn(d_value, wv_ref[...])
    d_x, dg_input = rms_back(x_ref[0].astype(jnp.float32), gi_ref[...], d_normed)
    grad_ref[0] = dhid_ref[0] + d_x
    dgi_ref[0] = dg_input
    dgk_ref[0] = dg_key


def flips(bit):
    return [(i, i ^ (1 << bit)) for i in range(lax.axis_size("dp"))]


def side(bit):
    return (lax.axis_index("dp") >> bit) & 1


def stack_step(own, received, bit, done, arrived=()):
    axis = sum(1 for other in done if other > bit)
    anywhere = pl.BlockSpec(memory_space=pl.ANY)
    arrived = list(arrived)
    return pl.pallas_call(
        functools.partial(stack_kernel, axis, len(arrived)),
        out_shape=jax.ShapeDtypeStruct(own.shape[:axis] + (2,) + own.shape[axis:], own.dtype),
        in_specs=[pl.BlockSpec(memory_space=pltpu.SMEM)] + [anywhere] * (2 + len(arrived)),
        out_specs=anywhere,
        scratch_shapes=[pltpu.SemaphoreType.DMA((2,))],
    )(side(bit)[None].astype(jnp.int32), own, received, *arrived)


def gather_rows(shard, order):
    current, steps = shard, []
    for i, bit in enumerate(order):
        received = lax.ppermute(current, "dp", flips(bit))
        steps.append(received)
        current = stack_step(current, received, bit, order[:i])
    return current.reshape((lax.axis_size("dp"),) + shard.shape), steps


class RowSum:
    def __init__(self, parts, order, axis):
        self.terms = [
            (part.reshape((2,) * len(order) + part.shape[1:]), list(range(len(order) - 1, -1, -1)))
            for part in parts
        ]
        self.join = axis
        self.order = order
        self.chosen = {}
        self.received = []

    @classmethod
    def from_halves(cls, keep, send, order):
        result = cls([], order, -1)
        shape = (2,) * (len(order) - 1) + keep.shape[1:]
        left = list(range(len(order) - 1, 0, -1))
        received = lax.ppermute(send, "dp", flips(0))
        result.terms = [(keep.reshape(shape), left)]
        result.received = [(received.reshape(shape), left)]
        result.chosen = {0: side(0)}
        result.sent = send
        return result

    def total(self, other=None):
        picks = dict(self.chosen)
        if other is not None:
            picks[other] = 1 - side(other)
        pieces = [self.pick(part, bits, picks) for part, bits in self.terms]
        value = jnp.concatenate(pieces, axis=self.join) if len(pieces) > 1 else pieces[0]
        value = value.astype(jnp.float32)
        for part, bits in self.received:
            value += self.pick(part, bits, picks).astype(jnp.float32)
        return value.astype(jnp.bfloat16)

    def pick(self, part, bits, picks):
        bits = list(bits)
        for bit, where in picks.items():
            if bit in bits:
                part = lax.dynamic_index_in_dim(part, where, bits.index(bit), keepdims=False)
                bits.remove(bit)
        return part

    def send(self, bit):
        self.sent = self.total(bit)
        return self.sent

    def step(self, bit):
        received = lax.ppermute(self.send(bit), "dp", flips(bit))
        self.chosen[bit] = side(bit)
        left = [b for b in range(len(self.order) - 1, -1, -1) if b not in self.chosen]
        self.received.append((received, left))
        return received


def seq_sum(part):
    count = lax.axis_size("seq")
    index = lax.axis_index("seq")
    half = count // 2
    terms = [part]

    def total():
        return sum(term.astype(jnp.float32) for term in terms)

    for t in range(half - 1):
        pairs = [(t, t + 1), (count - 1 - t, count - 2 - t)]
        terms.append(lax.ppermute(total().astype(jnp.bfloat16), "seq", pairs))
    middle = [(half - 1, half), (half, half - 1)]
    terms.append(lax.ppermute(total().astype(jnp.bfloat16), "seq", middle))
    result = total()
    for t in range(half - 2, -1, -1):
        pairs = [(t + 1, t), (count - 2 - t, count - 1 - t)]
        received = lax.ppermute(result.astype(jnp.bfloat16), "seq", pairs)
        outer = (index == t) | (index == count - 1 - t)
        result = jnp.where(outer, received.astype(jnp.float32), result)
    return result


def body(
    tokens,
    cotangent,
    segments,
    positions,
    query_weight,
    key_weight,
    value_weight,
    output_weight,
    gate_weight,
    up_weight,
    down_weight,
    norm_gains,
    query_first,
    key_first,
    value_first,
    output_first,
    gate_first,
    up_first,
    down_first,
    gains_first,
    query_second,
    key_second,
    value_second,
    output_second,
    gate_second,
    up_second,
    down_second,
    gains_second,
):
    count = lax.axis_size("dp")
    bits = (count - 1).bit_length()
    order_a = list(range(1, bits)) + [0]
    order_b = list(range(bits - 1, 0, -1)) + [0]
    low = jnp.bfloat16
    f32 = jnp.float32
    width = tokens.shape[2]
    key_rows = key_weight.shape[0]
    gain_rows = norm_gains.shape[0]
    rest_rows = 2 * key_rows + 16

    def array(shape, kind):
        return jax.ShapeDtypeStruct(shape, kind)

    query_shard, rest_shard = pl.pallas_call(
        cast_first_kernel,
        out_shape=[array(query_weight.shape, low), array((rest_rows, width), low)],
    )(query_weight, key_weight, value_weight, norm_gains[None])
    query_all, query_steps = gather_rows(query_shard, order_a)
    rest_all, rest_steps = gather_rows(rest_shard, order_b)
    w_query = query_all.reshape(-1, width)
    w_key = rest_all[:, :key_rows].reshape(-1, width)
    w_value = rest_all[:, key_rows : 2 * key_rows].reshape(-1, width)
    gains_all = rest_all[:, 2 * key_rows, :gain_rows].reshape(-1)
    block = pl.BlockSpec(memory_space=pltpu.VMEM)
    anywhere = pl.BlockSpec(memory_space=pl.ANY)
    arrived = [query_steps[-2], rest_steps[-2]]
    gate_up_shard, pair_shard = pl.pallas_call(
        functools.partial(cast_rest_kernel, len(arrived)),
        out_shape=[
            array((2 * gate_weight.shape[0], width), low),
            array((down_weight.shape[0], down_weight.shape[1] + output_weight.shape[1]), low),
        ],
        in_specs=[block] * 4 + [anywhere] * len(arrived),
    )(gate_weight, up_weight, down_weight, output_weight, *arrived)

    seqs, rows, _ = tokens.shape
    size = w_key.shape[0]
    heads = w_query.shape[0] // size
    units = down_weight.shape[1]
    shards = lax.axis_size("seq")
    far = WINDOW - rows
    part = rows // 2
    span = part + WINDOW
    gains_float = gains_all.astype(jnp.float32)[None]
    g_input, g_attn, g_pre, g_ffn = (
        gains_float[:, i * width : (i + 1) * width] for i in range(4)
    )
    g_query = gains_float[:, 4 * width : 4 * width + size]
    g_key = gains_float[:, 4 * width + size : 4 * width + 2 * size]
    angles = positions.astype(jnp.float32)[..., None] * frequencies(size)
    cosine, sine = jnp.cos(angles), jnp.sin(angles)
    core_side = side(0)[None].astype(jnp.int32)
    first_row = lax.axis_index("seq") * rows
    padded = jnp.concatenate([jnp.full((seqs, WINDOW), -1, jnp.int32), segments], axis=1)
    window_ids = lax.dynamic_slice_in_dim(padded, first_row, WINDOW + rows, 1)
    query_ids = window_ids[:, WINDOW:, None]
    key_ids = jnp.stack([window_ids[:, :span], window_ids[:, part:]], axis=1)[:, :, None, :]

    def call(kernel, outs, out_specs, in_specs, scratch, flops, moved):
        return pl.pallas_call(
            kernel,
            grid=(seqs,),
            out_shape=outs,
            in_specs=in_specs,
            out_specs=out_specs,
            scratch_shapes=scratch,
            compiler_params=kernel_params(),
            cost_estimate=pl.CostEstimate(flops=flops, bytes_accessed=moved, transcendentals=0),
        )

    tokens_all = seqs * rows
    head_block = per_seq(2, heads * part, size)
    q_shape = (seqs, 2, heads * part, size)
    normed, pair_own, key_raw = call(
        functools.partial(project_pair_kernel, 2),
        [
            array((seqs, rows, width), low),
            array((seqs, rows, 2 * size), low),
            array((seqs, rows, size), low),
        ],
        [per_seq(rows, width), per_seq(rows, 2 * size), per_seq(rows, size)],
        [
            per_seq(rows, width),
            per_seq(rows, size // 2),
            per_seq(rows, size // 2),
            whole(*w_key.shape),
            whole(*w_value.shape),
            whole(1, width),
            whole(1, size),
            anywhere,
            anywhere,
        ],
        [],
        4 * tokens_all * width * size,
        6_000_000,
    )(tokens, cosine, sine, w_key, w_value, g_input, g_key, query_ids, key_ids)
    pair_first = lax.ppermute(pair_shard, "dp", flips(order_b[0]))
    query, query_raw = call(
        functools.partial(project_query_kernel, heads, 1),
        [array(q_shape, low), array(q_shape, low)],
        [head_block, head_block],
        [
            per_seq(rows, width),
            per_seq(rows, size // 2),
            per_seq(rows, size // 2),
            whole(*w_query.shape),
            whole(1, size),
            anywhere,
        ],
        [],
        2 * tokens_all * width * heads * size,
        8_000_000,
    )(normed, cosine, sine, w_query, g_query, pair_first)

    upward = [(i, i + 1) for i in range(shards - 1)]
    pair_near = lax.ppermute(pair_own, "seq", upward)
    gate_up_half, pair_half = gate_up_shard, pair_shard
    pair_far = None
    for i in range(bits - 1):
        pair_received = pair_first
        if i:
            pair_received = lax.ppermute(pair_half, "dp", flips(order_b[i]))
        gate_up_received = lax.ppermute(gate_up_half, "dp", flips(order_a[i]))
        waits = [query] if i == 0 else [pair_far]
        pair_half = stack_step(pair_half, pair_received, order_b[i], order_b[:i], waits)
        gate_up_half = stack_step(gate_up_half, gate_up_received, order_a[i], order_a[:i], waits)
        if i == 0:
            far_send = pl.pallas_call(
                functools.partial(tail_rows_kernel, 2),
                out_shape=array((seqs, far, 2 * size), low),
                in_specs=[anywhere] * 3,
                out_specs=anywhere,
                scratch_shapes=[pltpu.SemaphoreType.DMA],
            )(pair_near, pair_half, gate_up_half)
            pair_far = lax.ppermute(far_send, "seq", upward[1:])
    pair_half = pair_half.reshape((count // 2,) + pair_shard.shape)
    gate_up_half = gate_up_half.reshape((count // 2,) + gate_up_shard.shape)
    pair_received = lax.ppermute(pair_half, "dp", flips(0))
    gate_up_received = lax.ppermute(gate_up_half, "dp", flips(0))

    window_specs = [
        per_seq(far, 2 * size),
        per_seq(rows, 2 * size),
        per_seq(rows, 2 * size),
        per_seq(rows, 1),
        per_seq(2, 1, span),
    ]
    attend_flops = 8 * tokens_all * heads * span * size
    mixed = call(
        functools.partial(attend_kernel, heads),
        array((seqs, rows, heads * size), low),
        per_seq(rows, heads * size),
        [head_block] + window_specs,
        [pltpu.VMEM((WINDOW + rows, 2 * size), low)],
        attend_flops,
        16_000_000,
    )(query, pair_far, pair_near, pair_own, query_ids, key_ids)

    (
        layer_output,
        pre_low,
        product_low,
        grad_down_low,
        grad_gate_low,
        grad_up_low,
        grad_attended_low,
        grad_hidden,
        grad_mixed,
        grad_gains_middle,
    ) = call(
        functools.partial(middle_kernel, heads, 512),
        [
            array((seqs, rows, width), low),
            array((seqs, rows, width), low),
            array((seqs, rows, units), low),
            array((seqs, rows, width), low),
            array((seqs, rows, units), low),
            array((seqs, rows, units), low),
            array((seqs, rows, width), low),
            array((seqs, rows, width), f32),
            array(q_shape, low),
            array((seqs, 3, width), f32),
        ],
        [
            per_seq(rows, width),
            per_seq(rows, width),
            per_seq(rows, units),
            per_seq(rows, width),
            per_seq(rows, units),
            per_seq(rows, units),
            per_seq(rows, width),
            per_seq(rows, width),
            head_block,
            per_seq(3, width),
        ],
        [
            pl.BlockSpec(memory_space=pltpu.SMEM),
            per_seq(rows, heads * size),
            per_seq(rows, width),
            per_seq(rows, width),
            anywhere,
            anywhere,
            anywhere,
            anywhere,
            whole(1, width),
            whole(1, width),
            whole(1, width),
        ],
        [
            pltpu.VMEM((rows, units), f32),
            pltpu.VMEM((rows, units), f32),
            pltpu.VMEM((count // 2, 2) + gate_up_shard.shape, low),
            pltpu.VMEM((count // 2, 2) + pair_shard.shape, low),
            pltpu.SemaphoreType.DMA((4,)),
        ],
        4 * tokens_all * width * (heads * size + 3 * units),
        40_000_000,
    )(
        core_side, mixed, tokens, cotangent, gate_up_half, gate_up_received, pair_half, pair_received,
        g_attn, g_pre, g_ffn,
    )

    def flat(values):
        return values.reshape(tokens_all, values.shape[-1])

    def grad_blocks(gradient, inputs):
        product = weight_grad(flat(gradient), flat(inputs)).astype(low)
        return product.reshape(count, -1, product.shape[1])

    back_a = [0] + order_a[:-1]
    back_b = [0] + order_b[:-1]
    shard_units = gate_weight.shape[0]
    shard_rows = down_weight.shape[0]
    half = count // 2
    direct = shard_units % 128 == 0 and shard_rows % 16 == 0
    if direct:
        columns = 512
        first = units // columns
        last = heads * size // columns
        pair_block = pl.BlockSpec((half, shard_rows, columns), lambda k, side: (0, 0, k))
        pair_shape = array((half, shard_rows, units + heads * size), low)
        fixed = pl.BlockSpec(
            (tokens_all, width), lambda k, side: (0, 0), pipeline_mode=pl.Buffered(1)
        )
        pair_send, pair_keep = pl.pallas_call(
            functools.partial(pair_grad_kernel, first),
            out_shape=[pair_shape, pair_shape],
            grid_spec=pltpu.PrefetchScalarGridSpec(
                num_scalar_prefetch=1,
                grid=(first + last,),
                in_specs=[
                    pl.BlockSpec(
                        (tokens_all, columns), lambda k, side: (0, jnp.minimum(k, first - 1))
                    ),
                    pl.BlockSpec(
                        (tokens_all, columns), lambda k, side: (0, jnp.maximum(k - first, 0))
                    ),
                    fixed,
                    fixed,
                ],
                out_specs=[pair_block, pair_block],
                scratch_shapes=[
                    pltpu.VMEM((width, tokens_all), low),
                    pltpu.VMEM((width, columns), f32),
                ],
            ),
            compiler_params=kernel_params(),
            cost_estimate=pl.CostEstimate(
                flops=2 * tokens_all * width * (units + heads * size),
                bytes_accessed=13_000_000,
                transcendentals=0,
            ),
        )(core_side, flat(product_low), flat(mixed), flat(grad_down_low), flat(grad_attended_low))
        down_out_sum = RowSum.from_halves(pair_keep, pair_send, back_b)

        def shard_of(g, side):
            return (0, 2 * (g % half) + jnp.where(g < half, 1 - side[0], side[0]))

        block_shape = (1, width, 2 * shard_units)
        half_shape = array((half, width, 2 * shard_units), low)
        gate_up_send, gate_up_keep = pl.pallas_call(
            gate_up_grad_kernel,
            out_shape=[half_shape, half_shape],
            grid_spec=pltpu.PrefetchScalarGridSpec(
                num_scalar_prefetch=1,
                grid=(count,),
                in_specs=[
                    pl.BlockSpec((tokens_all, shard_units), shard_of),
                    pl.BlockSpec((tokens_all, shard_units), shard_of),
                    fixed,
                    anywhere,
                ],
                out_specs=[
                    pl.BlockSpec(block_shape, lambda g, side: (jnp.minimum(g, half - 1), 0, 0)),
                    pl.BlockSpec(block_shape, lambda g, side: (jnp.maximum(g - half, 0), 0, 0)),
                ],
                scratch_shapes=[pltpu.VMEM((width, tokens_all), low)],
            ),
            compiler_params=kernel_params(),
            cost_estimate=pl.CostEstimate(
                flops=4 * tokens_all * width * units, bytes_accessed=14_000_000, transcendentals=0
            ),
        )(core_side, flat(grad_gate_low), flat(grad_up_low), flat(pre_low), pair_send)
        gate_up_sum = RowSum.from_halves(gate_up_keep, gate_up_send, back_a)
    else:
        down_out_sum = RowSum(
            [grad_blocks(grad_down_low, product_low), grad_blocks(grad_attended_low, mixed)],
            back_b,
            -1,
        )
        down_out_sum.step(0)

        def turned_blocks(gradient):
            product = weight_grad(flat(pre_low), flat(gradient)).astype(low)
            return product.reshape(width, count, shard_units).transpose(1, 0, 2)

        gate_up_sum = RowSum(
            [turned_blocks(grad_gate_low), turned_blocks(grad_up_low)], back_a, -1
        )
        gate_up_sum.step(0)

    def at_seq(s, *tail):
        return pl.BlockSpec((1,) + tail, lambda g: (s,) + (0,) * len(tail))

    def seq_call(kernel, outs, out_specs, in_specs, operands, scratch, alias, flops):
        return pl.pallas_call(
            kernel,
            grid=(1,),
            out_shape=outs,
            in_specs=in_specs,
            out_specs=out_specs,
            scratch_shapes=scratch,
            input_output_aliases=alias,
            compiler_params=kernel_params(),
            cost_estimate=pl.CostEstimate(
                flops=flops, bytes_accessed=8_000_000, transcendentals=0
            ),
        )(*operands)

    def attend_back(s, buffer, arrived):
        kinds = [
            array((1, far, 2 * size), low),
            array((1, rows, 2 * size), f32),
            array((1, rows, 2 * size), f32),
            array((seqs, rows, heads * size), low),
            array((1, 1, size), f32),
        ]
        specs = [
            at_seq(0, far, 2 * size),
            at_seq(0, rows, 2 * size),
            at_seq(0, rows, 2 * size),
            at_seq(s, rows, heads * size),
            at_seq(0, 1, size),
        ]
        in_specs = [
            at_seq(s, 2, heads * part, size),
            at_seq(s, 2, heads * part, size),
            at_seq(s, far, 2 * size),
            at_seq(s, rows, 2 * size),
            at_seq(s, rows, 2 * size),
            at_seq(s, rows, 1),
            at_seq(s, 2, 1, span),
            at_seq(s, rows, heads * size),
            at_seq(s, 2, heads * part, size),
            at_seq(s, rows, size // 2),
            at_seq(s, rows, size // 2),
            whole(1, size),
        ]
        operands = [
            query, query_raw, pair_far, pair_near, pair_own, query_ids, key_ids, mixed, grad_mixed,
            cosine, sine, g_query,
        ]
        alias = {}
        extra = list(arrived)
        if buffer is not None:
            alias = {len(operands): 3}
            extra = [buffer] + extra
        return seq_call(
            functools.partial(attend_back_kernel, heads, len(extra)),
            kinds,
            specs,
            in_specs + [anywhere] * len(extra),
            operands + extra,
            [
                pltpu.VMEM((WINDOW + rows, 2 * size), low),
                pltpu.VMEM((WINDOW + rows, 2 * size), f32),
            ],
            alias,
            attend_flops * 3 // seqs,
        )

    downward = [(i + 1, i) for i in range(shards - 1)]
    grad_query_low = None
    down_out_sum.step(back_b[1])
    arrived = [gate_up_sum.sent, down_out_sum.sent]
    own_parts, query_gains, near_sums, from_near = [], [], [], []
    for s in range(seqs):
        grad_far, grad_near, grad_own, grad_query_low, g_part = attend_back(
            s, grad_query_low, arrived
        )
        from_far = lax.ppermute(grad_far, "seq", downward[1:])
        own_parts.append(grad_own)
        query_gains.append(g_part)
        near_sum = (
            grad_near
            + jnp.pad(from_far.astype(f32), ((0, 0), (rows - far, 0), (0, 0)))
        ).astype(low)
        near_sums.append(near_sum)
        from_near.append(lax.ppermute(near_sum, "seq", downward))
        if s == 0:
            gate_up_sum.step(back_a[1])
            arrived = [gate_up_sum.sent]
        elif s == 1:
            arrived = [near_sums[0]]
    for bit in back_b[2:]:
        down_out_sum.step(bit)
    query_columns = heads * size
    grad_w_query = pl.pallas_call(
        functools.partial(query_grad_kernel, 2),
        grid=(heads,),
        out_shape=array((query_columns, width), low),
        in_specs=[
            pl.BlockSpec((tokens_all, size), lambda i: (0, i)),
            whole(tokens_all, width),
            anywhere,
            anywhere,
        ],
        out_specs=pl.BlockSpec((size, width), lambda i: (i, 0)),
        compiler_params=kernel_params(),
        cost_estimate=pl.CostEstimate(
            flops=2 * tokens_all * width * query_columns, bytes_accessed=5_000_000, transcendentals=0
        ),
    )(flat(grad_query_low), flat(normed), near_sums[1], down_out_sum.sent)
    for bit in back_a[2:]:
        gate_up_sum.step(bit)
    down_out_part = down_out_sum.total()

    def input_back(s, buffers, arrived):
        kinds = [
            array((seqs, rows, width), f32),
            array((seqs, rows, 2 * size), low),
            array((1, 1, width), f32),
            array((1, 1, size), f32),
        ]
        specs = [
            at_seq(s, rows, width),
            at_seq(s, rows, 2 * size),
            at_seq(0, 1, width),
            at_seq(0, 1, size),
        ]
        in_specs = [
            at_seq(0, rows, 2 * size),
            at_seq(0, rows, 2 * size),
            at_seq(s, rows, size),
            at_seq(s, rows, size // 2),
            at_seq(s, rows, size // 2),
            whole(*w_key.shape),
            whole(*w_value.shape),
            at_seq(s, rows, heads * size),
            whole(*w_query.shape),
            at_seq(s, rows, width),
            at_seq(s, rows, width),
            whole(1, width),
            whole(1, size),
        ]
        operands = [
            own_parts[s], from_near[s], key_raw, cosine, sine, w_key, w_value, grad_query_low,
            w_query, tokens, grad_hidden, g_input, g_key,
        ]
        alias = {}
        extra = list(arrived)
        if buffers:
            alias = {len(operands): 0, len(operands) + 1: 1}
            extra = list(buffers) + extra
        return seq_call(
            functools.partial(input_back_kernel, len(extra)),
            kinds,
            specs,
            in_specs + [anywhere] * len(extra),
            operands + extra,
            [],
            alias,
            2 * rows * width * size * (heads + 2),
        )

    buffers = []
    input_gains, key_gains = [], []
    waits = [[grad_w_query, near_sums[-1]], [gate_up_sum.sent], [down_out_part]]
    waits += [[]] * seqs
    for s in range(seqs):
        *buffers, g_part, g_key_part = input_back(s, buffers, waits[s])
        input_gains.append(g_part)
        key_gains.append(g_key_part)
    input_grad, grad_pair_low = buffers
    pair_blocks = grad_blocks(grad_pair_low, normed).reshape(2, count, key_rows, width)
    grad_gains = jnp.concatenate(
        [
            sum(input_gains).reshape(-1),
            jnp.sum(grad_gains_middle, axis=0).reshape(-1),
            sum(query_gains).reshape(-1),
            sum(key_gains).reshape(-1),
        ]
    )
    gain_block = jnp.pad(
        grad_gains.astype(low).reshape(count, 1, gain_rows),
        ((0, 0), (0, 15), (0, width - gain_rows)),
    )
    query_rows = query_weight.shape[0]
    rest_sum = RowSum(
        [grad_w_query.reshape(count, query_rows, width), pair_blocks[0], pair_blocks[1], gain_block],
        back_b,
        -2,
    )
    for bit in back_b:
        rest_sum.step(bit)
    down_out_total = seq_sum(down_out_part)
    gate_up_part = gate_up_sum.total()
    gate_total = seq_sum(gate_up_part[:, :shard_units]).T
    up_total = seq_sum(gate_up_part[:, shard_units:]).T
    rest_total = seq_sum(rest_sum.total())
    query_total = rest_total[:query_rows]
    rest_total = rest_total[query_rows:]
    down_total = down_out_total[:, :units]
    output_total = down_out_total[:, units:]
    key_total = rest_total[:key_rows]
    value_total = rest_total[key_rows : 2 * key_rows]
    gains_total = rest_total[2 * key_rows, :gain_rows]
    query_momentum, query_variance, query_updated = adam_step(
        query_weight, query_first, query_second, query_total, WEIGHT_DECAY
    )
    key_momentum, key_variance, key_updated = adam_step(
        key_weight, key_first, key_second, key_total, WEIGHT_DECAY
    )
    value_momentum, value_variance, value_updated = adam_step(
        value_weight, value_first, value_second, value_total, WEIGHT_DECAY
    )
    output_momentum, output_variance, output_updated = adam_step(
        output_weight, output_first, output_second, output_total, WEIGHT_DECAY
    )
    gate_momentum, gate_variance, gate_updated = adam_step(
        gate_weight, gate_first, gate_second, gate_total, WEIGHT_DECAY
    )
    up_momentum, up_variance, up_updated = adam_step(
        up_weight, up_first, up_second, up_total, WEIGHT_DECAY
    )
    down_momentum, down_variance, down_updated = adam_step(
        down_weight, down_first, down_second, down_total, WEIGHT_DECAY
    )
    gains_momentum, gains_variance, gains_updated = adam_step(
        norm_gains, gains_first, gains_second, gains_total, 0.0
    )
    return (
        layer_output,
        input_grad,
        query_momentum,
        key_momentum,
        value_momentum,
        output_momentum,
        gate_momentum,
        up_momentum,
        down_momentum,
        gains_momentum,
        query_variance,
        key_variance,
        value_variance,
        output_variance,
        gate_variance,
        up_variance,
        down_variance,
        gains_variance,
        query_updated,
        key_updated,
        value_updated,
        output_updated,
        gate_updated,
        up_updated,
        down_updated,
        gains_updated,
    )


def solution(mesh):
    return jax.shard_map(
        body,
        mesh=mesh,
        in_specs=(
            P("dp", "seq", None),
            P("dp", "seq", None),
            P("dp", None),
            P("dp", "seq"),
            P("dp", None),
            P("dp", None),
            P("dp", None),
            P("dp", None),
            P("dp", None),
            P("dp", None),
            P("dp", None),
            P("dp"),
            P("dp", None),
            P("dp", None),
            P("dp", None),
            P("dp", None),
            P("dp", None),
            P("dp", None),
            P("dp", None),
            P("dp"),
            P("dp", None),
            P("dp", None),
            P("dp", None),
            P("dp", None),
            P("dp", None),
            P("dp", None),
            P("dp", None),
            P("dp"),
        ),
        out_specs=(
            P("dp", "seq", None),
            P("dp", "seq", None),
            P("dp", None),
            P("dp", None),
            P("dp", None),
            P("dp", None),
            P("dp", None),
            P("dp", None),
            P("dp", None),
            P("dp"),
            P("dp", None),
            P("dp", None),
            P("dp", None),
            P("dp", None),
            P("dp", None),
            P("dp", None),
            P("dp", None),
            P("dp"),
            P("dp", None),
            P("dp", None),
            P("dp", None),
            P("dp", None),
            P("dp", None),
            P("dp", None),
            P("dp", None),
            P("dp"),
        ),
        check_vma=False,
    )
```

```python
import functools
import math

import jax
import jax.numpy as jnp
from jax import lax
from jax.experimental import pallas as pl
from jax.experimental.pallas import tpu as pltpu
from jax.sharding import PartitionSpec as P

WINDOW = 512
STEP = 10


NORM_EPSILON = 1e-06
ROPE_BASE = 10000.0
LEARN_RATE = 0.08
BETA_FIRST = 0.9
BETA_SECOND = 0.95
ADAM_EPSILON = 1e-08
WEIGHT_DECAY = 0.01
MASKED_SCORE = -1000000000.0


def frequencies(size):
    return ROPE_BASE ** (-2.0 * jnp.arange(size // 2).astype(jnp.float32) / size)


def weight_grad(gradients, inputs):
    return lax.dot_general(
        gradients, inputs, (((0,), (0,)), ((), ())), preferred_element_type=jnp.float32
    )


def adam_step(weight, first_moment, second_moment, gradient, decay_rate):
    momentum = BETA_FIRST * first_moment + (1.0 - BETA_FIRST) * gradient
    variance = BETA_SECOND * second_moment + (1.0 - BETA_SECOND) * gradient * gradient
    corrected = momentum / (1.0 - BETA_FIRST**STEP)
    scaled = variance / (1.0 - BETA_SECOND**STEP)
    updated = weight - LEARN_RATE * (
        corrected / (jnp.sqrt(scaled) + ADAM_EPSILON) + decay_rate * weight
    )
    return (momentum, variance, updated)


VMEM_BYTES = 56 * 1024 * 1024


def kernel_params():
    return pltpu.CompilerParams(
        dimension_semantics=("arbitrary",), vmem_limit_bytes=VMEM_BYTES
    )


def per_seq(*tail):
    return pl.BlockSpec((1,) + tail, lambda s: (s,) + (0,) * len(tail))


def whole(*shape):
    return pl.BlockSpec(shape, lambda s: (0,) * len(shape), pipeline_mode=pl.Buffered(1))


def dot_nt(a, b):
    return lax.dot_general(a, b, (((1,), (1,)), ((), ())), preferred_element_type=jnp.float32)


def dot_nn(a, b):
    return lax.dot_general(a, b, (((1,), (0,)), ((), ())), preferred_element_type=jnp.float32)


def dot_tn(a, b):
    return lax.dot_general(a, b, (((0,), (0,)), ((), ())), preferred_element_type=jnp.float32)


def inverse_rms(values):
    return lax.rsqrt(jnp.mean(values * values, axis=-1, keepdims=True) + NORM_EPSILON)


def rms_back(values, gain, grad):
    inverse = inverse_rms(values)
    unit = values * inverse
    scaled = grad * (1.0 + gain)
    return (
        inverse * (scaled - unit * jnp.mean(unit * scaled, axis=-1, keepdims=True)),
        jnp.sum(grad * unit, axis=0, keepdims=True),
    )


def turn(values, cosine, sine):
    half = values.shape[-1] // 2
    first, second = values[:, :half], values[:, half:]
    return jnp.concatenate(
        [first * cosine - second * sine, second * cosine + first * sine], axis=-1
    )


def stack_heads(values, heads):
    return jnp.concatenate([values] * heads, axis=0)


def cast_first_kernel(wq_ref, wk_ref, wv_ref, gain_ref, q_ref, rest_ref):
    q_ref[...] = wq_ref[...].astype(jnp.bfloat16)
    width = wq_ref.shape[1]
    gains = gain_ref[...]
    tail = width - gains.shape[1]
    block = jnp.broadcast_to(gains, (16, gains.shape[1]))
    if tail:
        block = jnp.concatenate([block, jnp.zeros((16, tail), jnp.float32)], axis=1)
    rest_ref[...] = jnp.concatenate([wk_ref[...], wv_ref[...], block], axis=0).astype(jnp.bfloat16)


def cast_rest_kernel(waits, wg_ref, wu_ref, wd_ref, wo_ref, *refs):
    out_ref, pair_ref = refs[waits:]
    rows = wg_ref.shape[0]
    units = wd_ref.shape[1]
    out_ref[:rows, :] = wg_ref[...].astype(jnp.bfloat16)
    out_ref[rows:, :] = wu_ref[...].astype(jnp.bfloat16)
    pair_ref[:, :units] = wd_ref[...].astype(jnp.bfloat16)
    pair_ref[:, units:] = wo_ref[...].astype(jnp.bfloat16)


def stack_kernel(axis, waits, side_ref, own_ref, received_ref, *refs):
    out_ref = refs[waits]
    upper = side_ref[0]
    lead = (slice(None),) * axis
    out_ref[lead + (upper,)] = own_ref[...]
    out_ref[lead + (1 - upper,)] = received_ref[...]


def tail_rows_kernel(waits, near_ref, *refs):
    out_ref = refs[waits]
    out_ref[...] = near_ref[:, near_ref.shape[1] - out_ref.shape[1] :]


def near_sum_kernel(waits, near_ref, far_ref, *refs):
    out_ref = refs[waits]
    keep = near_ref.shape[1] - far_ref.shape[1]
    out_ref[0, :keep] = near_ref[0, :keep].astype(jnp.bfloat16)
    total = near_ref[0, keep:] + far_ref[0].astype(jnp.float32)
    out_ref[0, keep:] = total.astype(jnp.bfloat16)


def sum_kernel(count, index_ref, *refs):
    total = refs[0][0].astype(jnp.float32)
    for ref in refs[1:count]:
        total += ref[0].astype(jnp.float32)
    refs[-1][0] = total.astype(jnp.bfloat16)


def gate_up_grad_kernel(side_ref, dgate_ref, dup_ref, pre_ref, after_ref, send_ref, keep_ref):
    step = pl.program_id(0)
    half = pl.num_programs(0) // 2
    rows = dgate_ref.shape[1]

    gate = dot_tn(dgate_ref[...], pre_ref[...]).astype(jnp.bfloat16)
    up = dot_tn(dup_ref[...], pre_ref[...]).astype(jnp.bfloat16)

    @pl.when(step < half)
    def _():
        send_ref[0, :rows, :] = gate
        send_ref[0, rows:, :] = up

    @pl.when(step >= half)
    def _():
        keep_ref[0, :rows, :] = gate
        keep_ref[0, rows:, :] = up


def pair_grad_kernel(
    first, side_ref, product_ref, mixed_ref, ddown_ref, datt_ref, send_ref, keep_ref, turned_ref, total_ref
):
    step = pl.program_id(0)
    upper = side_ref[0]
    half, rows = send_ref.shape[0], send_ref.shape[1]

    @pl.when(step == 0)
    def _():
        turned_ref[...] = ddown_ref[...].T

    @pl.when(step == first)
    def _():
        turned_ref[...] = datt_ref[...].T

    @pl.when(step < first)
    def _():
        total_ref[...] = dot_nn(turned_ref[...], product_ref[...])

    @pl.when(step >= first)
    def _():
        total_ref[...] = dot_nn(turned_ref[...], mixed_ref[...])

    for i in range(half):
        mine = pl.multiple_of((2 * i + upper) * rows, rows)
        other = pl.multiple_of((2 * i + 1 - upper) * rows, rows)
        keep_ref[i] = total_ref[pl.ds(mine, rows), :].astype(jnp.bfloat16)
        send_ref[i] = total_ref[pl.ds(other, rows), :].astype(jnp.bfloat16)


def query_grad_kernel(waits, dq_ref, normed_ref, *refs):
    refs[waits][...] = dot_tn(dq_ref[...], normed_ref[...]).astype(jnp.bfloat16)


def project_pair_kernel(
    waits, x_ref, cos_ref, sin_ref, wk_ref, wv_ref, gi_ref, gk_ref, *refs
):
    normed_ref, kv_ref, kraw_ref = refs[waits:]
    x = x_ref[0].astype(jnp.float32)
    size = wk_ref.shape[0]
    normed = (x * inverse_rms(x) * (1.0 + gi_ref[...])).astype(jnp.bfloat16)
    normed_ref[0] = normed
    k_raw = dot_nt(normed, wk_ref[...])
    kraw_ref[0] = k_raw.astype(jnp.bfloat16)
    key = turn(k_raw * inverse_rms(k_raw) * (1.0 + gk_ref[...]), cos_ref[0], sin_ref[0])
    kv_ref[0, :, :size] = key.astype(jnp.bfloat16)
    kv_ref[0, :, size:] = dot_nt(normed, wv_ref[...]).astype(jnp.bfloat16)


def project_query_kernel(
    heads, waits, normed_ref, cos_ref, sin_ref, wq_ref, gq_ref, *refs
):
    q_ref, qraw_ref = refs[waits:]
    size = gq_ref.shape[-1]
    part = normed_ref.shape[1] // 2
    normed = normed_ref[0]
    cosine, sine = cos_ref[0], sin_ref[0]
    for head in range(heads):
        raw = dot_nt(normed, wq_ref[head * size : (head + 1) * size, :])
        query = turn(raw * inverse_rms(raw) * (1.0 + gq_ref[...]), cosine, sine)
        query = (query * size ** (-0.5)).astype(jnp.bfloat16)
        raw = raw.astype(jnp.bfloat16)
        for t in range(2):
            span = slice(head * part, (head + 1) * part)
            q_ref[0, t, span, :] = query[t * part : (t + 1) * part]
            qraw_ref[0, t, span, :] = raw[t * part : (t + 1) * part]


def load_window(far_ref, near_ref, own_ref, win_ref):
    far, near = far_ref.shape[1], near_ref.shape[1]
    win_ref[:far, :] = far_ref[0]
    win_ref[far : far + near, :] = near_ref[0]
    win_ref[far + near :, :] = own_ref[0]


def mask_bias(qid_ref, kid_ref, t, part, span):
    ids = qid_ref[0, t * part : (t + 1) * part, :] == kid_ref[0, t]
    row = lax.broadcasted_iota(jnp.int32, (part, span), 0)
    column = lax.broadcasted_iota(jnp.int32, (part, span), 1)
    ok = ids & (column > row) & (column <= row + WINDOW)
    return jnp.where(ok, 0.0, MASKED_SCORE)


def attend_kernel(heads, q_ref, far_ref, near_ref, own_ref, qid_ref, kid_ref, mixed_ref, win_ref):
    size = q_ref.shape[-1]
    part = q_ref.shape[2] // heads
    span = part + WINDOW
    load_window(far_ref, near_ref, own_ref, win_ref)
    for t in range(2):
        bias = mask_bias(qid_ref, kid_ref, t, part, span)
        keys = win_ref[t * part : t * part + span, :size]
        values = win_ref[t * part : t * part + span, size:]
        for head in range(heads):
            scores = dot_nt(q_ref[0, t, head * part : (head + 1) * part, :], keys)
            weights = jnp.exp(scores + bias)
            total = jnp.sum(weights, axis=-1, keepdims=True)
            mixed = dot_nn(weights.astype(jnp.bfloat16), values) / total
            mixed_ref[0, t * part : (t + 1) * part, head * size : (head + 1) * size] = (
                mixed.astype(jnp.bfloat16)
            )


def middle_kernel(
    heads, chunk, side_ref, mixed_ref, x_ref, cot_ref, gu_own_ref, gu_got_ref, do_own_ref, do_got_ref, ga_ref, gp_ref, gf_ref,
    out_ref, pre_ref, product_ref, ddown_ref, dgate_ref, dup_ref, datt_ref, dhid_ref, dmix_ref, dg_ref,
    act_ref, slope_ref, wgu_ref, wdo_blocks_ref, sems,
):
    @pl.when(pl.program_id(0) == 0)
    def _():
        upper = side_ref[0]
        copies = []
        for i, (source, target) in enumerate(
            [(do_own_ref, wdo_blocks_ref), (do_got_ref, wdo_blocks_ref), (gu_own_ref, wgu_ref), (gu_got_ref, wgu_ref)]
        ):
            place = upper if i % 2 == 0 else 1 - upper
            copies.append(pltpu.make_async_copy(source, target.at[:, place], sems.at[i]))
        for copy in copies:
            copy.start()
        for copy in copies:
            copy.wait()

    def pair_columns(start, stop):
        picked = wdo_blocks_ref[:, :, :, start:stop]
        return picked.reshape(-1, stop - start)

    shard = wgu_ref.shape[2] // 2
    units = 2 * wgu_ref.shape[0] * shard
    group = chunk // shard

    def gate_up_rows(start, which):
        first = start // shard // 2
        picked = wgu_ref[first : first + group // 2, :, which * shard : (which + 1) * shard, :]
        return picked.reshape(chunk, picked.shape[-1])

    size = dmix_ref.shape[-1]
    part = dmix_ref.shape[2] // heads
    x = x_ref[0].astype(jnp.float32)
    attended = dot_nt(mixed_ref[0], pair_columns(units, units + heads * size))
    hidden = x + attended * inverse_rms(attended) * (1.0 + ga_ref[...])
    pre = (hidden * inverse_rms(hidden) * (1.0 + gp_ref[...])).astype(jnp.bfloat16)
    pre_ref[0] = pre
    down = jnp.zeros(x.shape, jnp.float32)
    root = (2.0 / math.pi) ** 0.5
    for start in range(0, units, chunk):
        span = slice(start, start + chunk)
        gate = dot_nt(pre, gate_up_rows(start, 0))
        up = dot_nt(pre, gate_up_rows(start, 1))
        square = gate * gate
        bend = jnp.tanh(gate * (root + (root * 0.044715) * square))
        half = 0.5 + 0.5 * bend
        act = gate * half
        slope = half + act * (1.0 - bend) * (root + (3.0 * root * 0.044715) * square)
        act_ref[:, span] = act
        slope_ref[:, span] = up * slope
        product = (act * up).astype(jnp.bfloat16)
        product_ref[0, :, span] = product
        down += dot_nt(product, pair_columns(start, start + chunk))
    out_ref[0] = (hidden + down * inverse_rms(down) * (1.0 + gf_ref[...])).astype(jnp.bfloat16)
    dy = cot_ref[0].astype(jnp.float32)
    d_down, dg_ffn = rms_back(down, gf_ref[...], dy)
    d_down = d_down.astype(jnp.bfloat16)
    ddown_ref[0] = d_down
    d_pre = jnp.zeros(x.shape, jnp.float32)
    for start in range(0, units, chunk):
        span = slice(start, start + chunk)
        d_product = dot_nn(d_down, pair_columns(start, start + chunk))
        d_gate = (d_product * slope_ref[:, span]).astype(jnp.bfloat16)
        d_up = (d_product * act_ref[:, span]).astype(jnp.bfloat16)
        dgate_ref[0, :, span] = d_gate
        dup_ref[0, :, span] = d_up
        d_pre += dot_nn(d_gate, gate_up_rows(start, 0)) + dot_nn(
            d_up, gate_up_rows(start, 1)
        )
    d_hidden, dg_pre = rms_back(hidden, gp_ref[...], d_pre)
    d_hidden = dy + d_hidden
    dhid_ref[0] = d_hidden
    d_att, dg_attn = rms_back(attended, ga_ref[...], d_hidden)
    d_att = d_att.astype(jnp.bfloat16)
    datt_ref[0] = d_att
    dg_ref[0] = jnp.concatenate([dg_attn, dg_pre, dg_ffn], axis=0)
    for head in range(heads):
        d_mixed = dot_nn(
            d_att, pair_columns(units + head * size, units + (head + 1) * size)
        ).astype(jnp.bfloat16)
        for t in range(2):
            dmix_ref[0, t, head * part : (head + 1) * part, :] = d_mixed[t * part : (t + 1) * part]


def attend_back_kernel(
    heads, waits, q_ref, qraw_ref, far_ref, near_ref, own_ref, qid_ref, kid_ref, mixed_ref, dmix_ref,
    cos_ref, sin_ref, gq_ref, *refs
):
    dfar_ref, dnear_ref, down_ref, dqraw_ref, dg_ref, win_ref, grad_ref = refs[waits:]
    size = q_ref.shape[-1]
    part = q_ref.shape[2] // heads
    span = part + WINDOW
    far, near = far_ref.shape[1], near_ref.shape[1]
    load_window(far_ref, near_ref, own_ref, win_ref)
    grad_ref[...] = jnp.zeros_like(grad_ref)
    dg = jnp.zeros((1, size), jnp.float32)
    for t in range(2):
        rows = slice(t * part, (t + 1) * part)
        window = slice(t * part, t * part + span)
        bias = mask_bias(qid_ref, kid_ref, t, part, span)
        keys = win_ref[window, :size]
        values = win_ref[window, size:]
        cosine, sine = cos_ref[0, rows, :], sin_ref[0, rows, :]
        for head in range(heads):
            line = slice(head * part, (head + 1) * part)
            lanes = slice(head * size, (head + 1) * size)
            query = q_ref[0, t, line, :]
            d_out = dmix_ref[0, t, line, :]
            weights = jnp.exp(dot_nt(query, keys) + bias)
            weights = weights * (1.0 / jnp.sum(weights, axis=-1, keepdims=True))
            delta = jnp.sum(
                d_out.astype(jnp.float32) * mixed_ref[0, rows, lanes].astype(jnp.float32),
                axis=-1,
                keepdims=True,
            )
            d_scores = (weights * (dot_nt(d_out, values) - delta)).astype(jnp.bfloat16)
            weights = weights.astype(jnp.bfloat16)
            grad_ref[window, :size] += dot_tn(d_scores, query)
            grad_ref[window, size:] += dot_tn(weights, d_out)
            d_query = dot_nn(d_scores, keys) * size ** (-0.5)
            d_raw, part_g = rms_back(
                qraw_ref[0, t, line, :].astype(jnp.float32),
                gq_ref[...],
                turn(d_query, cosine, -sine),
            )
            dqraw_ref[0, rows, lanes] = d_raw.astype(jnp.bfloat16)
            dg += part_g
    dg_ref[0] = dg
    dfar_ref[0] = grad_ref[:far, :].astype(jnp.bfloat16)
    dnear_ref[0] = grad_ref[far : far + near, :]
    down_ref[0] = grad_ref[far + near :, :]


def input_back_kernel(
    waits, own_ref, recv_ref, kraw_ref, cos_ref, sin_ref, wk_ref, wv_ref, dq_ref, wq_ref, x_ref, dhid_ref,
    gi_ref, gk_ref, *refs
):
    grad_ref, dpair_ref, dgi_ref, dgk_ref = refs[waits:]
    size = wk_ref.shape[0]
    total = own_ref[0] + recv_ref[0].astype(jnp.float32)
    d_key = turn(total[:, :size], cos_ref[0], -sin_ref[0])
    d_raw, dg_key = rms_back(kraw_ref[0].astype(jnp.float32), gk_ref[...], d_key)
    d_raw = d_raw.astype(jnp.bfloat16)
    d_value = total[:, size:].astype(jnp.bfloat16)
    dpair_ref[0, :, :size] = d_raw
    dpair_ref[0, :, size:] = d_value
    d_normed = dot_nn(dq_ref[0], wq_ref[...])
    d_normed += dot_nn(d_raw, wk_ref[...]) + dot_nn(d_value, wv_ref[...])
    d_x, dg_input = rms_back(x_ref[0].astype(jnp.float32), gi_ref[...], d_normed)
    grad_ref[0] = dhid_ref[0] + d_x
    dgi_ref[0] = dg_input
    dgk_ref[0] = dg_key


def flips(bit):
    return [(i, i ^ (1 << bit)) for i in range(lax.axis_size("dp"))]


def side(bit):
    return (lax.axis_index("dp") >> bit) & 1


def stack_step(own, received, bit, done, arrived=()):
    axis = sum(1 for other in done if other > bit)
    anywhere = pl.BlockSpec(memory_space=pl.ANY)
    block = pl.BlockSpec(memory_space=pltpu.VMEM)
    arrived = list(arrived)
    return pl.pallas_call(
        functools.partial(stack_kernel, axis, len(arrived)),
        out_shape=jax.ShapeDtypeStruct(own.shape[:axis] + (2,) + own.shape[axis:], own.dtype),
        in_specs=[pl.BlockSpec(memory_space=pltpu.SMEM)]
        + [block] * 2
        + [anywhere] * len(arrived),
        out_specs=block,
        compiler_params=pltpu.CompilerParams(vmem_limit_bytes=VMEM_BYTES),
    )(side(bit)[None].astype(jnp.int32), own, received, *arrived)


def gather_rows(shard, order):
    current, steps = shard, []
    for i, bit in enumerate(order):
        received = lax.ppermute(current, "dp", flips(bit))
        steps.append(received)
        current = stack_step(current, received, bit, order[:i])
    return current.reshape((lax.axis_size("dp"),) + shard.shape), steps


class RowSum:
    def __init__(self, parts, order, axis):
        self.terms = [
            (part.reshape((2,) * len(order) + part.shape[1:]), list(range(len(order) - 1, -1, -1)))
            for part in parts
        ]
        self.join = axis
        self.order = order
        self.chosen = {}
        self.received = []

    @classmethod
    def from_halves(cls, keep, send, order):
        result = cls([], order, -1)
        shape = (2,) * (len(order) - 1) + keep.shape[1:]
        left = list(range(len(order) - 1, 0, -1))
        received = lax.ppermute(send, "dp", flips(0))
        result.terms = [(keep.reshape(shape), left)]
        result.received = [(received.reshape(shape), left)]
        result.chosen = {0: side(0)}
        result.sent = send
        return result

    def total(self, other=None):
        picks = dict(self.chosen)
        if other is not None:
            picks[other] = 1 - side(other)
        pieces = [self.pick(part, bits, picks) for part, bits in self.terms]
        value = jnp.concatenate(pieces, axis=self.join) if len(pieces) > 1 else pieces[0]
        value = value.astype(jnp.float32)
        for part, bits in self.received:
            value += self.pick(part, bits, picks).astype(jnp.float32)
        return value.astype(jnp.bfloat16)

    def ordered_total(self, after, other=None):
        picks = dict(self.chosen)
        if other is not None:
            picks[other] = 1 - side(other)
        left = [b for b in range(len(self.order) - 1, -1, -1) if b not in picks]
        places = jnp.arange(2 ** len(left), dtype=jnp.int32)
        terms = self.terms + self.received
        index = []
        for part, bits in terms:
            flat = jnp.zeros_like(places)
            for bit in bits:
                if bit in picks:
                    value = picks[bit]
                else:
                    value = (places >> (len(left) - 1 - left.index(bit))) & 1
                flat = 2 * flat + value
            index.append(flat)
        block = terms[0][0].shape[-2:]
        anywhere = pl.BlockSpec(memory_space=pl.ANY)

        def spec(k):
            return pl.BlockSpec((1,) + block, lambda g, index: (index[k, g], 0, 0))

        out = pl.pallas_call(
            functools.partial(sum_kernel, len(terms)),
            out_shape=jax.ShapeDtypeStruct((len(places),) + block, jnp.bfloat16),
            grid_spec=pltpu.PrefetchScalarGridSpec(
                num_scalar_prefetch=1,
                grid=(len(places),),
                in_specs=[spec(k) for k in range(len(terms))] + [anywhere] * len(after),
                out_specs=pl.BlockSpec((1,) + block, lambda g, index: (g, 0, 0)),
            ),
            compiler_params=kernel_params(),
        )(jnp.stack(index), *[part.reshape((-1,) + block) for part, _ in terms], *after)
        return out.reshape((2,) * len(left) + block)

    def ordered_step(self, bit, after):
        self.sent = self.ordered_total(after, bit)
        self.receive(bit)

    def receive(self, bit):
        received = lax.ppermute(self.sent, "dp", flips(bit))
        self.chosen[bit] = side(bit)
        left = [b for b in range(len(self.order) - 1, -1, -1) if b not in self.chosen]
        self.received.append((received, left))
        return received

    def pick(self, part, bits, picks):
        bits = list(bits)
        for bit, where in picks.items():
            if bit in bits:
                part = lax.dynamic_index_in_dim(part, where, bits.index(bit), keepdims=False)
                bits.remove(bit)
        return part

    def send(self, bit):
        self.sent = self.total(bit)
        return self.sent

    def step(self, bit):
        self.send(bit)
        return self.receive(bit)


def seq_sum(part):
    count = lax.axis_size("seq")
    index = lax.axis_index("seq")
    half = count // 2
    terms = [part]

    def total():
        return sum(term.astype(jnp.float32) for term in terms)

    for t in range(half - 1):
        pairs = [(t, t + 1), (count - 1 - t, count - 2 - t)]
        terms.append(lax.ppermute(total().astype(jnp.bfloat16), "seq", pairs))
    middle = [(half - 1, half), (half, half - 1)]
    terms.append(lax.ppermute(total().astype(jnp.bfloat16), "seq", middle))
    result = total()
    for t in range(half - 2, -1, -1):
        pairs = [(t + 1, t), (count - 2 - t, count - 1 - t)]
        received = lax.ppermute(result.astype(jnp.bfloat16), "seq", pairs)
        outer = (index == t) | (index == count - 1 - t)
        result = jnp.where(outer, received.astype(jnp.float32), result)
    return result


def body(
    tokens,
    cotangent,
    segments,
    positions,
    query_weight,
    key_weight,
    value_weight,
    output_weight,
    gate_weight,
    up_weight,
    down_weight,
    norm_gains,
    query_first,
    key_first,
    value_first,
    output_first,
    gate_first,
    up_first,
    down_first,
    gains_first,
    query_second,
    key_second,
    value_second,
    output_second,
    gate_second,
    up_second,
    down_second,
    gains_second,
):
    count = lax.axis_size("dp")
    bits = (count - 1).bit_length()
    order_a = list(range(1, bits)) + [0]
    order_b = list(range(bits - 1, 0, -1)) + [0]
    low = jnp.bfloat16
    f32 = jnp.float32
    width = tokens.shape[2]
    key_rows = key_weight.shape[0]
    gain_rows = norm_gains.shape[0]
    rest_rows = 2 * key_rows + 16

    def array(shape, kind):
        return jax.ShapeDtypeStruct(shape, kind)

    query_shard, rest_shard = pl.pallas_call(
        cast_first_kernel,
        out_shape=[array(query_weight.shape, low), array((rest_rows, width), low)],
    )(query_weight, key_weight, value_weight, norm_gains[None])
    query_all, query_steps = gather_rows(query_shard, order_a)
    rest_all, rest_steps = gather_rows(rest_shard, order_b)
    w_query = query_all.reshape(-1, width)
    w_key = rest_all[:, :key_rows].reshape(-1, width)
    w_value = rest_all[:, key_rows : 2 * key_rows].reshape(-1, width)
    gains_all = rest_all[:, 2 * key_rows, :gain_rows].reshape(-1)
    block = pl.BlockSpec(memory_space=pltpu.VMEM)
    anywhere = pl.BlockSpec(memory_space=pl.ANY)
    arrived = [query_steps[-2], rest_steps[-2]]
    gate_up_shard, pair_shard = pl.pallas_call(
        functools.partial(cast_rest_kernel, len(arrived)),
        out_shape=[
            array((2 * gate_weight.shape[0], width), low),
            array((down_weight.shape[0], down_weight.shape[1] + output_weight.shape[1]), low),
        ],
        in_specs=[block] * 4 + [anywhere] * len(arrived),
    )(gate_weight, up_weight, down_weight, output_weight, *arrived)

    seqs, rows, _ = tokens.shape
    size = w_key.shape[0]
    heads = w_query.shape[0] // size
    units = down_weight.shape[1]
    shards = lax.axis_size("seq")
    far = WINDOW - rows
    part = rows // 2
    span = part + WINDOW
    gains_float = gains_all.astype(jnp.float32)[None]
    g_input, g_attn, g_pre, g_ffn = (
        gains_float[:, i * width : (i + 1) * width] for i in range(4)
    )
    g_query = gains_float[:, 4 * width : 4 * width + size]
    g_key = gains_float[:, 4 * width + size : 4 * width + 2 * size]
    angles = positions.astype(jnp.float32)[..., None] * frequencies(size)
    cosine, sine = jnp.cos(angles), jnp.sin(angles)
    core_side = side(0)[None].astype(jnp.int32)
    first_row = lax.axis_index("seq") * rows
    padded = jnp.concatenate([jnp.full((seqs, WINDOW), -1, jnp.int32), segments], axis=1)
    window_ids = lax.dynamic_slice_in_dim(padded, first_row, WINDOW + rows, 1)
    query_ids = window_ids[:, WINDOW:, None]
    key_ids = jnp.stack([window_ids[:, :span], window_ids[:, part:]], axis=1)[:, :, None, :]

    def call(kernel, outs, out_specs, in_specs, scratch, flops, moved):
        return pl.pallas_call(
            kernel,
            grid=(seqs,),
            out_shape=outs,
            in_specs=in_specs,
            out_specs=out_specs,
            scratch_shapes=scratch,
            compiler_params=kernel_params(),
            cost_estimate=pl.CostEstimate(flops=flops, bytes_accessed=moved, transcendentals=0),
        )

    tokens_all = seqs * rows
    head_block = per_seq(2, heads * part, size)
    q_shape = (seqs, 2, heads * part, size)
    normed, pair_own, key_raw = call(
        functools.partial(project_pair_kernel, 2),
        [
            array((seqs, rows, width), low),
            array((seqs, rows, 2 * size), low),
            array((seqs, rows, size), low),
        ],
        [per_seq(rows, width), per_seq(rows, 2 * size), per_seq(rows, size)],
        [
            per_seq(rows, width),
            per_seq(rows, size // 2),
            per_seq(rows, size // 2),
            whole(*w_key.shape),
            whole(*w_value.shape),
            whole(1, width),
            whole(1, size),
            anywhere,
            anywhere,
        ],
        [],
        4 * tokens_all * width * size,
        6_000_000,
    )(tokens, cosine, sine, w_key, w_value, g_input, g_key, query_ids, key_ids)
    pair_first = lax.ppermute(pair_shard, "dp", flips(order_b[0]))
    query, query_raw = call(
        functools.partial(project_query_kernel, heads, 1),
        [array(q_shape, low), array(q_shape, low)],
        [head_block, head_block],
        [
            per_seq(rows, width),
            per_seq(rows, size // 2),
            per_seq(rows, size // 2),
            whole(*w_query.shape),
            whole(1, size),
            anywhere,
        ],
        [],
        2 * tokens_all * width * heads * size,
        8_000_000,
    )(normed, cosine, sine, w_query, g_query, pair_first)

    upward = [(i, i + 1) for i in range(shards - 1)]
    pair_near = lax.ppermute(pair_own, "seq", upward)
    gate_up_half, pair_half = gate_up_shard, pair_shard
    pair_far = None
    for i in range(bits - 1):
        pair_received = pair_first
        if i:
            pair_received = lax.ppermute(pair_half, "dp", flips(order_b[i]))
        gate_up_received = lax.ppermute(gate_up_half, "dp", flips(order_a[i]))
        waits = [query] if i == 0 else [pair_far]
        pair_half = stack_step(pair_half, pair_received, order_b[i], order_b[:i], waits)
        gate_up_half = stack_step(gate_up_half, gate_up_received, order_a[i], order_a[:i], waits)
        if i == 0:
            far_send = pl.pallas_call(
                functools.partial(tail_rows_kernel, 2),
                out_shape=array((seqs, far, 2 * size), low),
                in_specs=[block, anywhere, anywhere],
                out_specs=block,
                compiler_params=pltpu.CompilerParams(vmem_limit_bytes=VMEM_BYTES),
            )(pair_near, pair_half, gate_up_half)
            pair_far = lax.ppermute(far_send, "seq", upward[1:])
    pair_half = pair_half.reshape((count // 2,) + pair_shard.shape)
    gate_up_half = gate_up_half.reshape((count // 2,) + gate_up_shard.shape)
    pair_received = lax.ppermute(pair_half, "dp", flips(0))
    gate_up_received = lax.ppermute(gate_up_half, "dp", flips(0))

    window_specs = [
        per_seq(far, 2 * size),
        per_seq(rows, 2 * size),
        per_seq(rows, 2 * size),
        per_seq(rows, 1),
        per_seq(2, 1, span),
    ]
    attend_flops = 8 * tokens_all * heads * span * size
    mixed = call(
        functools.partial(attend_kernel, heads),
        array((seqs, rows, heads * size), low),
        per_seq(rows, heads * size),
        [head_block] + window_specs,
        [pltpu.VMEM((WINDOW + rows, 2 * size), low)],
        attend_flops,
        16_000_000,
    )(query, pair_far, pair_near, pair_own, query_ids, key_ids)

    (
        layer_output,
        pre_low,
        product_low,
        grad_down_low,
        grad_gate_low,
        grad_up_low,
        grad_attended_low,
        grad_hidden,
        grad_mixed,
        grad_gains_middle,
    ) = call(
        functools.partial(middle_kernel, heads, 512),
        [
            array((seqs, rows, width), low),
            array((seqs, rows, width), low),
            array((seqs, rows, units), low),
            array((seqs, rows, width), low),
            array((seqs, rows, units), low),
            array((seqs, rows, units), low),
            array((seqs, rows, width), low),
            array((seqs, rows, width), f32),
            array(q_shape, low),
            array((seqs, 3, width), f32),
        ],
        [
            per_seq(rows, width),
            per_seq(rows, width),
            per_seq(rows, units),
            per_seq(rows, width),
            per_seq(rows, units),
            per_seq(rows, units),
            per_seq(rows, width),
            per_seq(rows, width),
            head_block,
            per_seq(3, width),
        ],
        [
            pl.BlockSpec(memory_space=pltpu.SMEM),
            per_seq(rows, heads * size),
            per_seq(rows, width),
            per_seq(rows, width),
            anywhere,
            anywhere,
            anywhere,
            anywhere,
            whole(1, width),
            whole(1, width),
            whole(1, width),
        ],
        [
            pltpu.VMEM((rows, units), f32),
            pltpu.VMEM((rows, units), f32),
            pltpu.VMEM((count // 2, 2) + gate_up_shard.shape, low),
            pltpu.VMEM((count // 2, 2) + pair_shard.shape, low),
            pltpu.SemaphoreType.DMA((4,)),
        ],
        4 * tokens_all * width * (heads * size + 3 * units),
        40_000_000,
    )(
        core_side, mixed, tokens, cotangent, gate_up_half, gate_up_received, pair_half, pair_received,
        g_attn, g_pre, g_ffn,
    )

    def flat(values):
        return values.reshape(tokens_all, values.shape[-1])

    def grad_blocks(gradient, inputs):
        product = weight_grad(flat(gradient), flat(inputs)).astype(low)
        return product.reshape(count, -1, product.shape[1])

    back_a = [0] + order_a[:-1]
    back_b = [0] + order_b[:-1]
    shard_units = gate_weight.shape[0]
    shard_rows = down_weight.shape[0]
    half = count // 2
    direct = shard_units % 128 == 0 and shard_rows % 16 == 0
    if direct:
        columns = 512
        first = units // columns
        last = heads * size // columns
        pair_block = pl.BlockSpec((half, shard_rows, columns), lambda k, side: (0, 0, k))
        pair_shape = array((half, shard_rows, units + heads * size), low)
        fixed = pl.BlockSpec(
            (tokens_all, width), lambda k, side: (0, 0), pipeline_mode=pl.Buffered(1)
        )
        pair_send, pair_keep = pl.pallas_call(
            functools.partial(pair_grad_kernel, first),
            out_shape=[pair_shape, pair_shape],
            grid_spec=pltpu.PrefetchScalarGridSpec(
                num_scalar_prefetch=1,
                grid=(first + last,),
                in_specs=[
                    pl.BlockSpec(
                        (tokens_all, columns), lambda k, side: (0, jnp.minimum(k, first - 1))
                    ),
                    pl.BlockSpec(
                        (tokens_all, columns), lambda k, side: (0, jnp.maximum(k - first, 0))
                    ),
                    fixed,
                    fixed,
                ],
                out_specs=[pair_block, pair_block],
                scratch_shapes=[
                    pltpu.VMEM((width, tokens_all), low),
                    pltpu.VMEM((width, columns), f32),
                ],
            ),
            compiler_params=kernel_params(),
            cost_estimate=pl.CostEstimate(
                flops=2 * tokens_all * width * (units + heads * size),
                bytes_accessed=13_000_000,
                transcendentals=0,
            ),
        )(core_side, flat(product_low), flat(mixed), flat(grad_down_low), flat(grad_attended_low))
        down_out_sum = RowSum.from_halves(pair_keep, pair_send, back_b)

        def shard_of(g, side):
            return (0, 2 * (g % half) + jnp.where(g < half, 1 - side[0], side[0]))

        block_shape = (1, 2 * shard_units, width)
        half_shape = array((half, 2 * shard_units, width), low)
        gate_up_send, gate_up_keep = pl.pallas_call(
            gate_up_grad_kernel,
            out_shape=[half_shape, half_shape],
            grid_spec=pltpu.PrefetchScalarGridSpec(
                num_scalar_prefetch=1,
                grid=(count,),
                in_specs=[
                    pl.BlockSpec((tokens_all, shard_units), shard_of),
                    pl.BlockSpec((tokens_all, shard_units), shard_of),
                    fixed,
                    anywhere,
                ],
                out_specs=[
                    pl.BlockSpec(block_shape, lambda g, side: (jnp.minimum(g, half - 1), 0, 0)),
                    pl.BlockSpec(block_shape, lambda g, side: (jnp.maximum(g - half, 0), 0, 0)),
                ],
            ),
            compiler_params=kernel_params(),
            cost_estimate=pl.CostEstimate(
                flops=4 * tokens_all * width * units, bytes_accessed=14_000_000, transcendentals=0
            ),
        )(core_side, flat(grad_gate_low), flat(grad_up_low), flat(pre_low), pair_send)
        gate_up_sum = RowSum.from_halves(gate_up_keep, gate_up_send, back_a)
    else:
        pair_blocks = jnp.concatenate(
            [grad_blocks(grad_down_low, product_low), grad_blocks(grad_attended_low, mixed)], axis=-1
        )
        down_out_sum = RowSum([pair_blocks], back_b, -1)
        down_out_sum.step(0)
        gate_up_blocks = jnp.concatenate(
            [grad_blocks(grad_gate_low, pre_low), grad_blocks(grad_up_low, pre_low)], axis=-2
        )
        gate_up_sum = RowSum([gate_up_blocks], back_a, -2)
        gate_up_sum.step(0)

    def at_seq(s, *tail):
        return pl.BlockSpec((1,) + tail, lambda g: (s,) + (0,) * len(tail))

    def seq_call(kernel, outs, out_specs, in_specs, operands, scratch, alias, flops):
        return pl.pallas_call(
            kernel,
            grid=(1,),
            out_shape=outs,
            in_specs=in_specs,
            out_specs=out_specs,
            scratch_shapes=scratch,
            input_output_aliases=alias,
            compiler_params=kernel_params(),
            cost_estimate=pl.CostEstimate(
                flops=flops, bytes_accessed=8_000_000, transcendentals=0
            ),
        )(*operands)

    def attend_back(s, buffer, arrived):
        kinds = [
            array((1, far, 2 * size), low),
            array((1, rows, 2 * size), f32),
            array((1, rows, 2 * size), f32),
            array((seqs, rows, heads * size), low),
            array((1, 1, size), f32),
        ]
        specs = [
            at_seq(0, far, 2 * size),
            at_seq(0, rows, 2 * size),
            at_seq(0, rows, 2 * size),
            at_seq(s, rows, heads * size),
            at_seq(0, 1, size),
        ]
        in_specs = [
            at_seq(s, 2, heads * part, size),
            at_seq(s, 2, heads * part, size),
            at_seq(s, far, 2 * size),
            at_seq(s, rows, 2 * size),
            at_seq(s, rows, 2 * size),
            at_seq(s, rows, 1),
            at_seq(s, 2, 1, span),
            at_seq(s, rows, heads * size),
            at_seq(s, 2, heads * part, size),
            at_seq(s, rows, size // 2),
            at_seq(s, rows, size // 2),
            whole(1, size),
        ]
        operands = [
            query, query_raw, pair_far, pair_near, pair_own, query_ids, key_ids, mixed, grad_mixed,
            cosine, sine, g_query,
        ]
        alias = {}
        extra = list(arrived)
        if buffer is not None:
            alias = {len(operands): 3}
            extra = [buffer] + extra
        return seq_call(
            functools.partial(attend_back_kernel, heads, len(extra)),
            kinds,
            specs,
            in_specs + [anywhere] * len(extra),
            operands + extra,
            [
                pltpu.VMEM((WINDOW + rows, 2 * size), low),
                pltpu.VMEM((WINDOW + rows, 2 * size), f32),
            ],
            alias,
            attend_flops * 3 // seqs,
        )

    downward = [(i + 1, i) for i in range(shards - 1)]
    grad_query_low = None
    arrived = [gate_up_sum.sent]

    def near_total(grad_near, from_far, after):
        return pl.pallas_call(
            functools.partial(near_sum_kernel, len(after)),
            out_shape=array(grad_near.shape, low),
            in_specs=[block] * 2 + [anywhere] * len(after),
            out_specs=block,
        )(grad_near, from_far, *after)

    own_parts, query_gains, near_sums, far_parts, near_parts = [], [], [], [], []
    for s in range(seqs):
        grad_far, grad_near, grad_own, grad_query_low, g_part = attend_back(
            s, grad_query_low, arrived
        )
        from_far = lax.ppermute(grad_far, "seq", downward[1:])
        own_parts.append(grad_own)
        query_gains.append(g_part)
        far_parts.append(from_far)
        near_parts.append(grad_near)
        if s == 0:
            down_out_sum.ordered_step(back_b[1], [grad_own])
            gate_up_sum.ordered_step(back_a[1], [down_out_sum.sent])
            arrived = [gate_up_sum.sent]
        elif s == 1:
            near_sums.append(near_total(near_parts[0], far_parts[0], [grad_own]))
            arrived = [near_sums[0]]
    for bit in back_b[2:]:
        down_out_sum.ordered_step(bit, [own_parts[-1]])
    near_sums.append(near_total(near_parts[1], far_parts[1], [down_out_sum.sent]))
    query_columns = heads * size
    grad_w_query = pl.pallas_call(
        functools.partial(query_grad_kernel, 2),
        grid=(heads,),
        out_shape=array((query_columns, width), low),
        in_specs=[
            pl.BlockSpec((tokens_all, size), lambda i: (0, i)),
            whole(tokens_all, width),
            anywhere,
            anywhere,
        ],
        out_specs=pl.BlockSpec((size, width), lambda i: (i, 0)),
        compiler_params=kernel_params(),
        cost_estimate=pl.CostEstimate(
            flops=2 * tokens_all * width * query_columns, bytes_accessed=5_000_000, transcendentals=0
        ),
    )(flat(grad_query_low), flat(normed), near_sums[1], down_out_sum.sent)
    near_sums.append(near_total(near_parts[2], far_parts[2], [grad_w_query]))
    from_near = [lax.ppermute(near_sum, "seq", downward) for near_sum in near_sums]
    for bit in back_a[2:]:
        gate_up_sum.ordered_step(bit, [near_sums[2]])

    def input_back(s, buffers, arrived):
        kinds = [
            array((seqs, rows, width), f32),
            array((seqs, rows, 2 * size), low),
            array((1, 1, width), f32),
            array((1, 1, size), f32),
        ]
        specs = [
            at_seq(s, rows, width),
            at_seq(s, rows, 2 * size),
            at_seq(0, 1, width),
            at_seq(0, 1, size),
        ]
        in_specs = [
            at_seq(0, rows, 2 * size),
            at_seq(0, rows, 2 * size),
            at_seq(s, rows, size),
            at_seq(s, rows, size // 2),
            at_seq(s, rows, size // 2),
            whole(*w_key.shape),
            whole(*w_value.shape),
            at_seq(s, rows, heads * size),
            whole(*w_query.shape),
            at_seq(s, rows, width),
            at_seq(s, rows, width),
            whole(1, width),
            whole(1, size),
        ]
        operands = [
            own_parts[s], from_near[s], key_raw, cosine, sine, w_key, w_value, grad_query_low,
            w_query, tokens, grad_hidden, g_input, g_key,
        ]
        alias = {}
        extra = list(arrived)
        if buffers:
            alias = {len(operands): 0, len(operands) + 1: 1}
            extra = list(buffers) + extra
        return seq_call(
            functools.partial(input_back_kernel, len(extra)),
            kinds,
            specs,
            in_specs + [anywhere] * len(extra),
            operands + extra,
            [],
            alias,
            2 * rows * width * size * (heads + 2),
        )

    buffers = []
    input_gains, key_gains = [], []
    for s in range(seqs):
        waits = [gate_up_sum.sent]
        if s == seqs - 1:
            down_out_part = down_out_sum.ordered_total([buffers[0]])
            waits = [down_out_part]
        *buffers, g_part, g_key_part = input_back(s, buffers, waits)
        input_gains.append(g_part)
        key_gains.append(g_key_part)
    input_grad, grad_pair_low = buffers
    key_value_blocks = grad_blocks(grad_pair_low, normed).reshape(2, count, key_rows, width)
    grad_gains = jnp.concatenate(
        [
            sum(input_gains).reshape(-1),
            jnp.sum(grad_gains_middle, axis=0).reshape(-1),
            sum(query_gains).reshape(-1),
            sum(key_gains).reshape(-1),
        ]
    )
    gain_block = jnp.pad(
        grad_gains.astype(low).reshape(count, 1, gain_rows),
        ((0, 0), (0, 15), (0, width - gain_rows)),
    )
    query_rows = query_weight.shape[0]
    rest_sum = RowSum(
        [
            grad_w_query.reshape(count, query_rows, width),
            key_value_blocks[0],
            key_value_blocks[1],
            gain_block,
        ],
        back_b,
        -2,
    )
    for bit in back_b:
        rest_sum.step(bit)
    down_out_total = seq_sum(down_out_part)
    gate_up_part = gate_up_sum.ordered_total([input_grad])
    gate_total = seq_sum(gate_up_part[:shard_units])
    up_total = seq_sum(gate_up_part[shard_units:])
    rest_total = seq_sum(rest_sum.total())
    query_total = rest_total[:query_rows]
    rest_total = rest_total[query_rows:]
    down_total = down_out_total[:, :units]
    output_total = down_out_total[:, units:]
    key_total = rest_total[:key_rows]
    value_total = rest_total[key_rows : 2 * key_rows]
    gains_total = rest_total[2 * key_rows, :gain_rows]
    query_momentum, query_variance, query_updated = adam_step(
        query_weight, query_first, query_second, query_total, WEIGHT_DECAY
    )
    key_momentum, key_variance, key_updated = adam_step(
        key_weight, key_first, key_second, key_total, WEIGHT_DECAY
    )
    value_momentum, value_variance, value_updated = adam_step(
        value_weight, value_first, value_second, value_total, WEIGHT_DECAY
    )
    output_momentum, output_variance, output_updated = adam_step(
        output_weight, output_first, output_second, output_total, WEIGHT_DECAY
    )
    gate_momentum, gate_variance, gate_updated = adam_step(
        gate_weight, gate_first, gate_second, gate_total, WEIGHT_DECAY
    )
    up_momentum, up_variance, up_updated = adam_step(
        up_weight, up_first, up_second, up_total, WEIGHT_DECAY
    )
    down_momentum, down_variance, down_updated = adam_step(
        down_weight, down_first, down_second, down_total, WEIGHT_DECAY
    )
    gains_momentum, gains_variance, gains_updated = adam_step(
        norm_gains, gains_first, gains_second, gains_total, 0.0
    )
    return (
        layer_output,
        input_grad,
        query_momentum,
        key_momentum,
        value_momentum,
        output_momentum,
        gate_momentum,
        up_momentum,
        down_momentum,
        gains_momentum,
        query_variance,
        key_variance,
        value_variance,
        output_variance,
        gate_variance,
        up_variance,
        down_variance,
        gains_variance,
        query_updated,
        key_updated,
        value_updated,
        output_updated,
        gate_updated,
        up_updated,
        down_updated,
        gains_updated,
    )


def solution(mesh):
    return jax.shard_map(
        body,
        mesh=mesh,
        in_specs=(
            P("dp", "seq", None),
            P("dp", "seq", None),
            P("dp", None),
            P("dp", "seq"),
            P("dp", None),
            P("dp", None),
            P("dp", None),
            P("dp", None),
            P("dp", None),
            P("dp", None),
            P("dp", None),
            P("dp"),
            P("dp", None),
            P("dp", None),
            P("dp", None),
            P("dp", None),
            P("dp", None),
            P("dp", None),
            P("dp", None),
            P("dp"),
            P("dp", None),
            P("dp", None),
            P("dp", None),
            P("dp", None),
            P("dp", None),
            P("dp", None),
            P("dp", None),
            P("dp"),
        ),
        out_specs=(
            P("dp", "seq", None),
            P("dp", "seq", None),
            P("dp", None),
            P("dp", None),
            P("dp", None),
            P("dp", None),
            P("dp", None),
            P("dp", None),
            P("dp", None),
            P("dp"),
            P("dp", None),
            P("dp", None),
            P("dp", None),
            P("dp", None),
            P("dp", None),
            P("dp", None),
            P("dp", None),
            P("dp"),
            P("dp", None),
            P("dp", None),
            P("dp", None),
            P("dp", None),
            P("dp", None),
            P("dp", None),
            P("dp", None),
            P("dp"),
        ),
        check_vma=False,
    )
```

```python
import functools
import math

import jax
import jax.numpy as jnp
from jax import lax
from jax.experimental import pallas as pl
from jax.experimental.pallas import tpu as pltpu
from jax.sharding import PartitionSpec as P

WINDOW = 512
STEP = 10


NORM_EPSILON = 1e-06
ROPE_BASE = 10000.0
LEARN_RATE = 0.08
BETA_FIRST = 0.9
BETA_SECOND = 0.95
ADAM_EPSILON = 1e-08
WEIGHT_DECAY = 0.01
MASKED_SCORE = -1000000000.0


def frequencies(size):
    return ROPE_BASE ** (-2.0 * jnp.arange(size // 2).astype(jnp.float32) / size)


def weight_grad(gradients, inputs):
    return lax.dot_general(
        gradients, inputs, (((0,), (0,)), ((), ())), preferred_element_type=jnp.float32
    )


def adam_step(weight, first_moment, second_moment, gradient, decay_rate):
    momentum = BETA_FIRST * first_moment + (1.0 - BETA_FIRST) * gradient
    variance = BETA_SECOND * second_moment + (1.0 - BETA_SECOND) * gradient * gradient
    corrected = momentum / (1.0 - BETA_FIRST**STEP)
    scaled = variance / (1.0 - BETA_SECOND**STEP)
    updated = weight - LEARN_RATE * (
        corrected / (jnp.sqrt(scaled) + ADAM_EPSILON) + decay_rate * weight
    )
    return (momentum, variance, updated)


VMEM_BYTES = 56 * 1024 * 1024


def kernel_params():
    return pltpu.CompilerParams(
        dimension_semantics=("arbitrary",), vmem_limit_bytes=VMEM_BYTES
    )


def per_seq(*tail):
    return pl.BlockSpec((1,) + tail, lambda s: (s,) + (0,) * len(tail))


def whole(*shape):
    return pl.BlockSpec(shape, lambda s: (0,) * len(shape), pipeline_mode=pl.Buffered(1))


def dot_nt(a, b):
    return lax.dot_general(a, b, (((1,), (1,)), ((), ())), preferred_element_type=jnp.float32)


def dot_nn(a, b):
    return lax.dot_general(a, b, (((1,), (0,)), ((), ())), preferred_element_type=jnp.float32)


def dot_tn(a, b):
    return lax.dot_general(a, b, (((0,), (0,)), ((), ())), preferred_element_type=jnp.float32)


def inverse_rms(values):
    return lax.rsqrt(jnp.mean(values * values, axis=-1, keepdims=True) + NORM_EPSILON)


def rms_back(values, gain, grad):
    inverse = inverse_rms(values)
    unit = values * inverse
    scaled = grad * (1.0 + gain)
    return (
        inverse * (scaled - unit * jnp.mean(unit * scaled, axis=-1, keepdims=True)),
        jnp.sum(grad * unit, axis=0, keepdims=True),
    )


def turn(values, cosine, sine):
    half = values.shape[-1] // 2
    first, second = values[:, :half], values[:, half:]
    return jnp.concatenate(
        [first * cosine - second * sine, second * cosine + first * sine], axis=-1
    )


def stack_heads(values, heads):
    return jnp.concatenate([values] * heads, axis=0)


def cast_first_kernel(wq_ref, wk_ref, wv_ref, gain_ref, out_ref):
    width = wq_ref.shape[1]
    gains = gain_ref[...]
    tail = width - gains.shape[1]
    block = jnp.broadcast_to(gains, (16, gains.shape[1]))
    if tail:
        block = jnp.concatenate([block, jnp.zeros((16, tail), jnp.float32)], axis=1)
    parts = [wq_ref[...], wk_ref[...], wv_ref[...], block]
    out_ref[...] = jnp.concatenate(parts, axis=0).astype(jnp.bfloat16)


def cast_rest_kernel(waits, wg_ref, wu_ref, wd_ref, wo_ref, *refs):
    gate_ref, up_ref, first_ref, second_ref = refs[waits:]
    cut = first_ref.shape[1]
    rest = wd_ref.shape[1] - cut
    gate_ref[...] = wg_ref[...].astype(jnp.bfloat16)
    up_ref[...] = wu_ref[...].astype(jnp.bfloat16)
    first_ref[...] = wd_ref[:, :cut].astype(jnp.bfloat16)
    second_ref[:, :rest] = wd_ref[:, cut:].astype(jnp.bfloat16)
    second_ref[:, rest:] = wo_ref[...].astype(jnp.bfloat16)


def stack_kernel(bits, axes, waits, index_ref, *refs):
    count = len(bits)
    outs = refs[2 * count + waits :]
    for i in range(count):
        upper = (index_ref[0] >> bits[i]) & 1
        lead = (slice(None),) * axes[i]
        outs[i][lead + (upper,)] = refs[2 * i][...]
        outs[i][lead + (1 - upper,)] = refs[2 * i + 1][...]


def tail_rows_kernel(waits, near_ref, *refs):
    out_ref = refs[waits]
    out_ref[...] = near_ref[:, near_ref.shape[1] - out_ref.shape[1] :]


def near_sum_kernel(waits, near_ref, far_ref, *refs):
    out_ref = refs[waits]
    keep = near_ref.shape[1] - far_ref.shape[1]
    out_ref[0, :keep] = near_ref[0, :keep].astype(jnp.bfloat16)
    total = near_ref[0, keep:] + far_ref[0].astype(jnp.float32)
    out_ref[0, keep:] = total.astype(jnp.bfloat16)


def sum_kernel(count, index_ref, *refs):
    total = refs[0][0].astype(jnp.float32)
    for ref in refs[1:count]:
        total += ref[0].astype(jnp.float32)
    refs[-1][0] = total.astype(jnp.bfloat16)


def gate_up_grad_kernel(side_ref, dgate_ref, dup_ref, pre_ref, after_ref, send_ref, keep_ref):
    step = pl.program_id(0)
    half = pl.num_programs(0) // 2
    rows = dgate_ref.shape[1]

    gate = dot_tn(dgate_ref[...], pre_ref[...]).astype(jnp.bfloat16)
    up = dot_tn(dup_ref[...], pre_ref[...]).astype(jnp.bfloat16)

    @pl.when(step < half)
    def _():
        send_ref[0, :rows, :] = gate
        send_ref[0, rows:, :] = up

    @pl.when(step >= half)
    def _():
        keep_ref[0, :rows, :] = gate
        keep_ref[0, rows:, :] = up


def pair_grad_kernel(
    first, side_ref, product_ref, mixed_ref, ddown_ref, datt_ref, send_ref, keep_ref, turned_ref, total_ref
):
    step = pl.program_id(0)
    upper = side_ref[0]
    half, rows = send_ref.shape[0], send_ref.shape[1]

    @pl.when(step == 0)
    def _():
        turned_ref[...] = ddown_ref[...].T

    @pl.when(step == first)
    def _():
        turned_ref[...] = datt_ref[...].T

    @pl.when(step < first)
    def _():
        total_ref[...] = dot_nn(turned_ref[...], product_ref[...])

    @pl.when(step >= first)
    def _():
        total_ref[...] = dot_nn(turned_ref[...], mixed_ref[...])

    for i in range(half):
        mine = pl.multiple_of((2 * i + upper) * rows, rows)
        other = pl.multiple_of((2 * i + 1 - upper) * rows, rows)
        keep_ref[i] = total_ref[pl.ds(mine, rows), :].astype(jnp.bfloat16)
        send_ref[i] = total_ref[pl.ds(other, rows), :].astype(jnp.bfloat16)


def query_grad_kernel(waits, dq_ref, normed_ref, *refs):
    refs[waits][...] = dot_tn(dq_ref[...], normed_ref[...]).astype(jnp.bfloat16)


def project_pair_kernel(
    waits, x_ref, cos_ref, sin_ref, wk_ref, wv_ref, gi_ref, gk_ref, *refs
):
    normed_ref, kv_ref, kraw_ref = refs[waits:]
    x = x_ref[0].astype(jnp.float32)
    size = wk_ref.shape[0]
    normed = (x * inverse_rms(x) * (1.0 + gi_ref[...])).astype(jnp.bfloat16)
    normed_ref[0] = normed
    k_raw = dot_nt(normed, wk_ref[...])
    kraw_ref[0] = k_raw.astype(jnp.bfloat16)
    key = turn(k_raw * inverse_rms(k_raw) * (1.0 + gk_ref[...]), cos_ref[0], sin_ref[0])
    kv_ref[0, :, :size] = key.astype(jnp.bfloat16)
    kv_ref[0, :, size:] = dot_nt(normed, wv_ref[...]).astype(jnp.bfloat16)


def project_query_kernel(
    heads, waits, normed_ref, cos_ref, sin_ref, wq_ref, gq_ref, *refs
):
    q_ref, qraw_ref = refs[waits:]
    size = gq_ref.shape[-1]
    part = normed_ref.shape[1] // 2
    normed = normed_ref[0]
    cosine, sine = cos_ref[0], sin_ref[0]
    for head in range(heads):
        raw = dot_nt(normed, wq_ref[head * size : (head + 1) * size, :])
        query = turn(raw * inverse_rms(raw) * (1.0 + gq_ref[...]), cosine, sine)
        query = (query * size ** (-0.5)).astype(jnp.bfloat16)
        raw = raw.astype(jnp.bfloat16)
        for t in range(2):
            span = slice(head * part, (head + 1) * part)
            q_ref[0, t, span, :] = query[t * part : (t + 1) * part]
            qraw_ref[0, t, span, :] = raw[t * part : (t + 1) * part]


def load_window(far_ref, near_ref, own_ref, win_ref):
    far, near = far_ref.shape[1], near_ref.shape[1]
    win_ref[:far, :] = far_ref[0]
    win_ref[far : far + near, :] = near_ref[0]
    win_ref[far + near :, :] = own_ref[0]


def mask_bias(qid_ref, kid_ref, t, part, span):
    ids = qid_ref[0, t * part : (t + 1) * part, :] == kid_ref[0, t]
    row = lax.broadcasted_iota(jnp.int32, (part, span), 0)
    column = lax.broadcasted_iota(jnp.int32, (part, span), 1)
    ok = ids & (column > row) & (column <= row + WINDOW)
    return jnp.where(ok, 0.0, MASKED_SCORE)


def attend_kernel(heads, q_ref, far_ref, near_ref, own_ref, qid_ref, kid_ref, mixed_ref, win_ref):
    size = q_ref.shape[-1]
    part = q_ref.shape[2] // heads
    span = part + WINDOW
    load_window(far_ref, near_ref, own_ref, win_ref)
    for t in range(2):
        bias = mask_bias(qid_ref, kid_ref, t, part, span)
        keys = win_ref[t * part : t * part + span, :size]
        values = win_ref[t * part : t * part + span, size:]
        for head in range(heads):
            scores = dot_nt(q_ref[0, t, head * part : (head + 1) * part, :], keys)
            weights = jnp.exp(scores + bias)
            total = jnp.sum(weights, axis=-1, keepdims=True)
            mixed = dot_nn(weights.astype(jnp.bfloat16), values) / total
            mixed_ref[0, t * part : (t + 1) * part, head * size : (head + 1) * size] = (
                mixed.astype(jnp.bfloat16)
            )


def middle_kernel(
    heads, chunk, side_ref, mixed_ref, x_ref, cot_ref, gate_own_ref, gate_got_ref, up_own_ref, up_got_ref,
    first_own_ref, first_got_ref, second_own_ref, second_got_ref, ga_ref, gp_ref, gf_ref,
    out_ref, pre_ref, product_ref, ddown_ref, dgate_ref, dup_ref, datt_ref, dhid_ref, dmix_ref, dg_ref,
    act_ref, slope_ref, wgu_ref, wdo_blocks_ref, sems,
):
    @pl.when(pl.program_id(0) == 0)
    def _():
        upper = side_ref[0]
        copies = []
        shard = gate_own_ref.shape[1]
        cut = first_own_ref.shape[2]
        places = [
            (slice(None, cut), first_own_ref, first_got_ref),
            (slice(cut, None), second_own_ref, second_got_ref),
        ]
        for lanes, own, got in places:
            for place, source in ((upper, own), (1 - upper, got)):
                target = wdo_blocks_ref.at[:, place, :, lanes]
                copies.append(pltpu.make_async_copy(source, target, sems.at[len(copies)]))
        places = [
            (slice(None, shard), gate_own_ref, gate_got_ref),
            (slice(shard, None), up_own_ref, up_got_ref),
        ]
        for lines, own, got in places:
            for place, source in ((upper, own), (1 - upper, got)):
                target = wgu_ref.at[:, place, lines, :]
                copies.append(pltpu.make_async_copy(source, target, sems.at[len(copies)]))
        for copy in copies:
            copy.start()
        for copy in copies:
            copy.wait()

    def pair_columns(start, stop):
        picked = wdo_blocks_ref[:, :, :, start:stop]
        return picked.reshape(-1, stop - start)

    shard = wgu_ref.shape[2] // 2
    units = 2 * wgu_ref.shape[0] * shard
    group = chunk // shard

    def gate_up_rows(start, which):
        first = start // shard // 2
        picked = wgu_ref[first : first + group // 2, :, which * shard : (which + 1) * shard, :]
        return picked.reshape(chunk, picked.shape[-1])

    size = dmix_ref.shape[-1]
    part = dmix_ref.shape[2] // heads
    x = x_ref[0].astype(jnp.float32)
    attended = dot_nt(mixed_ref[0], pair_columns(units, units + heads * size))
    hidden = x + attended * inverse_rms(attended) * (1.0 + ga_ref[...])
    pre = (hidden * inverse_rms(hidden) * (1.0 + gp_ref[...])).astype(jnp.bfloat16)
    pre_ref[0] = pre
    down = jnp.zeros(x.shape, jnp.float32)
    root = (2.0 / math.pi) ** 0.5
    for start in range(0, units, chunk):
        span = slice(start, start + chunk)
        gate = dot_nt(pre, gate_up_rows(start, 0))
        up = dot_nt(pre, gate_up_rows(start, 1))
        square = gate * gate
        bend = jnp.tanh(gate * (root + (root * 0.044715) * square))
        half = 0.5 + 0.5 * bend
        act = gate * half
        slope = half + act * (1.0 - bend) * (root + (3.0 * root * 0.044715) * square)
        act_ref[:, span] = act
        slope_ref[:, span] = up * slope
        product = (act * up).astype(jnp.bfloat16)
        product_ref[0, :, span] = product
        down += dot_nt(product, pair_columns(start, start + chunk))
    out_ref[0] = (hidden + down * inverse_rms(down) * (1.0 + gf_ref[...])).astype(jnp.bfloat16)
    dy = cot_ref[0].astype(jnp.float32)
    d_down, dg_ffn = rms_back(down, gf_ref[...], dy)
    d_down = d_down.astype(jnp.bfloat16)
    ddown_ref[0] = d_down
    d_pre = jnp.zeros(x.shape, jnp.float32)
    for start in range(0, units, chunk):
        span = slice(start, start + chunk)
        d_product = dot_nn(d_down, pair_columns(start, start + chunk))
        d_gate = (d_product * slope_ref[:, span]).astype(jnp.bfloat16)
        d_up = (d_product * act_ref[:, span]).astype(jnp.bfloat16)
        dgate_ref[0, :, span] = d_gate
        dup_ref[0, :, span] = d_up
        d_pre += dot_nn(d_gate, gate_up_rows(start, 0)) + dot_nn(
            d_up, gate_up_rows(start, 1)
        )
    d_hidden, dg_pre = rms_back(hidden, gp_ref[...], d_pre)
    d_hidden = dy + d_hidden
    dhid_ref[0] = d_hidden
    d_att, dg_attn = rms_back(attended, ga_ref[...], d_hidden)
    d_att = d_att.astype(jnp.bfloat16)
    datt_ref[0] = d_att
    dg_ref[0] = jnp.concatenate([dg_attn, dg_pre, dg_ffn], axis=0)
    for head in range(heads):
        d_mixed = dot_nn(
            d_att, pair_columns(units + head * size, units + (head + 1) * size)
        ).astype(jnp.bfloat16)
        for t in range(2):
            dmix_ref[0, t, head * part : (head + 1) * part, :] = d_mixed[t * part : (t + 1) * part]


def attend_back_kernel(
    heads, waits, q_ref, qraw_ref, far_ref, near_ref, own_ref, qid_ref, kid_ref, mixed_ref, dmix_ref,
    cos_ref, sin_ref, gq_ref, *refs
):
    dfar_ref, dnear_ref, down_ref, dqraw_ref, dg_ref, win_ref, grad_ref = refs[waits:]
    size = q_ref.shape[-1]
    part = q_ref.shape[2] // heads
    span = part + WINDOW
    far, near = far_ref.shape[1], near_ref.shape[1]
    load_window(far_ref, near_ref, own_ref, win_ref)
    grad_ref[...] = jnp.zeros_like(grad_ref)
    dg = jnp.zeros((1, size), jnp.float32)
    for t in range(2):
        rows = slice(t * part, (t + 1) * part)
        window = slice(t * part, t * part + span)
        bias = mask_bias(qid_ref, kid_ref, t, part, span)
        keys = win_ref[window, :size]
        values = win_ref[window, size:]
        cosine, sine = cos_ref[0, rows, :], sin_ref[0, rows, :]
        for head in range(heads):
            line = slice(head * part, (head + 1) * part)
            lanes = slice(head * size, (head + 1) * size)
            query = q_ref[0, t, line, :]
            d_out = dmix_ref[0, t, line, :]
            weights = jnp.exp(dot_nt(query, keys) + bias)
            weights = weights * (1.0 / jnp.sum(weights, axis=-1, keepdims=True))
            delta = jnp.sum(
                d_out.astype(jnp.float32) * mixed_ref[0, rows, lanes].astype(jnp.float32),
                axis=-1,
                keepdims=True,
            )
            d_scores = (weights * (dot_nt(d_out, values) - delta)).astype(jnp.bfloat16)
            weights = weights.astype(jnp.bfloat16)
            grad_ref[window, :size] += dot_tn(d_scores, query)
            grad_ref[window, size:] += dot_tn(weights, d_out)
            d_query = dot_nn(d_scores, keys) * size ** (-0.5)
            d_raw, part_g = rms_back(
                qraw_ref[0, t, line, :].astype(jnp.float32),
                gq_ref[...],
                turn(d_query, cosine, -sine),
            )
            dqraw_ref[0, rows, lanes] = d_raw.astype(jnp.bfloat16)
            dg += part_g
    dg_ref[0] = dg
    dfar_ref[0] = grad_ref[:far, :].astype(jnp.bfloat16)
    dnear_ref[0] = grad_ref[far : far + near, :]
    down_ref[0] = grad_ref[far + near :, :]


def input_back_kernel(
    waits, own_ref, recv_ref, kraw_ref, cos_ref, sin_ref, wk_ref, wv_ref, dq_ref, wq_ref, x_ref, dhid_ref,
    gi_ref, gk_ref, *refs
):
    grad_ref, dpair_ref, dgi_ref, dgk_ref = refs[waits:]
    size = wk_ref.shape[0]
    total = own_ref[0] + recv_ref[0].astype(jnp.float32)
    d_key = turn(total[:, :size], cos_ref[0], -sin_ref[0])
    d_raw, dg_key = rms_back(kraw_ref[0].astype(jnp.float32), gk_ref[...], d_key)
    d_raw = d_raw.astype(jnp.bfloat16)
    d_value = total[:, size:].astype(jnp.bfloat16)
    dpair_ref[0, :, :size] = d_raw
    dpair_ref[0, :, size:] = d_value
    d_normed = dot_nn(dq_ref[0], wq_ref[...])
    d_normed += dot_nn(d_raw, wk_ref[...]) + dot_nn(d_value, wv_ref[...])
    d_x, dg_input = rms_back(x_ref[0].astype(jnp.float32), gi_ref[...], d_normed)
    grad_ref[0] = dhid_ref[0] + d_x
    dgi_ref[0] = dg_input
    dgk_ref[0] = dg_key


def flips(bit):
    return [(i, i ^ (1 << bit)) for i in range(lax.axis_size("dp"))]


def device_index():
    return lax.axis_index("dp")[None].astype(jnp.int32)


def side(bit):
    return (lax.axis_index("dp") >> bit) & 1


def stack_step(pairs, bits, done, arrived=()):
    axes = [sum(1 for other in before if other > bit) for bit, before in zip(bits, done)]
    anywhere = pl.BlockSpec(memory_space=pl.ANY)
    block = pl.BlockSpec(memory_space=pltpu.VMEM)
    arrived = list(arrived)
    shapes = [
        own.shape[:axis] + (2,) + own.shape[axis:] for (own, _), axis in zip(pairs, axes)
    ]
    return pl.pallas_call(
        functools.partial(stack_kernel, bits, axes, len(arrived)),
        out_shape=[jax.ShapeDtypeStruct(shape, jnp.bfloat16) for shape in shapes],
        in_specs=[pl.BlockSpec(memory_space=pltpu.SMEM)]
        + [block] * (2 * len(pairs))
        + [anywhere] * len(arrived),
        out_specs=[block] * len(pairs),
        compiler_params=pltpu.CompilerParams(vmem_limit_bytes=VMEM_BYTES),
    )(device_index(), *[array for pair in pairs for array in pair], *arrived)


class RowSum:
    def __init__(self, parts, order, axis):
        self.terms = [
            (part.reshape((2,) * len(order) + part.shape[1:]), list(range(len(order) - 1, -1, -1)))
            for part in parts
        ]
        self.join = axis
        self.order = order
        self.chosen = {}
        self.received = []

    @classmethod
    def from_halves(cls, keep, send, order):
        result = cls([], order, -1)
        shape = (2,) * (len(order) - 1) + keep.shape[1:]
        left = list(range(len(order) - 1, 0, -1))
        received = lax.ppermute(send, "dp", flips(0))
        result.terms = [(keep.reshape(shape), left)]
        result.received = [(received.reshape(shape), left)]
        result.chosen = {0: side(0)}
        result.sent = send
        return result

    def total(self, other=None):
        picks = dict(self.chosen)
        if other is not None:
            picks[other] = 1 - side(other)
        pieces = [self.pick(part, bits, picks) for part, bits in self.terms]
        value = jnp.concatenate(pieces, axis=self.join) if len(pieces) > 1 else pieces[0]
        value = value.astype(jnp.float32)
        for part, bits in self.received:
            value += self.pick(part, bits, picks).astype(jnp.float32)
        return value.astype(jnp.bfloat16)

    def ordered_total(self, after, other=None):
        gone = set(self.chosen) | ({other} if other is not None else set())
        left = [b for b in range(len(self.order) - 1, -1, -1) if b not in gone]
        terms = self.terms + self.received
        block = terms[0][0].shape[-2:]
        anywhere = pl.BlockSpec(memory_space=pl.ANY)

        def spec(bits):
            def place(g, index):
                flat = 0
                for bit in bits:
                    if bit in gone:
                        value = (index[0] >> bit) & 1
                        value = 1 - value if bit == other else value
                    else:
                        value = (g >> (len(left) - 1 - left.index(bit))) & 1
                    flat = 2 * flat + value
                return (flat, 0, 0)

            return pl.BlockSpec((1,) + block, place)

        count = 2 ** len(left)
        out = pl.pallas_call(
            functools.partial(sum_kernel, len(terms)),
            out_shape=jax.ShapeDtypeStruct((count,) + block, jnp.bfloat16),
            grid_spec=pltpu.PrefetchScalarGridSpec(
                num_scalar_prefetch=1,
                grid=(count,),
                in_specs=[spec(bits) for _, bits in terms] + [anywhere] * len(after),
                out_specs=pl.BlockSpec((1,) + block, lambda g, index: (g, 0, 0)),
            ),
            compiler_params=kernel_params(),
        )(device_index(), *[part.reshape((-1,) + block) for part, _ in terms], *after)
        return out.reshape((2,) * len(left) + block)

    def ordered_step(self, bit, after):
        self.sent = self.ordered_total(after, bit)
        self.receive(bit)

    def receive(self, bit):
        received = lax.ppermute(self.sent, "dp", flips(bit))
        self.chosen[bit] = side(bit)
        left = [b for b in range(len(self.order) - 1, -1, -1) if b not in self.chosen]
        self.received.append((received, left))
        return received

    def pick(self, part, bits, picks):
        bits = list(bits)
        for bit, where in picks.items():
            if bit in bits:
                part = lax.dynamic_index_in_dim(part, where, bits.index(bit), keepdims=False)
                bits.remove(bit)
        return part

    def send(self, bit):
        self.sent = self.total(bit)
        return self.sent

    def step(self, bit):
        self.send(bit)
        return self.receive(bit)


def seq_sum(part):
    count = lax.axis_size("seq")
    index = lax.axis_index("seq")
    half = count // 2
    terms = [part]

    def total():
        return sum(term.astype(jnp.float32) for term in terms)

    for t in range(half - 1):
        pairs = [(t, t + 1), (count - 1 - t, count - 2 - t)]
        terms.append(lax.ppermute(total().astype(jnp.bfloat16), "seq", pairs))
    middle = [(half - 1, half), (half, half - 1)]
    terms.append(lax.ppermute(total().astype(jnp.bfloat16), "seq", middle))
    result = total()
    for t in range(half - 2, -1, -1):
        pairs = [(t + 1, t), (count - 2 - t, count - 1 - t)]
        received = lax.ppermute(result.astype(jnp.bfloat16), "seq", pairs)
        outer = (index == t) | (index == count - 1 - t)
        result = jnp.where(outer, received.astype(jnp.float32), result)
    return result


def body(
    tokens,
    cotangent,
    segments,
    positions,
    query_weight,
    key_weight,
    value_weight,
    output_weight,
    gate_weight,
    up_weight,
    down_weight,
    norm_gains,
    query_first,
    key_first,
    value_first,
    output_first,
    gate_first,
    up_first,
    down_first,
    gains_first,
    query_second,
    key_second,
    value_second,
    output_second,
    gate_second,
    up_second,
    down_second,
    gains_second,
):
    count = lax.axis_size("dp")
    bits = (count - 1).bit_length()
    order_a = list(range(1, bits)) + [0]
    order_b = list(range(bits - 1, 0, -1)) + [0]
    low = jnp.bfloat16
    f32 = jnp.float32
    width = tokens.shape[2]
    key_rows = key_weight.shape[0]
    gain_rows = norm_gains.shape[0]
    rest_rows = 2 * key_rows + 16

    def array(shape, kind):
        return jax.ShapeDtypeStruct(shape, kind)

    query_rows = query_weight.shape[0]
    first_shard = pl.pallas_call(
        cast_first_kernel,
        out_shape=array((query_rows + rest_rows, width), low),
    )(query_weight, key_weight, value_weight, norm_gains[None])
    block = pl.BlockSpec(memory_space=pltpu.VMEM)
    anywhere = pl.BlockSpec(memory_space=pl.ANY)
    first_received = lax.ppermute(first_shard, "dp", flips(order_b[0]))
    pair_width = down_weight.shape[1] + output_weight.shape[1]
    pair_half_shape = array((down_weight.shape[0], pair_width // 2), low)
    shards_low = pl.pallas_call(
        functools.partial(cast_rest_kernel, 1),
        out_shape=[
            array(gate_weight.shape, low),
            array(up_weight.shape, low),
            pair_half_shape,
            pair_half_shape,
        ],
        in_specs=[block] * 4 + [anywhere],
    )(gate_weight, up_weight, down_weight, output_weight, first_received)
    rest_orders = [order_a, order_b, order_a, order_b]

    def rest_step(blocks, i):
        return [
            lax.ppermute(own, "dp", flips(order[i])) for own, order in zip(blocks, rest_orders)
        ]

    def rest_stack(blocks, received, i, arrived):
        return stack_step(
            list(zip(blocks, received)),
            [order[i] for order in rest_orders],
            [order[:i] for order in rest_orders],
            arrived,
        )

    (first_all,) = stack_step([(first_shard, first_received)], [order_b[0]], [[]])
    for i in range(1, bits):
        first_received = lax.ppermute(first_all, "dp", flips(order_b[i]))
        (first_all,) = stack_step(
            [(first_all, first_received)], [order_b[i]], [order_b[:i]], shards_low[:1]
        )
    first_all = first_all.reshape((count,) + first_shard.shape)
    rest_received = rest_step(shards_low, 0)
    key_start = query_rows + key_rows
    w_query = first_all[:, :query_rows].reshape(-1, width)
    w_key = first_all[:, query_rows:key_start].reshape(-1, width)
    w_value = first_all[:, key_start : key_start + key_rows].reshape(-1, width)
    gains_all = first_all[:, key_start + key_rows, :gain_rows].reshape(-1)
    seqs, rows, _ = tokens.shape
    size = w_key.shape[0]
    heads = w_query.shape[0] // size
    units = down_weight.shape[1]
    shards = lax.axis_size("seq")
    far = WINDOW - rows
    part = rows // 2
    span = part + WINDOW
    gains_float = gains_all.astype(jnp.float32)[None]
    g_input, g_attn, g_pre, g_ffn = (
        gains_float[:, i * width : (i + 1) * width] for i in range(4)
    )
    g_query = gains_float[:, 4 * width : 4 * width + size]
    g_key = gains_float[:, 4 * width + size : 4 * width + 2 * size]
    angles = positions.astype(jnp.float32)[..., None] * frequencies(size)
    cosine, sine = jnp.cos(angles), jnp.sin(angles)
    core_side = side(0)[None].astype(jnp.int32)
    first_row = lax.axis_index("seq") * rows
    padded = jnp.concatenate([jnp.full((seqs, WINDOW), -1, jnp.int32), segments], axis=1)
    window_ids = lax.dynamic_slice_in_dim(padded, first_row, WINDOW + rows, 1)
    query_ids = window_ids[:, WINDOW:, None]
    key_ids = jnp.stack([window_ids[:, :span], window_ids[:, part:]], axis=1)[:, :, None, :]

    def call(kernel, outs, out_specs, in_specs, scratch, flops, moved):
        return pl.pallas_call(
            kernel,
            grid=(seqs,),
            out_shape=outs,
            in_specs=in_specs,
            out_specs=out_specs,
            scratch_shapes=scratch,
            compiler_params=kernel_params(),
            cost_estimate=pl.CostEstimate(flops=flops, bytes_accessed=moved, transcendentals=0),
        )

    tokens_all = seqs * rows
    head_block = per_seq(2, heads * part, size)
    q_shape = (seqs, 2, heads * part, size)
    normed, pair_own, key_raw = call(
        functools.partial(project_pair_kernel, 6),
        [
            array((seqs, rows, width), low),
            array((seqs, rows, 2 * size), low),
            array((seqs, rows, size), low),
        ],
        [per_seq(rows, width), per_seq(rows, 2 * size), per_seq(rows, size)],
        [
            per_seq(rows, width),
            per_seq(rows, size // 2),
            per_seq(rows, size // 2),
            whole(*w_key.shape),
            whole(*w_value.shape),
            whole(1, width),
            whole(1, size),
        ]
        + [anywhere] * 6,
        [],
        4 * tokens_all * width * size,
        6_000_000,
    )(
        tokens, cosine, sine, w_key, w_value, g_input, g_key, query_ids, key_ids, *rest_received
    )
    upward = [(i, i + 1) for i in range(shards - 1)]
    pair_near = lax.ppermute(pair_own, "seq", upward)
    rest_blocks = rest_stack(shards_low, rest_received, 0, [pair_own])
    query, query_raw = call(
        functools.partial(project_query_kernel, heads, 1),
        [array(q_shape, low), array(q_shape, low)],
        [head_block, head_block],
        [
            per_seq(rows, width),
            per_seq(rows, size // 2),
            per_seq(rows, size // 2),
            whole(*w_query.shape),
            whole(1, size),
            anywhere,
        ],
        [],
        2 * tokens_all * width * heads * size,
        8_000_000,
    )(normed, cosine, sine, w_query, g_query, rest_blocks[0])

    far_send = pl.pallas_call(
        functools.partial(tail_rows_kernel, 1),
        out_shape=array((seqs, far, 2 * size), low),
        in_specs=[block, anywhere],
        out_specs=block,
        compiler_params=pltpu.CompilerParams(vmem_limit_bytes=VMEM_BYTES),
    )(pair_near, query)
    pair_far = lax.ppermute(far_send, "seq", upward[1:])
    for i in range(1, bits - 1):
        rest_blocks = rest_stack(rest_blocks, rest_step(rest_blocks, i), i, [pair_far])
    rest_blocks = [
        blocks.reshape((count // 2,) + blocks.shape[-2:]) for blocks in rest_blocks
    ]
    rest_received = [lax.ppermute(blocks, "dp", flips(0)) for blocks in rest_blocks]
    rest_operands = [array for pair in zip(rest_blocks, rest_received) for array in pair]

    window_specs = [
        per_seq(far, 2 * size),
        per_seq(rows, 2 * size),
        per_seq(rows, 2 * size),
        per_seq(rows, 1),
        per_seq(2, 1, span),
    ]
    attend_flops = 8 * tokens_all * heads * span * size
    mixed = call(
        functools.partial(attend_kernel, heads),
        array((seqs, rows, heads * size), low),
        per_seq(rows, heads * size),
        [head_block] + window_specs,
        [pltpu.VMEM((WINDOW + rows, 2 * size), low)],
        attend_flops,
        16_000_000,
    )(query, pair_far, pair_near, pair_own, query_ids, key_ids)

    (
        layer_output,
        pre_low,
        product_low,
        grad_down_low,
        grad_gate_low,
        grad_up_low,
        grad_attended_low,
        grad_hidden,
        grad_mixed,
        grad_gains_middle,
    ) = call(
        functools.partial(middle_kernel, heads, 512),
        [
            array((seqs, rows, width), low),
            array((seqs, rows, width), low),
            array((seqs, rows, units), low),
            array((seqs, rows, width), low),
            array((seqs, rows, units), low),
            array((seqs, rows, units), low),
            array((seqs, rows, width), low),
            array((seqs, rows, width), f32),
            array(q_shape, low),
            array((seqs, 3, width), f32),
        ],
        [
            per_seq(rows, width),
            per_seq(rows, width),
            per_seq(rows, units),
            per_seq(rows, width),
            per_seq(rows, units),
            per_seq(rows, units),
            per_seq(rows, width),
            per_seq(rows, width),
            head_block,
            per_seq(3, width),
        ],
        [
            pl.BlockSpec(memory_space=pltpu.SMEM),
            per_seq(rows, heads * size),
            per_seq(rows, width),
            per_seq(rows, width),
            anywhere,
            anywhere,
            anywhere,
            anywhere,
            anywhere,
            anywhere,
            anywhere,
            anywhere,
            whole(1, width),
            whole(1, width),
            whole(1, width),
        ],
        [
            pltpu.VMEM((rows, units), f32),
            pltpu.VMEM((rows, units), f32),
            pltpu.VMEM((count // 2, 2, 2 * gate_weight.shape[0], width), low),
            pltpu.VMEM((count // 2, 2, down_weight.shape[0], pair_width), low),
            pltpu.SemaphoreType.DMA((8,)),
        ],
        4 * tokens_all * width * (heads * size + 3 * units),
        40_000_000,
    )(
        core_side, mixed, tokens, cotangent, *rest_operands, g_attn, g_pre, g_ffn,
    )

    def flat(values):
        return values.reshape(tokens_all, values.shape[-1])

    def grad_blocks(gradient, inputs):
        product = weight_grad(flat(gradient), flat(inputs)).astype(low)
        return product.reshape(count, -1, product.shape[1])

    back_a = [0] + order_a[:-1]
    back_b = [0] + order_b[:-1]
    shard_units = gate_weight.shape[0]
    shard_rows = down_weight.shape[0]
    half = count // 2
    direct = shard_units % 128 == 0 and shard_rows % 16 == 0
    if direct:
        columns = 512
        first = units // columns
        last = heads * size // columns
        pair_block = pl.BlockSpec((half, shard_rows, columns), lambda k, side: (0, 0, k))
        pair_shape = array((half, shard_rows, units + heads * size), low)
        fixed = pl.BlockSpec(
            (tokens_all, width), lambda k, side: (0, 0), pipeline_mode=pl.Buffered(1)
        )
        pair_send, pair_keep = pl.pallas_call(
            functools.partial(pair_grad_kernel, first),
            out_shape=[pair_shape, pair_shape],
            grid_spec=pltpu.PrefetchScalarGridSpec(
                num_scalar_prefetch=1,
                grid=(first + last,),
                in_specs=[
                    pl.BlockSpec(
                        (tokens_all, columns), lambda k, side: (0, jnp.minimum(k, first - 1))
                    ),
                    pl.BlockSpec(
                        (tokens_all, columns), lambda k, side: (0, jnp.maximum(k - first, 0))
                    ),
                    fixed,
                    fixed,
                ],
                out_specs=[pair_block, pair_block],
                scratch_shapes=[
                    pltpu.VMEM((width, tokens_all), low),
                    pltpu.VMEM((width, columns), f32),
                ],
            ),
            compiler_params=kernel_params(),
            cost_estimate=pl.CostEstimate(
                flops=2 * tokens_all * width * (units + heads * size),
                bytes_accessed=13_000_000,
                transcendentals=0,
            ),
        )(core_side, flat(product_low), flat(mixed), flat(grad_down_low), flat(grad_attended_low))
        down_out_sum = RowSum.from_halves(pair_keep, pair_send, back_b)

        def shard_of(g, side):
            return (0, 2 * (g % half) + jnp.where(g < half, 1 - side[0], side[0]))

        block_shape = (1, 2 * shard_units, width)
        half_shape = array((half, 2 * shard_units, width), low)
        gate_up_send, gate_up_keep = pl.pallas_call(
            gate_up_grad_kernel,
            out_shape=[half_shape, half_shape],
            grid_spec=pltpu.PrefetchScalarGridSpec(
                num_scalar_prefetch=1,
                grid=(count,),
                in_specs=[
                    pl.BlockSpec((tokens_all, shard_units), shard_of),
                    pl.BlockSpec((tokens_all, shard_units), shard_of),
                    fixed,
                    anywhere,
                ],
                out_specs=[
                    pl.BlockSpec(block_shape, lambda g, side: (jnp.minimum(g, half - 1), 0, 0)),
                    pl.BlockSpec(block_shape, lambda g, side: (jnp.maximum(g - half, 0), 0, 0)),
                ],
            ),
            compiler_params=kernel_params(),
            cost_estimate=pl.CostEstimate(
                flops=4 * tokens_all * width * units, bytes_accessed=14_000_000, transcendentals=0
            ),
        )(core_side, flat(grad_gate_low), flat(grad_up_low), flat(pre_low), pair_send)
        gate_up_sum = RowSum.from_halves(gate_up_keep, gate_up_send, back_a)
    else:
        pair_blocks = jnp.concatenate(
            [grad_blocks(grad_down_low, product_low), grad_blocks(grad_attended_low, mixed)], axis=-1
        )
        down_out_sum = RowSum([pair_blocks], back_b, -1)
        down_out_sum.step(0)
        gate_up_blocks = jnp.concatenate(
            [grad_blocks(grad_gate_low, pre_low), grad_blocks(grad_up_low, pre_low)], axis=-2
        )
        gate_up_sum = RowSum([gate_up_blocks], back_a, -2)
        gate_up_sum.step(0)

    def at_seq(s, *tail):
        return pl.BlockSpec((1,) + tail, lambda g: (s,) + (0,) * len(tail))

    def seq_call(kernel, outs, out_specs, in_specs, operands, scratch, alias, flops):
        return pl.pallas_call(
            kernel,
            grid=(1,),
            out_shape=outs,
            in_specs=in_specs,
            out_specs=out_specs,
            scratch_shapes=scratch,
            input_output_aliases=alias,
            compiler_params=kernel_params(),
            cost_estimate=pl.CostEstimate(
                flops=flops, bytes_accessed=8_000_000, transcendentals=0
            ),
        )(*operands)

    def attend_back(s, buffer, arrived):
        kinds = [
            array((1, far, 2 * size), low),
            array((1, rows, 2 * size), f32),
            array((1, rows, 2 * size), f32),
            array((seqs, rows, heads * size), low),
            array((1, 1, size), f32),
        ]
        specs = [
            at_seq(0, far, 2 * size),
            at_seq(0, rows, 2 * size),
            at_seq(0, rows, 2 * size),
            at_seq(s, rows, heads * size),
            at_seq(0, 1, size),
        ]
        in_specs = [
            at_seq(s, 2, heads * part, size),
            at_seq(s, 2, heads * part, size),
            at_seq(s, far, 2 * size),
            at_seq(s, rows, 2 * size),
            at_seq(s, rows, 2 * size),
            at_seq(s, rows, 1),
            at_seq(s, 2, 1, span),
            at_seq(s, rows, heads * size),
            at_seq(s, 2, heads * part, size),
            at_seq(s, rows, size // 2),
            at_seq(s, rows, size // 2),
            whole(1, size),
        ]
        operands = [
            query, query_raw, pair_far, pair_near, pair_own, query_ids, key_ids, mixed, grad_mixed,
            cosine, sine, g_query,
        ]
        alias = {}
        extra = list(arrived)
        if buffer is not None:
            alias = {len(operands): 3}
            extra = [buffer] + extra
        return seq_call(
            functools.partial(attend_back_kernel, heads, len(extra)),
            kinds,
            specs,
            in_specs + [anywhere] * len(extra),
            operands + extra,
            [
                pltpu.VMEM((WINDOW + rows, 2 * size), low),
                pltpu.VMEM((WINDOW + rows, 2 * size), f32),
            ],
            alias,
            attend_flops * 3 // seqs,
        )

    downward = [(i + 1, i) for i in range(shards - 1)]
    grad_query_low = None
    arrived = [gate_up_sum.sent]

    def near_total(grad_near, from_far, after):
        return pl.pallas_call(
            functools.partial(near_sum_kernel, len(after)),
            out_shape=array(grad_near.shape, low),
            in_specs=[block] * 2 + [anywhere] * len(after),
            out_specs=block,
        )(grad_near, from_far, *after)

    own_parts, query_gains, near_sums, far_parts, near_parts = [], [], [], [], []
    for s in range(seqs):
        grad_far, grad_near, grad_own, grad_query_low, g_part = attend_back(
            s, grad_query_low, arrived
        )
        from_far = lax.ppermute(grad_far, "seq", downward[1:])
        own_parts.append(grad_own)
        query_gains.append(g_part)
        far_parts.append(from_far)
        near_parts.append(grad_near)
        if s == 0:
            down_out_sum.ordered_step(back_b[1], [grad_own])
            gate_up_sum.ordered_step(back_a[1], [down_out_sum.sent])
            arrived = [gate_up_sum.sent]
        elif s == 1:
            near_sums.append(near_total(near_parts[0], far_parts[0], [grad_own]))
            arrived = [near_sums[0]]
    for bit in back_b[2:]:
        down_out_sum.ordered_step(bit, [own_parts[-1]])
    near_sums.append(near_total(near_parts[1], far_parts[1], [down_out_sum.sent]))
    query_columns = heads * size
    grad_w_query = pl.pallas_call(
        functools.partial(query_grad_kernel, 2),
        grid=(heads,),
        out_shape=array((query_columns, width), low),
        in_specs=[
            pl.BlockSpec((tokens_all, size), lambda i: (0, i)),
            whole(tokens_all, width),
            anywhere,
            anywhere,
        ],
        out_specs=pl.BlockSpec((size, width), lambda i: (i, 0)),
        compiler_params=kernel_params(),
        cost_estimate=pl.CostEstimate(
            flops=2 * tokens_all * width * query_columns, bytes_accessed=5_000_000, transcendentals=0
        ),
    )(flat(grad_query_low), flat(normed), near_sums[1], down_out_sum.sent)
    near_sums.append(near_total(near_parts[2], far_parts[2], [grad_w_query]))
    from_near = [lax.ppermute(near_sum, "seq", downward) for near_sum in near_sums]
    for bit in back_a[2:]:
        gate_up_sum.ordered_step(bit, [near_sums[2]])

    def input_back(s, buffers, arrived):
        kinds = [
            array((seqs, rows, width), f32),
            array((seqs, rows, 2 * size), low),
            array((1, 1, width), f32),
            array((1, 1, size), f32),
        ]
        specs = [
            at_seq(s, rows, width),
            at_seq(s, rows, 2 * size),
            at_seq(0, 1, width),
            at_seq(0, 1, size),
        ]
        in_specs = [
            at_seq(0, rows, 2 * size),
            at_seq(0, rows, 2 * size),
            at_seq(s, rows, size),
            at_seq(s, rows, size // 2),
            at_seq(s, rows, size // 2),
            whole(*w_key.shape),
            whole(*w_value.shape),
            at_seq(s, rows, heads * size),
            whole(*w_query.shape),
            at_seq(s, rows, width),
            at_seq(s, rows, width),
            whole(1, width),
            whole(1, size),
        ]
        operands = [
            own_parts[s], from_near[s], key_raw, cosine, sine, w_key, w_value, grad_query_low,
            w_query, tokens, grad_hidden, g_input, g_key,
        ]
        alias = {}
        extra = list(arrived)
        if buffers:
            alias = {len(operands): 0, len(operands) + 1: 1}
            extra = list(buffers) + extra
        return seq_call(
            functools.partial(input_back_kernel, len(extra)),
            kinds,
            specs,
            in_specs + [anywhere] * len(extra),
            operands + extra,
            [],
            alias,
            2 * rows * width * size * (heads + 2),
        )

    buffers = []
    input_gains, key_gains = [], []
    for s in range(seqs):
        waits = [gate_up_sum.sent]
        if s == seqs - 1:
            down_out_part = down_out_sum.ordered_total([buffers[0]])
            waits = [down_out_part]
        *buffers, g_part, g_key_part = input_back(s, buffers, waits)
        input_gains.append(g_part)
        key_gains.append(g_key_part)
    input_grad, grad_pair_low = buffers
    key_value_blocks = grad_blocks(grad_pair_low, normed).reshape(2, count, key_rows, width)
    grad_gains = jnp.concatenate(
        [
            sum(input_gains).reshape(-1),
            jnp.sum(grad_gains_middle, axis=0).reshape(-1),
            sum(query_gains).reshape(-1),
            sum(key_gains).reshape(-1),
        ]
    )
    gain_block = jnp.pad(
        grad_gains.astype(low).reshape(count, 1, gain_rows),
        ((0, 0), (0, 15), (0, width - gain_rows)),
    )
    rest_sum = RowSum(
        [
            grad_w_query.reshape(count, query_rows, width),
            key_value_blocks[0],
            key_value_blocks[1],
            gain_block,
        ],
        back_b,
        -2,
    )
    rest_sum.step(back_b[0])
    gate_up_part = gate_up_sum.ordered_total([rest_sum.sent])
    for bit in back_b[1:]:
        rest_sum.step(bit)
    down_out_total = seq_sum(down_out_part)
    gate_total = seq_sum(gate_up_part[:shard_units])
    up_total = seq_sum(gate_up_part[shard_units:])
    rest_total = seq_sum(rest_sum.total())
    query_total = rest_total[:query_rows]
    rest_total = rest_total[query_rows:]
    down_total = down_out_total[:, :units]
    output_total = down_out_total[:, units:]
    key_total = rest_total[:key_rows]
    value_total = rest_total[key_rows : 2 * key_rows]
    gains_total = rest_total[2 * key_rows, :gain_rows]
    query_momentum, query_variance, query_updated = adam_step(
        query_weight, query_first, query_second, query_total, WEIGHT_DECAY
    )
    key_momentum, key_variance, key_updated = adam_step(
        key_weight, key_first, key_second, key_total, WEIGHT_DECAY
    )
    value_momentum, value_variance, value_updated = adam_step(
        value_weight, value_first, value_second, value_total, WEIGHT_DECAY
    )
    output_momentum, output_variance, output_updated = adam_step(
        output_weight, output_first, output_second, output_total, WEIGHT_DECAY
    )
    gate_momentum, gate_variance, gate_updated = adam_step(
        gate_weight, gate_first, gate_second, gate_total, WEIGHT_DECAY
    )
    up_momentum, up_variance, up_updated = adam_step(
        up_weight, up_first, up_second, up_total, WEIGHT_DECAY
    )
    down_momentum, down_variance, down_updated = adam_step(
        down_weight, down_first, down_second, down_total, WEIGHT_DECAY
    )
    gains_momentum, gains_variance, gains_updated = adam_step(
        norm_gains, gains_first, gains_second, gains_total, 0.0
    )
    return (
        layer_output,
        input_grad,
        query_momentum,
        key_momentum,
        value_momentum,
        output_momentum,
        gate_momentum,
        up_momentum,
        down_momentum,
        gains_momentum,
        query_variance,
        key_variance,
        value_variance,
        output_variance,
        gate_variance,
        up_variance,
        down_variance,
        gains_variance,
        query_updated,
        key_updated,
        value_updated,
        output_updated,
        gate_updated,
        up_updated,
        down_updated,
        gains_updated,
    )


def solution(mesh):
    return jax.shard_map(
        body,
        mesh=mesh,
        in_specs=(
            P("dp", "seq", None),
            P("dp", "seq", None),
            P("dp", None),
            P("dp", "seq"),
            P("dp", None),
            P("dp", None),
            P("dp", None),
            P("dp", None),
            P("dp", None),
            P("dp", None),
            P("dp", None),
            P("dp"),
            P("dp", None),
            P("dp", None),
            P("dp", None),
            P("dp", None),
            P("dp", None),
            P("dp", None),
            P("dp", None),
            P("dp"),
            P("dp", None),
            P("dp", None),
            P("dp", None),
            P("dp", None),
            P("dp", None),
            P("dp", None),
            P("dp", None),
            P("dp"),
        ),
        out_specs=(
            P("dp", "seq", None),
            P("dp", "seq", None),
            P("dp", None),
            P("dp", None),
            P("dp", None),
            P("dp", None),
            P("dp", None),
            P("dp", None),
            P("dp", None),
            P("dp"),
            P("dp", None),
            P("dp", None),
            P("dp", None),
            P("dp", None),
            P("dp", None),
            P("dp", None),
            P("dp", None),
            P("dp"),
            P("dp", None),
            P("dp", None),
            P("dp", None),
            P("dp", None),
            P("dp", None),
            P("dp", None),
            P("dp", None),
            P("dp"),
        ),
        check_vma=False,
    )
```

```python
import functools
import math

import jax
import jax.numpy as jnp
from jax import lax
from jax.experimental import pallas as pl
from jax.experimental.pallas import tpu as pltpu
from jax.sharding import PartitionSpec as P

WINDOW = 512
STEP = 10


NORM_EPSILON = 1e-06
ROPE_BASE = 10000.0
LEARN_RATE = 0.08
BETA_FIRST = 0.9
BETA_SECOND = 0.95
ADAM_EPSILON = 1e-08
WEIGHT_DECAY = 0.01
MASKED_SCORE = -1000000000.0


def frequencies(size):
    return ROPE_BASE ** (-2.0 * jnp.arange(size // 2).astype(jnp.float32) / size)


def weight_grad(gradients, inputs):
    return lax.dot_general(
        gradients, inputs, (((0,), (0,)), ((), ())), preferred_element_type=jnp.float32
    )


def adam_step(weight, first_moment, second_moment, gradient, decay_rate):
    momentum = BETA_FIRST * first_moment + (1.0 - BETA_FIRST) * gradient
    variance = BETA_SECOND * second_moment + (1.0 - BETA_SECOND) * gradient * gradient
    corrected = momentum / (1.0 - BETA_FIRST**STEP)
    scaled = variance / (1.0 - BETA_SECOND**STEP)
    updated = weight - LEARN_RATE * (
        corrected / (jnp.sqrt(scaled) + ADAM_EPSILON) + decay_rate * weight
    )
    return (momentum, variance, updated)


VMEM_BYTES = 56 * 1024 * 1024


def kernel_params():
    return pltpu.CompilerParams(
        dimension_semantics=("arbitrary",), vmem_limit_bytes=VMEM_BYTES
    )


def per_seq(*tail):
    return pl.BlockSpec((1,) + tail, lambda s: (s,) + (0,) * len(tail))


def whole(*shape):
    return pl.BlockSpec(shape, lambda s: (0,) * len(shape), pipeline_mode=pl.Buffered(1))


def dot_nt(a, b):
    return lax.dot_general(a, b, (((1,), (1,)), ((), ())), preferred_element_type=jnp.float32)


def dot_nn(a, b):
    return lax.dot_general(a, b, (((1,), (0,)), ((), ())), preferred_element_type=jnp.float32)


def dot_tn(a, b):
    return lax.dot_general(a, b, (((0,), (0,)), ((), ())), preferred_element_type=jnp.float32)


def inverse_rms(values):
    return lax.rsqrt(jnp.mean(values * values, axis=-1, keepdims=True) + NORM_EPSILON)


def rms_back(values, gain, grad):
    inverse = inverse_rms(values)
    unit = values * inverse
    scaled = grad * (1.0 + gain)
    return (
        inverse * (scaled - unit * jnp.mean(unit * scaled, axis=-1, keepdims=True)),
        jnp.sum(grad * unit, axis=0, keepdims=True),
    )


def turn(values, cosine, sine):
    half = values.shape[-1] // 2
    first, second = values[:, :half], values[:, half:]
    return jnp.concatenate(
        [first * cosine - second * sine, second * cosine + first * sine], axis=-1
    )


def stack_heads(values, heads):
    return jnp.concatenate([values] * heads, axis=0)


def cast_first_kernel(wq_ref, wk_ref, wv_ref, gain_ref, out_ref):
    width = wq_ref.shape[1]
    gains = gain_ref[...]
    tail = width - gains.shape[1]
    block = jnp.broadcast_to(gains, (16, gains.shape[1]))
    if tail:
        block = jnp.concatenate([block, jnp.zeros((16, tail), jnp.float32)], axis=1)
    parts = [wq_ref[...], wk_ref[...], wv_ref[...], block]
    out_ref[...] = jnp.concatenate(parts, axis=0).astype(jnp.bfloat16)


def cast_rest_kernel(waits, wg_ref, wu_ref, wd_ref, wo_ref, *refs):
    gate_ref, up_ref, first_ref, second_ref = refs[waits:]
    cut = first_ref.shape[1]
    rest = wd_ref.shape[1] - cut
    gate_ref[...] = wg_ref[...].astype(jnp.bfloat16)
    up_ref[...] = wu_ref[...].astype(jnp.bfloat16)
    first_ref[...] = wd_ref[:, :cut].astype(jnp.bfloat16)
    second_ref[:, :rest] = wd_ref[:, cut:].astype(jnp.bfloat16)
    second_ref[:, rest:] = wo_ref[...].astype(jnp.bfloat16)


def stack_kernel(bits, axes, waits, index_ref, *refs):
    count = len(bits)
    outs = refs[2 * count + waits :]
    for i in range(count):
        upper = (index_ref[0] >> bits[i]) & 1
        lead = (slice(None),) * axes[i]
        outs[i][lead + (upper,)] = refs[2 * i][...]
        outs[i][lead + (1 - upper,)] = refs[2 * i + 1][...]


def tail_rows_kernel(waits, near_ref, *refs):
    out_ref = refs[waits]
    out_ref[...] = near_ref[:, near_ref.shape[1] - out_ref.shape[1] :]


def near_sum_kernel(waits, near_ref, far_ref, *refs):
    out_ref = refs[waits]
    keep = near_ref.shape[1] - far_ref.shape[1]
    out_ref[0, :keep] = near_ref[0, :keep].astype(jnp.bfloat16)
    total = near_ref[0, keep:] + far_ref[0].astype(jnp.float32)
    out_ref[0, keep:] = total.astype(jnp.bfloat16)


def sum_kernel(count, index_ref, *refs):
    total = refs[0][0].astype(jnp.float32)
    for ref in refs[1:count]:
        total += ref[0].astype(jnp.float32)
    refs[-1][0] = total.astype(jnp.bfloat16)


def gate_up_grad_kernel(side_ref, dgate_ref, dup_ref, pre_ref, after_ref, send_ref, keep_ref):
    step = pl.program_id(0)
    half = pl.num_programs(0) // 2
    rows = dgate_ref.shape[1]

    gate = dot_tn(dgate_ref[...], pre_ref[...]).astype(jnp.bfloat16)
    up = dot_tn(dup_ref[...], pre_ref[...]).astype(jnp.bfloat16)

    @pl.when(step < half)
    def _():
        send_ref[0, :rows, :] = gate
        send_ref[0, rows:, :] = up

    @pl.when(step >= half)
    def _():
        keep_ref[0, :rows, :] = gate
        keep_ref[0, rows:, :] = up


def pair_grad_kernel(
    first, side_ref, product_ref, mixed_ref, ddown_ref, datt_ref, send_ref, keep_ref, turned_ref, total_ref
):
    step = pl.program_id(0)
    upper = side_ref[0]
    half, rows = send_ref.shape[0], send_ref.shape[1]

    @pl.when(step == 0)
    def _():
        turned_ref[...] = ddown_ref[...].T

    @pl.when(step == first)
    def _():
        turned_ref[...] = datt_ref[...].T

    @pl.when(step < first)
    def _():
        total_ref[...] = dot_nn(turned_ref[...], product_ref[...])

    @pl.when(step >= first)
    def _():
        total_ref[...] = dot_nn(turned_ref[...], mixed_ref[...])

    for i in range(half):
        mine = pl.multiple_of((2 * i + upper) * rows, rows)
        other = pl.multiple_of((2 * i + 1 - upper) * rows, rows)
        keep_ref[i] = total_ref[pl.ds(mine, rows), :].astype(jnp.bfloat16)
        send_ref[i] = total_ref[pl.ds(other, rows), :].astype(jnp.bfloat16)


def query_grad_kernel(waits, dq_ref, normed_ref, *refs):
    refs[waits][...] = dot_tn(dq_ref[...], normed_ref[...]).astype(jnp.bfloat16)


def project_pair_kernel(
    waits, x_ref, cos_ref, sin_ref, wk_ref, wv_ref, gi_ref, gk_ref, *refs
):
    normed_ref, kv_ref, kraw_ref = refs[waits:]
    x = x_ref[0].astype(jnp.float32)
    size = wk_ref.shape[0]
    normed = (x * inverse_rms(x) * (1.0 + gi_ref[...])).astype(jnp.bfloat16)
    normed_ref[0] = normed
    k_raw = dot_nt(normed, wk_ref[...])
    kraw_ref[0] = k_raw.astype(jnp.bfloat16)
    key = turn(k_raw * inverse_rms(k_raw) * (1.0 + gk_ref[...]), cos_ref[0], sin_ref[0])
    kv_ref[0, :, :size] = key.astype(jnp.bfloat16)
    kv_ref[0, :, size:] = dot_nt(normed, wv_ref[...]).astype(jnp.bfloat16)


def project_query_kernel(
    heads, waits, normed_ref, cos_ref, sin_ref, wq_ref, gq_ref, *refs
):
    q_ref, qraw_ref = refs[waits:]
    size = gq_ref.shape[-1]
    part = normed_ref.shape[1] // 2
    normed = normed_ref[0]
    cosine, sine = cos_ref[0], sin_ref[0]
    for head in range(heads):
        raw = dot_nt(normed, wq_ref[head * size : (head + 1) * size, :])
        query = turn(raw * inverse_rms(raw) * (1.0 + gq_ref[...]), cosine, sine)
        query = (query * size ** (-0.5)).astype(jnp.bfloat16)
        raw = raw.astype(jnp.bfloat16)
        for t in range(2):
            span = slice(head * part, (head + 1) * part)
            q_ref[0, t, span, :] = query[t * part : (t + 1) * part]
            qraw_ref[0, t, span, :] = raw[t * part : (t + 1) * part]


def load_window(far_ref, near_ref, own_ref, win_ref):
    far, near = far_ref.shape[1], near_ref.shape[1]
    win_ref[:far, :] = far_ref[0]
    win_ref[far : far + near, :] = near_ref[0]
    win_ref[far + near :, :] = own_ref[0]


def mask_bias(qid_ref, kid_ref, t, part, span):
    ids = qid_ref[0, t * part : (t + 1) * part, :] == kid_ref[0, t]
    row = lax.broadcasted_iota(jnp.int32, (part, span), 0)
    column = lax.broadcasted_iota(jnp.int32, (part, span), 1)
    ok = ids & (column > row) & (column <= row + WINDOW)
    return jnp.where(ok, 0.0, MASKED_SCORE)


def attend_kernel(heads, q_ref, far_ref, near_ref, own_ref, qid_ref, kid_ref, mixed_ref, win_ref):
    size = q_ref.shape[-1]
    part = q_ref.shape[2] // heads
    span = part + WINDOW
    load_window(far_ref, near_ref, own_ref, win_ref)
    for t in range(2):
        bias = mask_bias(qid_ref, kid_ref, t, part, span)
        keys = win_ref[t * part : t * part + span, :size]
        values = win_ref[t * part : t * part + span, size:]
        for head in range(heads):
            scores = dot_nt(q_ref[0, t, head * part : (head + 1) * part, :], keys)
            weights = jnp.exp(scores + bias)
            total = jnp.sum(weights, axis=-1, keepdims=True)
            mixed = dot_nn(weights.astype(jnp.bfloat16), values) / total
            mixed_ref[0, t * part : (t + 1) * part, head * size : (head + 1) * size] = (
                mixed.astype(jnp.bfloat16)
            )


def middle_kernel(
    heads, chunk, side_ref, mixed_ref, x_ref, cot_ref, gate_own_ref, gate_got_ref, up_own_ref, up_got_ref,
    first_own_ref, first_got_ref, second_own_ref, second_got_ref, ga_ref, gp_ref, gf_ref,
    out_ref, pre_ref, product_ref, ddown_ref, dgate_ref, dup_ref, datt_ref, dhid_ref, dmix_ref, dg_ref,
    act_ref, slope_ref, wgu_ref, wdo_blocks_ref, sems,
):
    @pl.when(pl.program_id(0) == 0)
    def _():
        upper = side_ref[0]
        copies = []
        shard = gate_own_ref.shape[1]
        cut = first_own_ref.shape[2]
        places = [
            (slice(None, cut), first_own_ref, first_got_ref),
            (slice(cut, None), second_own_ref, second_got_ref),
        ]
        for lanes, own, got in places:
            for place, source in ((upper, own), (1 - upper, got)):
                target = wdo_blocks_ref.at[:, place, :, lanes]
                copies.append(pltpu.make_async_copy(source, target, sems.at[len(copies)]))
        places = [
            (slice(None, shard), gate_own_ref, gate_got_ref),
            (slice(shard, None), up_own_ref, up_got_ref),
        ]
        for lines, own, got in places:
            for place, source in ((upper, own), (1 - upper, got)):
                target = wgu_ref.at[:, place, lines, :]
                copies.append(pltpu.make_async_copy(source, target, sems.at[len(copies)]))
        for copy in copies:
            copy.start()
        for copy in copies:
            copy.wait()

    def pair_columns(start, stop):
        picked = wdo_blocks_ref[:, :, :, start:stop]
        return picked.reshape(-1, stop - start)

    shard = wgu_ref.shape[2] // 2
    units = 2 * wgu_ref.shape[0] * shard
    group = chunk // shard

    def gate_up_rows(start, which):
        first = start // shard // 2
        picked = wgu_ref[first : first + group // 2, :, which * shard : (which + 1) * shard, :]
        return picked.reshape(chunk, picked.shape[-1])

    size = dmix_ref.shape[-1]
    part = dmix_ref.shape[2] // heads
    x = x_ref[0].astype(jnp.float32)
    attended = dot_nt(mixed_ref[0], pair_columns(units, units + heads * size))
    hidden = x + attended * inverse_rms(attended) * (1.0 + ga_ref[...])
    pre = (hidden * inverse_rms(hidden) * (1.0 + gp_ref[...])).astype(jnp.bfloat16)
    pre_ref[0] = pre
    down = jnp.zeros(x.shape, jnp.float32)
    root = (2.0 / math.pi) ** 0.5
    for start in range(0, units, chunk):
        span = slice(start, start + chunk)
        gate = dot_nt(pre, gate_up_rows(start, 0))
        up = dot_nt(pre, gate_up_rows(start, 1))
        square = gate * gate
        bend = jnp.tanh(gate * (root + (root * 0.044715) * square))
        half = 0.5 + 0.5 * bend
        act = gate * half
        slope = half + act * (1.0 - bend) * (root + (3.0 * root * 0.044715) * square)
        act_ref[:, span] = act
        slope_ref[:, span] = up * slope
        product = (act * up).astype(jnp.bfloat16)
        product_ref[0, :, span] = product
        down += dot_nt(product, pair_columns(start, start + chunk))
    out_ref[0] = (hidden + down * inverse_rms(down) * (1.0 + gf_ref[...])).astype(jnp.bfloat16)
    dy = cot_ref[0].astype(jnp.float32)
    d_down, dg_ffn = rms_back(down, gf_ref[...], dy)
    d_down = d_down.astype(jnp.bfloat16)
    ddown_ref[0] = d_down
    d_pre = jnp.zeros(x.shape, jnp.float32)
    for start in range(0, units, chunk):
        span = slice(start, start + chunk)
        d_product = dot_nn(d_down, pair_columns(start, start + chunk))
        d_gate = (d_product * slope_ref[:, span]).astype(jnp.bfloat16)
        d_up = (d_product * act_ref[:, span]).astype(jnp.bfloat16)
        dgate_ref[0, :, span] = d_gate
        dup_ref[0, :, span] = d_up
        d_pre += dot_nn(d_gate, gate_up_rows(start, 0)) + dot_nn(
            d_up, gate_up_rows(start, 1)
        )
    d_hidden, dg_pre = rms_back(hidden, gp_ref[...], d_pre)
    d_hidden = dy + d_hidden
    dhid_ref[0] = d_hidden
    d_att, dg_attn = rms_back(attended, ga_ref[...], d_hidden)
    d_att = d_att.astype(jnp.bfloat16)
    datt_ref[0] = d_att
    dg_ref[0] = jnp.concatenate([dg_attn, dg_pre, dg_ffn], axis=0)
    for head in range(heads):
        d_mixed = dot_nn(
            d_att, pair_columns(units + head * size, units + (head + 1) * size)
        ).astype(jnp.bfloat16)
        for t in range(2):
            dmix_ref[0, t, head * part : (head + 1) * part, :] = d_mixed[t * part : (t + 1) * part]


def attend_back_kernel(
    heads, waits, q_ref, qraw_ref, far_ref, near_ref, own_ref, qid_ref, kid_ref, mixed_ref, dmix_ref,
    cos_ref, sin_ref, gq_ref, *refs
):
    dfar_ref, dnear_ref, down_ref, dqraw_ref, dg_ref, win_ref, grad_ref = refs[waits:]
    size = q_ref.shape[-1]
    part = q_ref.shape[2] // heads
    span = part + WINDOW
    far, near = far_ref.shape[1], near_ref.shape[1]
    load_window(far_ref, near_ref, own_ref, win_ref)
    grad_ref[...] = jnp.zeros_like(grad_ref)
    dg = jnp.zeros((1, size), jnp.float32)
    for t in range(2):
        rows = slice(t * part, (t + 1) * part)
        window = slice(t * part, t * part + span)
        bias = mask_bias(qid_ref, kid_ref, t, part, span)
        keys = win_ref[window, :size]
        values = win_ref[window, size:]
        cosine, sine = cos_ref[0, rows, :], sin_ref[0, rows, :]
        for head in range(heads):
            line = slice(head * part, (head + 1) * part)
            lanes = slice(head * size, (head + 1) * size)
            query = q_ref[0, t, line, :]
            d_out = dmix_ref[0, t, line, :]
            weights = jnp.exp(dot_nt(query, keys) + bias)
            weights = weights * (1.0 / jnp.sum(weights, axis=-1, keepdims=True))
            delta = jnp.sum(
                d_out.astype(jnp.float32) * mixed_ref[0, rows, lanes].astype(jnp.float32),
                axis=-1,
                keepdims=True,
            )
            d_scores = (weights * (dot_nt(d_out, values) - delta)).astype(jnp.bfloat16)
            weights = weights.astype(jnp.bfloat16)
            grad_ref[window, :size] += dot_tn(d_scores, query)
            grad_ref[window, size:] += dot_tn(weights, d_out)
            d_query = dot_nn(d_scores, keys) * size ** (-0.5)
            d_raw, part_g = rms_back(
                qraw_ref[0, t, line, :].astype(jnp.float32),
                gq_ref[...],
                turn(d_query, cosine, -sine),
            )
            dqraw_ref[0, rows, lanes] = d_raw.astype(jnp.bfloat16)
            dg += part_g
    dg_ref[0] = dg
    dfar_ref[0] = grad_ref[:far, :].astype(jnp.bfloat16)
    dnear_ref[0] = grad_ref[far : far + near, :]
    down_ref[0] = grad_ref[far + near :, :]


def input_back_kernel(
    waits, own_ref, recv_ref, kraw_ref, cos_ref, sin_ref, wk_ref, wv_ref, dq_ref, wq_ref, x_ref, dhid_ref,
    gi_ref, gk_ref, *refs
):
    grad_ref, dpair_ref, dgi_ref, dgk_ref = refs[waits:]
    size = wk_ref.shape[0]
    total = own_ref[0] + recv_ref[0].astype(jnp.float32)
    d_key = turn(total[:, :size], cos_ref[0], -sin_ref[0])
    d_raw, dg_key = rms_back(kraw_ref[0].astype(jnp.float32), gk_ref[...], d_key)
    d_raw = d_raw.astype(jnp.bfloat16)
    d_value = total[:, size:].astype(jnp.bfloat16)
    dpair_ref[0, :, :size] = d_raw
    dpair_ref[0, :, size:] = d_value
    d_normed = dot_nn(dq_ref[0], wq_ref[...])
    d_normed += dot_nn(d_raw, wk_ref[...]) + dot_nn(d_value, wv_ref[...])
    d_x, dg_input = rms_back(x_ref[0].astype(jnp.float32), gi_ref[...], d_normed)
    grad_ref[0] = dhid_ref[0] + d_x
    dgi_ref[0] = dg_input
    dgk_ref[0] = dg_key


def flips(bit):
    return [(i, i ^ (1 << bit)) for i in range(lax.axis_size("dp"))]


def device_index():
    return lax.axis_index("dp")[None].astype(jnp.int32)


def side(bit):
    return (lax.axis_index("dp") >> bit) & 1


def stack_step(pairs, bits, done, arrived=()):
    axes = [sum(1 for other in before if other > bit) for bit, before in zip(bits, done)]
    anywhere = pl.BlockSpec(memory_space=pl.ANY)
    block = pl.BlockSpec(memory_space=pltpu.VMEM)
    arrived = list(arrived)
    shapes = [
        own.shape[:axis] + (2,) + own.shape[axis:] for (own, _), axis in zip(pairs, axes)
    ]
    return pl.pallas_call(
        functools.partial(stack_kernel, bits, axes, len(arrived)),
        out_shape=[jax.ShapeDtypeStruct(shape, jnp.bfloat16) for shape in shapes],
        in_specs=[pl.BlockSpec(memory_space=pltpu.SMEM)]
        + [block] * (2 * len(pairs))
        + [anywhere] * len(arrived),
        out_specs=[block] * len(pairs),
        compiler_params=pltpu.CompilerParams(vmem_limit_bytes=VMEM_BYTES),
    )(device_index(), *[array for pair in pairs for array in pair], *arrived)


class RowSum:
    def __init__(self, parts, order, axis):
        self.terms = [
            (part.reshape((2,) * len(order) + part.shape[1:]), list(range(len(order) - 1, -1, -1)))
            for part in parts
        ]
        self.join = axis
        self.order = order
        self.chosen = {}
        self.received = []

    @classmethod
    def from_halves(cls, keep, send, order):
        result = cls([], order, -1)
        shape = (2,) * (len(order) - 1) + keep.shape[1:]
        left = list(range(len(order) - 1, 0, -1))
        received = lax.ppermute(send, "dp", flips(0))
        result.terms = [(keep.reshape(shape), left)]
        result.received = [(received.reshape(shape), left)]
        result.chosen = {0: side(0)}
        result.sent = send
        return result

    def total(self, other=None):
        picks = dict(self.chosen)
        if other is not None:
            picks[other] = 1 - side(other)
        pieces = [self.pick(part, bits, picks) for part, bits in self.terms]
        value = jnp.concatenate(pieces, axis=self.join) if len(pieces) > 1 else pieces[0]
        value = value.astype(jnp.float32)
        for part, bits in self.received:
            value += self.pick(part, bits, picks).astype(jnp.float32)
        return value.astype(jnp.bfloat16)

    def ordered_total(self, after, other=None):
        gone = set(self.chosen) | ({other} if other is not None else set())
        left = [b for b in range(len(self.order) - 1, -1, -1) if b not in gone]
        terms = self.terms + self.received
        block = terms[0][0].shape[-2:]
        anywhere = pl.BlockSpec(memory_space=pl.ANY)

        def spec(bits):
            def place(g, index):
                flat = 0
                for bit in bits:
                    if bit in gone:
                        value = (index[0] >> bit) & 1
                        value = 1 - value if bit == other else value
                    else:
                        value = (g >> (len(left) - 1 - left.index(bit))) & 1
                    flat = 2 * flat + value
                return (flat, 0, 0)

            return pl.BlockSpec((1,) + block, place)

        count = 2 ** len(left)
        out = pl.pallas_call(
            functools.partial(sum_kernel, len(terms)),
            out_shape=jax.ShapeDtypeStruct((count,) + block, jnp.bfloat16),
            grid_spec=pltpu.PrefetchScalarGridSpec(
                num_scalar_prefetch=1,
                grid=(count,),
                in_specs=[spec(bits) for _, bits in terms] + [anywhere] * len(after),
                out_specs=pl.BlockSpec((1,) + block, lambda g, index: (g, 0, 0)),
            ),
            compiler_params=kernel_params(),
        )(device_index(), *[part.reshape((-1,) + block) for part, _ in terms], *after)
        return out.reshape((2,) * len(left) + block)

    def ordered_step(self, bit, after):
        self.sent = self.ordered_total(after, bit)
        self.receive(bit)

    def receive(self, bit):
        received = lax.ppermute(self.sent, "dp", flips(bit))
        self.chosen[bit] = side(bit)
        left = [b for b in range(len(self.order) - 1, -1, -1) if b not in self.chosen]
        self.received.append((received, left))
        return received

    def pick(self, part, bits, picks):
        bits = list(bits)
        for bit, where in picks.items():
            if bit in bits:
                part = lax.dynamic_index_in_dim(part, where, bits.index(bit), keepdims=False)
                bits.remove(bit)
        return part

    def send(self, bit):
        self.sent = self.total(bit)
        return self.sent

    def step(self, bit):
        self.send(bit)
        return self.receive(bit)


def seq_sum(part):
    count = lax.axis_size("seq")
    total = part.astype(jnp.float32)
    distance = 1
    while distance < count:
        pairs = [(i, i ^ distance) for i in range(count)]
        received = lax.ppermute(total.astype(jnp.bfloat16), "seq", pairs)
        total = total.astype(jnp.bfloat16).astype(jnp.float32) + received.astype(jnp.float32)
        distance *= 2
    return total


def body(
    tokens,
    cotangent,
    segments,
    positions,
    query_weight,
    key_weight,
    value_weight,
    output_weight,
    gate_weight,
    up_weight,
    down_weight,
    norm_gains,
    query_first,
    key_first,
    value_first,
    output_first,
    gate_first,
    up_first,
    down_first,
    gains_first,
    query_second,
    key_second,
    value_second,
    output_second,
    gate_second,
    up_second,
    down_second,
    gains_second,
):
    count = lax.axis_size("dp")
    bits = (count - 1).bit_length()
    order_a = list(range(1, bits)) + [0]
    order_b = list(range(bits - 1, 0, -1)) + [0]
    low = jnp.bfloat16
    f32 = jnp.float32
    width = tokens.shape[2]
    key_rows = key_weight.shape[0]
    gain_rows = norm_gains.shape[0]
    rest_rows = 2 * key_rows + 16

    def array(shape, kind):
        return jax.ShapeDtypeStruct(shape, kind)

    query_rows = query_weight.shape[0]
    first_shard = pl.pallas_call(
        cast_first_kernel,
        out_shape=array((query_rows + rest_rows, width), low),
    )(query_weight, key_weight, value_weight, norm_gains[None])
    block = pl.BlockSpec(memory_space=pltpu.VMEM)
    anywhere = pl.BlockSpec(memory_space=pl.ANY)
    first_received = lax.ppermute(first_shard, "dp", flips(order_b[0]))
    pair_width = down_weight.shape[1] + output_weight.shape[1]
    pair_half_shape = array((down_weight.shape[0], pair_width // 2), low)
    shards_low = pl.pallas_call(
        functools.partial(cast_rest_kernel, 1),
        out_shape=[
            array(gate_weight.shape, low),
            array(up_weight.shape, low),
            pair_half_shape,
            pair_half_shape,
        ],
        in_specs=[block] * 4 + [anywhere],
    )(gate_weight, up_weight, down_weight, output_weight, first_received)
    rest_orders = [order_a, order_b, order_a, order_b]

    def rest_step(blocks, i):
        return [
            lax.ppermute(own, "dp", flips(order[i])) for own, order in zip(blocks, rest_orders)
        ]

    def rest_stack(blocks, received, i, arrived):
        return stack_step(
            list(zip(blocks, received)),
            [order[i] for order in rest_orders],
            [order[:i] for order in rest_orders],
            arrived,
        )

    (first_all,) = stack_step([(first_shard, first_received)], [order_b[0]], [[]])
    for i in range(1, bits):
        first_received = lax.ppermute(first_all, "dp", flips(order_b[i]))
        (first_all,) = stack_step(
            [(first_all, first_received)], [order_b[i]], [order_b[:i]], shards_low[:1]
        )
    first_all = first_all.reshape((count,) + first_shard.shape)
    rest_received = rest_step(shards_low, 0)
    key_start = query_rows + key_rows
    w_query = first_all[:, :query_rows].reshape(-1, width)
    w_key = first_all[:, query_rows:key_start].reshape(-1, width)
    w_value = first_all[:, key_start : key_start + key_rows].reshape(-1, width)
    gains_all = first_all[:, key_start + key_rows, :gain_rows].reshape(-1)
    seqs, rows, _ = tokens.shape
    size = w_key.shape[0]
    heads = w_query.shape[0] // size
    units = down_weight.shape[1]
    shards = lax.axis_size("seq")
    far = WINDOW - rows
    part = rows // 2
    span = part + WINDOW
    gains_float = gains_all.astype(jnp.float32)[None]
    g_input, g_attn, g_pre, g_ffn = (
        gains_float[:, i * width : (i + 1) * width] for i in range(4)
    )
    g_query = gains_float[:, 4 * width : 4 * width + size]
    g_key = gains_float[:, 4 * width + size : 4 * width + 2 * size]
    angles = positions.astype(jnp.float32)[..., None] * frequencies(size)
    cosine, sine = jnp.cos(angles), jnp.sin(angles)
    core_side = side(0)[None].astype(jnp.int32)
    first_row = lax.axis_index("seq") * rows
    padded = jnp.concatenate([jnp.full((seqs, WINDOW), -1, jnp.int32), segments], axis=1)
    window_ids = lax.dynamic_slice_in_dim(padded, first_row, WINDOW + rows, 1)
    query_ids = window_ids[:, WINDOW:, None]
    key_ids = jnp.stack([window_ids[:, :span], window_ids[:, part:]], axis=1)[:, :, None, :]

    def call(kernel, outs, out_specs, in_specs, scratch, flops, moved):
        return pl.pallas_call(
            kernel,
            grid=(seqs,),
            out_shape=outs,
            in_specs=in_specs,
            out_specs=out_specs,
            scratch_shapes=scratch,
            compiler_params=kernel_params(),
            cost_estimate=pl.CostEstimate(flops=flops, bytes_accessed=moved, transcendentals=0),
        )

    tokens_all = seqs * rows
    head_block = per_seq(2, heads * part, size)
    q_shape = (seqs, 2, heads * part, size)
    normed, pair_own, key_raw = call(
        functools.partial(project_pair_kernel, 6),
        [
            array((seqs, rows, width), low),
            array((seqs, rows, 2 * size), low),
            array((seqs, rows, size), low),
        ],
        [per_seq(rows, width), per_seq(rows, 2 * size), per_seq(rows, size)],
        [
            per_seq(rows, width),
            per_seq(rows, size // 2),
            per_seq(rows, size // 2),
            whole(*w_key.shape),
            whole(*w_value.shape),
            whole(1, width),
            whole(1, size),
        ]
        + [anywhere] * 6,
        [],
        4 * tokens_all * width * size,
        6_000_000,
    )(
        tokens, cosine, sine, w_key, w_value, g_input, g_key, query_ids, key_ids, *rest_received
    )
    upward = [(i, i + 1) for i in range(shards - 1)]
    pair_near = lax.ppermute(pair_own, "seq", upward)
    rest_blocks = rest_stack(shards_low, rest_received, 0, [pair_own])
    query, query_raw = call(
        functools.partial(project_query_kernel, heads, 1),
        [array(q_shape, low), array(q_shape, low)],
        [head_block, head_block],
        [
            per_seq(rows, width),
            per_seq(rows, size // 2),
            per_seq(rows, size // 2),
            whole(*w_query.shape),
            whole(1, size),
            anywhere,
        ],
        [],
        2 * tokens_all * width * heads * size,
        8_000_000,
    )(normed, cosine, sine, w_query, g_query, rest_blocks[0])

    far_send = pl.pallas_call(
        functools.partial(tail_rows_kernel, 1),
        out_shape=array((seqs, far, 2 * size), low),
        in_specs=[block, anywhere],
        out_specs=block,
        compiler_params=pltpu.CompilerParams(vmem_limit_bytes=VMEM_BYTES),
    )(pair_near, query)
    pair_far = lax.ppermute(far_send, "seq", upward[1:])
    for i in range(1, bits - 1):
        rest_blocks = rest_stack(rest_blocks, rest_step(rest_blocks, i), i, [pair_far])
    rest_blocks = [
        blocks.reshape((count // 2,) + blocks.shape[-2:]) for blocks in rest_blocks
    ]
    rest_received = [lax.ppermute(blocks, "dp", flips(0)) for blocks in rest_blocks]
    rest_operands = [array for pair in zip(rest_blocks, rest_received) for array in pair]

    window_specs = [
        per_seq(far, 2 * size),
        per_seq(rows, 2 * size),
        per_seq(rows, 2 * size),
        per_seq(rows, 1),
        per_seq(2, 1, span),
    ]
    attend_flops = 8 * tokens_all * heads * span * size
    mixed = call(
        functools.partial(attend_kernel, heads),
        array((seqs, rows, heads * size), low),
        per_seq(rows, heads * size),
        [head_block] + window_specs,
        [pltpu.VMEM((WINDOW + rows, 2 * size), low)],
        attend_flops,
        16_000_000,
    )(query, pair_far, pair_near, pair_own, query_ids, key_ids)

    (
        layer_output,
        pre_low,
        product_low,
        grad_down_low,
        grad_gate_low,
        grad_up_low,
        grad_attended_low,
        grad_hidden,
        grad_mixed,
        grad_gains_middle,
    ) = call(
        functools.partial(middle_kernel, heads, 512),
        [
            array((seqs, rows, width), low),
            array((seqs, rows, width), low),
            array((seqs, rows, units), low),
            array((seqs, rows, width), low),
            array((seqs, rows, units), low),
            array((seqs, rows, units), low),
            array((seqs, rows, width), low),
            array((seqs, rows, width), f32),
            array(q_shape, low),
            array((seqs, 3, width), f32),
        ],
        [
            per_seq(rows, width),
            per_seq(rows, width),
            per_seq(rows, units),
            per_seq(rows, width),
            per_seq(rows, units),
            per_seq(rows, units),
            per_seq(rows, width),
            per_seq(rows, width),
            head_block,
            per_seq(3, width),
        ],
        [
            pl.BlockSpec(memory_space=pltpu.SMEM),
            per_seq(rows, heads * size),
            per_seq(rows, width),
            per_seq(rows, width),
            anywhere,
            anywhere,
            anywhere,
            anywhere,
            anywhere,
            anywhere,
            anywhere,
            anywhere,
            whole(1, width),
            whole(1, width),
            whole(1, width),
        ],
        [
            pltpu.VMEM((rows, units), f32),
            pltpu.VMEM((rows, units), f32),
            pltpu.VMEM((count // 2, 2, 2 * gate_weight.shape[0], width), low),
            pltpu.VMEM((count // 2, 2, down_weight.shape[0], pair_width), low),
            pltpu.SemaphoreType.DMA((8,)),
        ],
        4 * tokens_all * width * (heads * size + 3 * units),
        40_000_000,
    )(
        core_side, mixed, tokens, cotangent, *rest_operands, g_attn, g_pre, g_ffn,
    )

    def flat(values):
        return values.reshape(tokens_all, values.shape[-1])

    def grad_blocks(gradient, inputs):
        product = weight_grad(flat(gradient), flat(inputs)).astype(low)
        return product.reshape(count, -1, product.shape[1])

    back_a = [0] + order_a[:-1]
    back_b = [0] + order_b[:-1]
    shard_units = gate_weight.shape[0]
    shard_rows = down_weight.shape[0]
    half = count // 2
    direct = shard_units % 128 == 0 and shard_rows % 16 == 0
    if direct:
        columns = 512
        first = units // columns
        last = heads * size // columns
        pair_block = pl.BlockSpec((half, shard_rows, columns), lambda k, side: (0, 0, k))
        pair_shape = array((half, shard_rows, units + heads * size), low)
        fixed = pl.BlockSpec(
            (tokens_all, width), lambda k, side: (0, 0), pipeline_mode=pl.Buffered(1)
        )
        pair_send, pair_keep = pl.pallas_call(
            functools.partial(pair_grad_kernel, first),
            out_shape=[pair_shape, pair_shape],
            grid_spec=pltpu.PrefetchScalarGridSpec(
                num_scalar_prefetch=1,
                grid=(first + last,),
                in_specs=[
                    pl.BlockSpec(
                        (tokens_all, columns), lambda k, side: (0, jnp.minimum(k, first - 1))
                    ),
                    pl.BlockSpec(
                        (tokens_all, columns), lambda k, side: (0, jnp.maximum(k - first, 0))
                    ),
                    fixed,
                    fixed,
                ],
                out_specs=[pair_block, pair_block],
                scratch_shapes=[
                    pltpu.VMEM((width, tokens_all), low),
                    pltpu.VMEM((width, columns), f32),
                ],
            ),
            compiler_params=kernel_params(),
            cost_estimate=pl.CostEstimate(
                flops=2 * tokens_all * width * (units + heads * size),
                bytes_accessed=13_000_000,
                transcendentals=0,
            ),
        )(core_side, flat(product_low), flat(mixed), flat(grad_down_low), flat(grad_attended_low))
        down_out_sum = RowSum.from_halves(pair_keep, pair_send, back_b)

        def shard_of(g, side):
            return (0, 2 * (g % half) + jnp.where(g < half, 1 - side[0], side[0]))

        block_shape = (1, 2 * shard_units, width)
        half_shape = array((half, 2 * shard_units, width), low)
        gate_up_send, gate_up_keep = pl.pallas_call(
            gate_up_grad_kernel,
            out_shape=[half_shape, half_shape],
            grid_spec=pltpu.PrefetchScalarGridSpec(
                num_scalar_prefetch=1,
                grid=(count,),
                in_specs=[
                    pl.BlockSpec((tokens_all, shard_units), shard_of),
                    pl.BlockSpec((tokens_all, shard_units), shard_of),
                    fixed,
                    anywhere,
                ],
                out_specs=[
                    pl.BlockSpec(block_shape, lambda g, side: (jnp.minimum(g, half - 1), 0, 0)),
                    pl.BlockSpec(block_shape, lambda g, side: (jnp.maximum(g - half, 0), 0, 0)),
                ],
            ),
            compiler_params=kernel_params(),
            cost_estimate=pl.CostEstimate(
                flops=4 * tokens_all * width * units, bytes_accessed=14_000_000, transcendentals=0
            ),
        )(core_side, flat(grad_gate_low), flat(grad_up_low), flat(pre_low), pair_send)
        gate_up_sum = RowSum.from_halves(gate_up_keep, gate_up_send, back_a)
    else:
        pair_blocks = jnp.concatenate(
            [grad_blocks(grad_down_low, product_low), grad_blocks(grad_attended_low, mixed)], axis=-1
        )
        down_out_sum = RowSum([pair_blocks], back_b, -1)
        down_out_sum.step(0)
        gate_up_blocks = jnp.concatenate(
            [grad_blocks(grad_gate_low, pre_low), grad_blocks(grad_up_low, pre_low)], axis=-2
        )
        gate_up_sum = RowSum([gate_up_blocks], back_a, -2)
        gate_up_sum.step(0)

    def at_seq(s, *tail):
        return pl.BlockSpec((1,) + tail, lambda g: (s,) + (0,) * len(tail))

    def seq_call(kernel, outs, out_specs, in_specs, operands, scratch, alias, flops):
        return pl.pallas_call(
            kernel,
            grid=(1,),
            out_shape=outs,
            in_specs=in_specs,
            out_specs=out_specs,
            scratch_shapes=scratch,
            input_output_aliases=alias,
            compiler_params=kernel_params(),
            cost_estimate=pl.CostEstimate(
                flops=flops, bytes_accessed=8_000_000, transcendentals=0
            ),
        )(*operands)

    def attend_back(s, buffer, arrived):
        kinds = [
            array((1, far, 2 * size), low),
            array((1, rows, 2 * size), f32),
            array((1, rows, 2 * size), f32),
            array((seqs, rows, heads * size), low),
            array((1, 1, size), f32),
        ]
        specs = [
            at_seq(0, far, 2 * size),
            at_seq(0, rows, 2 * size),
            at_seq(0, rows, 2 * size),
            at_seq(s, rows, heads * size),
            at_seq(0, 1, size),
        ]
        in_specs = [
            at_seq(s, 2, heads * part, size),
            at_seq(s, 2, heads * part, size),
            at_seq(s, far, 2 * size),
            at_seq(s, rows, 2 * size),
            at_seq(s, rows, 2 * size),
            at_seq(s, rows, 1),
            at_seq(s, 2, 1, span),
            at_seq(s, rows, heads * size),
            at_seq(s, 2, heads * part, size),
            at_seq(s, rows, size // 2),
            at_seq(s, rows, size // 2),
            whole(1, size),
        ]
        operands = [
            query, query_raw, pair_far, pair_near, pair_own, query_ids, key_ids, mixed, grad_mixed,
            cosine, sine, g_query,
        ]
        alias = {}
        extra = list(arrived)
        if buffer is not None:
            alias = {len(operands): 3}
            extra = [buffer] + extra
        return seq_call(
            functools.partial(attend_back_kernel, heads, len(extra)),
            kinds,
            specs,
            in_specs + [anywhere] * len(extra),
            operands + extra,
            [
                pltpu.VMEM((WINDOW + rows, 2 * size), low),
                pltpu.VMEM((WINDOW + rows, 2 * size), f32),
            ],
            alias,
            attend_flops * 3 // seqs,
        )

    downward = [(i + 1, i) for i in range(shards - 1)]
    grad_query_low = None
    arrived = [gate_up_sum.sent]

    def near_total(grad_near, from_far, after):
        return pl.pallas_call(
            functools.partial(near_sum_kernel, len(after)),
            out_shape=array(grad_near.shape, low),
            in_specs=[block] * 2 + [anywhere] * len(after),
            out_specs=block,
        )(grad_near, from_far, *after)

    own_parts, query_gains, near_sums, far_parts, near_parts = [], [], [], [], []
    for s in range(seqs):
        grad_far, grad_near, grad_own, grad_query_low, g_part = attend_back(
            s, grad_query_low, arrived
        )
        from_far = lax.ppermute(grad_far, "seq", downward[1:])
        own_parts.append(grad_own)
        query_gains.append(g_part)
        far_parts.append(from_far)
        near_parts.append(grad_near)
        if s == 0:
            down_out_sum.ordered_step(back_b[1], [grad_own])
            gate_up_sum.ordered_step(back_a[1], [down_out_sum.sent])
            arrived = [gate_up_sum.sent]
        elif s == 1:
            near_sums.append(near_total(near_parts[0], far_parts[0], [grad_own]))
            from_near = [lax.ppermute(near_sums[0], "seq", downward)]
            arrived = [near_sums[0]]
    for bit in back_b[2:]:
        down_out_sum.ordered_step(bit, [own_parts[-1]])
    near_sums.append(near_total(near_parts[1], far_parts[1], [down_out_sum.sent]))
    from_near.append(lax.ppermute(near_sums[1], "seq", downward))
    query_columns = heads * size
    grad_w_query = pl.pallas_call(
        functools.partial(query_grad_kernel, 3),
        grid=(heads,),
        out_shape=array((query_columns, width), low),
        in_specs=[
            pl.BlockSpec((tokens_all, size), lambda i: (0, i)),
            whole(tokens_all, width),
            anywhere,
            anywhere,
            anywhere,
        ],
        out_specs=pl.BlockSpec((size, width), lambda i: (i, 0)),
        compiler_params=kernel_params(),
        cost_estimate=pl.CostEstimate(
            flops=2 * tokens_all * width * query_columns, bytes_accessed=5_000_000, transcendentals=0
        ),
    )(
        flat(grad_query_low), flat(normed), near_sums[1], down_out_sum.sent, from_near[0]
    )
    near_sums.append(near_total(near_parts[2], far_parts[2], [grad_w_query]))
    from_near.append(lax.ppermute(near_sums[2], "seq", downward))
    for bit in back_a[2:]:
        gate_up_sum.ordered_step(bit, [near_sums[2], from_near[1]])

    def input_back(s, buffers, arrived):
        kinds = [
            array((seqs, rows, width), f32),
            array((seqs, rows, 2 * size), low),
            array((1, 1, width), f32),
            array((1, 1, size), f32),
        ]
        specs = [
            at_seq(s, rows, width),
            at_seq(s, rows, 2 * size),
            at_seq(0, 1, width),
            at_seq(0, 1, size),
        ]
        in_specs = [
            at_seq(0, rows, 2 * size),
            at_seq(0, rows, 2 * size),
            at_seq(s, rows, size),
            at_seq(s, rows, size // 2),
            at_seq(s, rows, size // 2),
            whole(*w_key.shape),
            whole(*w_value.shape),
            at_seq(s, rows, heads * size),
            whole(*w_query.shape),
            at_seq(s, rows, width),
            at_seq(s, rows, width),
            whole(1, width),
            whole(1, size),
        ]
        operands = [
            own_parts[s], from_near[s], key_raw, cosine, sine, w_key, w_value, grad_query_low,
            w_query, tokens, grad_hidden, g_input, g_key,
        ]
        alias = {}
        extra = list(arrived)
        if buffers:
            alias = {len(operands): 0, len(operands) + 1: 1}
            extra = list(buffers) + extra
        return seq_call(
            functools.partial(input_back_kernel, len(extra)),
            kinds,
            specs,
            in_specs + [anywhere] * len(extra),
            operands + extra,
            [],
            alias,
            2 * rows * width * size * (heads + 2),
        )

    buffers = []
    input_gains, key_gains = [], []
    for s in range(seqs):
        waits = [gate_up_sum.sent]
        if s == seqs - 1:
            down_out_part = down_out_sum.ordered_total(
                [buffers[0], from_near[s], gate_up_sum.received[-1][0]]
            )
            gate_up_part = gate_up_sum.ordered_total([down_out_part])
            waits = [gate_up_part]
        *buffers, g_part, g_key_part = input_back(s, buffers, waits)
        input_gains.append(g_part)
        key_gains.append(g_key_part)
    input_grad, grad_pair_low = buffers
    key_value_blocks = grad_blocks(grad_pair_low, normed).reshape(2, count, key_rows, width)
    grad_gains = jnp.concatenate(
        [
            sum(input_gains).reshape(-1),
            jnp.sum(grad_gains_middle, axis=0).reshape(-1),
            sum(query_gains).reshape(-1),
            sum(key_gains).reshape(-1),
        ]
    )
    gain_block = jnp.pad(
        grad_gains.astype(low).reshape(count, 1, gain_rows),
        ((0, 0), (0, 15), (0, width - gain_rows)),
    )
    rest_sum = RowSum(
        [
            grad_w_query.reshape(count, query_rows, width),
            key_value_blocks[0],
            key_value_blocks[1],
            gain_block,
        ],
        back_b,
        -2,
    )
    for bit in back_b:
        rest_sum.step(bit)
    down_out_total = seq_sum(down_out_part)
    gate_total = seq_sum(gate_up_part[:shard_units])
    up_total = seq_sum(gate_up_part[shard_units:])
    rest_total = seq_sum(rest_sum.total())
    query_total = rest_total[:query_rows]
    rest_total = rest_total[query_rows:]
    down_total = down_out_total[:, :units]
    output_total = down_out_total[:, units:]
    key_total = rest_total[:key_rows]
    value_total = rest_total[key_rows : 2 * key_rows]
    gains_total = rest_total[2 * key_rows, :gain_rows]
    query_momentum, query_variance, query_updated = adam_step(
        query_weight, query_first, query_second, query_total, WEIGHT_DECAY
    )
    key_momentum, key_variance, key_updated = adam_step(
        key_weight, key_first, key_second, key_total, WEIGHT_DECAY
    )
    value_momentum, value_variance, value_updated = adam_step(
        value_weight, value_first, value_second, value_total, WEIGHT_DECAY
    )
    output_momentum, output_variance, output_updated = adam_step(
        output_weight, output_first, output_second, output_total, WEIGHT_DECAY
    )
    gate_momentum, gate_variance, gate_updated = adam_step(
        gate_weight, gate_first, gate_second, gate_total, WEIGHT_DECAY
    )
    up_momentum, up_variance, up_updated = adam_step(
        up_weight, up_first, up_second, up_total, WEIGHT_DECAY
    )
    down_momentum, down_variance, down_updated = adam_step(
        down_weight, down_first, down_second, down_total, WEIGHT_DECAY
    )
    gains_momentum, gains_variance, gains_updated = adam_step(
        norm_gains, gains_first, gains_second, gains_total, 0.0
    )
    return (
        layer_output,
        input_grad,
        query_momentum,
        key_momentum,
        value_momentum,
        output_momentum,
        gate_momentum,
        up_momentum,
        down_momentum,
        gains_momentum,
        query_variance,
        key_variance,
        value_variance,
        output_variance,
        gate_variance,
        up_variance,
        down_variance,
        gains_variance,
        query_updated,
        key_updated,
        value_updated,
        output_updated,
        gate_updated,
        up_updated,
        down_updated,
        gains_updated,
    )


def solution(mesh):
    return jax.shard_map(
        body,
        mesh=mesh,
        in_specs=(
            P("dp", "seq", None),
            P("dp", "seq", None),
            P("dp", None),
            P("dp", "seq"),
            P("dp", None),
            P("dp", None),
            P("dp", None),
            P("dp", None),
            P("dp", None),
            P("dp", None),
            P("dp", None),
            P("dp"),
            P("dp", None),
            P("dp", None),
            P("dp", None),
            P("dp", None),
            P("dp", None),
            P("dp", None),
            P("dp", None),
            P("dp"),
            P("dp", None),
            P("dp", None),
            P("dp", None),
            P("dp", None),
            P("dp", None),
            P("dp", None),
            P("dp", None),
            P("dp"),
        ),
        out_specs=(
            P("dp", "seq", None),
            P("dp", "seq", None),
            P("dp", None),
            P("dp", None),
            P("dp", None),
            P("dp", None),
            P("dp", None),
            P("dp", None),
            P("dp", None),
            P("dp"),
            P("dp", None),
            P("dp", None),
            P("dp", None),
            P("dp", None),
            P("dp", None),
            P("dp", None),
            P("dp", None),
            P("dp"),
            P("dp", None),
            P("dp", None),
            P("dp", None),
            P("dp", None),
            P("dp", None),
            P("dp", None),
            P("dp", None),
            P("dp"),
        ),
        check_vma=False,
    )
```

```python
import functools
import math

import jax
import jax.numpy as jnp
from jax import lax
from jax.experimental import pallas as pl
from jax.experimental.pallas import tpu as pltpu
from jax.sharding import PartitionSpec as P

WINDOW = 512
STEP = 10


NORM_EPSILON = 1e-06
ROPE_BASE = 10000.0
LEARN_RATE = 0.08
BETA_FIRST = 0.9
BETA_SECOND = 0.95
ADAM_EPSILON = 1e-08
WEIGHT_DECAY = 0.01
MASKED_SCORE = -1000000000.0


def frequencies(size):
    return ROPE_BASE ** (-2.0 * jnp.arange(size // 2).astype(jnp.float32) / size)


def weight_grad(gradients, inputs):
    return lax.dot_general(
        gradients, inputs, (((0,), (0,)), ((), ())), preferred_element_type=jnp.float32
    )


def adam_step(weight, first_moment, second_moment, gradient, decay_rate):
    momentum = BETA_FIRST * first_moment + (1.0 - BETA_FIRST) * gradient
    variance = BETA_SECOND * second_moment + (1.0 - BETA_SECOND) * gradient * gradient
    corrected = momentum / (1.0 - BETA_FIRST**STEP)
    scaled = variance / (1.0 - BETA_SECOND**STEP)
    updated = weight - LEARN_RATE * (
        corrected / (jnp.sqrt(scaled) + ADAM_EPSILON) + decay_rate * weight
    )
    return (momentum, variance, updated)


VMEM_BYTES = 56 * 1024 * 1024


def kernel_params():
    return pltpu.CompilerParams(
        dimension_semantics=("arbitrary",), vmem_limit_bytes=VMEM_BYTES
    )


def per_seq(*tail):
    return pl.BlockSpec((1,) + tail, lambda s: (s,) + (0,) * len(tail))


def whole(*shape):
    return pl.BlockSpec(shape, lambda s: (0,) * len(shape), pipeline_mode=pl.Buffered(1))


def dot_nt(a, b):
    return lax.dot_general(a, b, (((1,), (1,)), ((), ())), preferred_element_type=jnp.float32)


def dot_nn(a, b):
    return lax.dot_general(a, b, (((1,), (0,)), ((), ())), preferred_element_type=jnp.float32)


def dot_tn(a, b):
    return lax.dot_general(a, b, (((0,), (0,)), ((), ())), preferred_element_type=jnp.float32)


def inverse_rms(values):
    return lax.rsqrt(jnp.mean(values * values, axis=-1, keepdims=True) + NORM_EPSILON)


def rms_back(values, gain, grad):
    inverse = inverse_rms(values)
    unit = values * inverse
    scaled = grad * (1.0 + gain)
    return (
        inverse * (scaled - unit * jnp.mean(unit * scaled, axis=-1, keepdims=True)),
        jnp.sum(grad * unit, axis=0, keepdims=True),
    )


def turn(values, cosine, sine):
    half = values.shape[-1] // 2
    first, second = values[:, :half], values[:, half:]
    return jnp.concatenate(
        [first * cosine - second * sine, second * cosine + first * sine], axis=-1
    )


def stack_heads(values, heads):
    return jnp.concatenate([values] * heads, axis=0)


def cast_first_kernel(wq_ref, wk_ref, wv_ref, gain_ref, out_ref):
    width = wq_ref.shape[1]
    gains = gain_ref[...]
    tail = width - gains.shape[1]
    block = jnp.broadcast_to(gains, (16, gains.shape[1]))
    if tail:
        block = jnp.concatenate([block, jnp.zeros((16, tail), jnp.float32)], axis=1)
    parts = [wq_ref[...], wk_ref[...], wv_ref[...], block]
    out_ref[...] = jnp.concatenate(parts, axis=0).astype(jnp.bfloat16)


def cast_rest_kernel(waits, wg_ref, wu_ref, wd_ref, wo_ref, *refs):
    gate_ref, up_ref, first_ref, second_ref = refs[waits:]
    cut = first_ref.shape[1]
    rest = wd_ref.shape[1] - cut
    gate_ref[...] = wg_ref[...].astype(jnp.bfloat16)
    up_ref[...] = wu_ref[...].astype(jnp.bfloat16)
    first_ref[...] = wd_ref[:, :cut].astype(jnp.bfloat16)
    second_ref[:, :rest] = wd_ref[:, cut:].astype(jnp.bfloat16)
    second_ref[:, rest:] = wo_ref[...].astype(jnp.bfloat16)


def stack_kernel(bits, axes, waits, index_ref, *refs):
    count = len(bits)
    outs = refs[2 * count + waits :]
    for i in range(count):
        upper = (index_ref[0] >> bits[i]) & 1
        lead = (slice(None),) * axes[i]
        outs[i][lead + (upper,)] = refs[2 * i][...]
        outs[i][lead + (1 - upper,)] = refs[2 * i + 1][...]


def tail_rows_kernel(waits, near_ref, *refs):
    out_ref = refs[waits]
    out_ref[...] = near_ref[:, near_ref.shape[1] - out_ref.shape[1] :]


def near_sum_kernel(waits, near_ref, far_ref, *refs):
    out_ref = refs[waits]
    keep = near_ref.shape[1] - far_ref.shape[1]
    out_ref[0, :keep] = near_ref[0, :keep].astype(jnp.bfloat16)
    total = near_ref[0, keep:] + far_ref[0].astype(jnp.float32)
    out_ref[0, keep:] = total.astype(jnp.bfloat16)


def sum_kernel(count, index_ref, *refs):
    total = refs[0][0].astype(jnp.float32)
    for ref in refs[1:count]:
        total += ref[0].astype(jnp.float32)
    refs[-1][0] = total.astype(jnp.bfloat16)


def gate_up_grad_kernel(side_ref, dgate_ref, dup_ref, pre_ref, after_ref, send_ref, keep_ref):
    step = pl.program_id(0)
    half = pl.num_programs(0) // 2
    rows = dgate_ref.shape[1]

    gate = dot_tn(dgate_ref[...], pre_ref[...]).astype(jnp.bfloat16)
    up = dot_tn(dup_ref[...], pre_ref[...]).astype(jnp.bfloat16)

    @pl.when(step < half)
    def _():
        send_ref[0, :rows, :] = gate
        send_ref[0, rows:, :] = up

    @pl.when(step >= half)
    def _():
        keep_ref[0, :rows, :] = gate
        keep_ref[0, rows:, :] = up


def pair_grad_kernel(
    first, side_ref, product_ref, mixed_ref, ddown_ref, datt_ref, send_ref, keep_ref, turned_ref, total_ref
):
    step = pl.program_id(0)
    upper = side_ref[0]
    half, rows = send_ref.shape[0], send_ref.shape[1]

    @pl.when(step == 0)
    def _():
        turned_ref[...] = ddown_ref[...].T

    @pl.when(step == first)
    def _():
        turned_ref[...] = datt_ref[...].T

    @pl.when(step < first)
    def _():
        total_ref[...] = dot_nn(turned_ref[...], product_ref[...])

    @pl.when(step >= first)
    def _():
        total_ref[...] = dot_nn(turned_ref[...], mixed_ref[...])

    for i in range(half):
        mine = pl.multiple_of((2 * i + upper) * rows, rows)
        other = pl.multiple_of((2 * i + 1 - upper) * rows, rows)
        keep_ref[i] = total_ref[pl.ds(mine, rows), :].astype(jnp.bfloat16)
        send_ref[i] = total_ref[pl.ds(other, rows), :].astype(jnp.bfloat16)


def query_grad_kernel(waits, dq_ref, normed_ref, *refs):
    refs[waits][...] = dot_tn(dq_ref[...], normed_ref[...]).astype(jnp.bfloat16)


def project_pair_kernel(
    waits, x_ref, cos_ref, sin_ref, wk_ref, wv_ref, gi_ref, gk_ref, *refs
):
    normed_ref, kv_ref, kraw_ref = refs[waits:]
    x = x_ref[0].astype(jnp.float32)
    size = wk_ref.shape[0]
    normed = (x * inverse_rms(x) * (1.0 + gi_ref[...])).astype(jnp.bfloat16)
    normed_ref[0] = normed
    k_raw = dot_nt(normed, wk_ref[...])
    kraw_ref[0] = k_raw.astype(jnp.bfloat16)
    key = turn(k_raw * inverse_rms(k_raw) * (1.0 + gk_ref[...]), cos_ref[0], sin_ref[0])
    kv_ref[0, :, :size] = key.astype(jnp.bfloat16)
    kv_ref[0, :, size:] = dot_nt(normed, wv_ref[...]).astype(jnp.bfloat16)


def project_query_kernel(
    heads, waits, normed_ref, cos_ref, sin_ref, wq_ref, gq_ref, *refs
):
    q_ref, qraw_ref = refs[waits:]
    size = gq_ref.shape[-1]
    part = normed_ref.shape[1] // 2
    normed = normed_ref[0]
    cosine, sine = cos_ref[0], sin_ref[0]
    for head in range(heads):
        raw = dot_nt(normed, wq_ref[head * size : (head + 1) * size, :])
        query = turn(raw * inverse_rms(raw) * (1.0 + gq_ref[...]), cosine, sine)
        query = (query * size ** (-0.5)).astype(jnp.bfloat16)
        raw = raw.astype(jnp.bfloat16)
        for t in range(2):
            span = slice(head * part, (head + 1) * part)
            q_ref[0, t, span, :] = query[t * part : (t + 1) * part]
            qraw_ref[0, t, span, :] = raw[t * part : (t + 1) * part]


def load_window(far_ref, near_ref, own_ref, win_ref):
    far, near = far_ref.shape[1], near_ref.shape[1]
    win_ref[:far, :] = far_ref[0]
    win_ref[far : far + near, :] = near_ref[0]
    win_ref[far + near :, :] = own_ref[0]


def mask_bias(qid_ref, kid_ref, t, part, span):
    ids = qid_ref[0, t * part : (t + 1) * part, :] == kid_ref[0, t]
    row = lax.broadcasted_iota(jnp.int32, (part, span), 0)
    column = lax.broadcasted_iota(jnp.int32, (part, span), 1)
    ok = ids & (column > row) & (column <= row + WINDOW)
    return jnp.where(ok, 0.0, MASKED_SCORE)


def attend_kernel(heads, q_ref, far_ref, near_ref, own_ref, qid_ref, kid_ref, mixed_ref, win_ref):
    size = q_ref.shape[-1]
    part = q_ref.shape[2] // heads
    span = part + WINDOW
    load_window(far_ref, near_ref, own_ref, win_ref)
    for t in range(2):
        bias = mask_bias(qid_ref, kid_ref, t, part, span)
        keys = win_ref[t * part : t * part + span, :size]
        values = win_ref[t * part : t * part + span, size:]
        scores = dot_nt(q_ref[0, t], keys).reshape(heads, part, span)
        weights = jnp.exp(scores + bias[None]).reshape(heads * part, span)
        total = jnp.sum(weights, axis=-1, keepdims=True)
        mixed = (dot_nn(weights.astype(jnp.bfloat16), values) / total).astype(jnp.bfloat16)
        for head in range(heads):
            mixed_ref[0, t * part : (t + 1) * part, head * size : (head + 1) * size] = mixed[
                head * part : (head + 1) * part
            ]


def middle_kernel(
    heads, chunk, side_ref, mixed_ref, x_ref, cot_ref, gate_own_ref, gate_got_ref, up_own_ref, up_got_ref,
    first_own_ref, first_got_ref, second_own_ref, second_got_ref, ga_ref, gp_ref, gf_ref,
    out_ref, pre_ref, product_ref, ddown_ref, dgate_ref, dup_ref, datt_ref, dhid_ref, dmix_ref, dg_ref,
    act_ref, slope_ref, wgu_ref, wdo_blocks_ref, sems,
):
    @pl.when(pl.program_id(0) == 0)
    def _():
        upper = side_ref[0]
        copies = []
        shard = gate_own_ref.shape[1]
        cut = first_own_ref.shape[2]
        places = [
            (slice(None, cut), first_own_ref, first_got_ref),
            (slice(cut, None), second_own_ref, second_got_ref),
        ]
        for lanes, own, got in places:
            for place, source in ((upper, own), (1 - upper, got)):
                target = wdo_blocks_ref.at[:, place, :, lanes]
                copies.append(pltpu.make_async_copy(source, target, sems.at[len(copies)]))
        places = [
            (slice(None, shard), gate_own_ref, gate_got_ref),
            (slice(shard, None), up_own_ref, up_got_ref),
        ]
        for lines, own, got in places:
            for place, source in ((upper, own), (1 - upper, got)):
                target = wgu_ref.at[:, place, lines, :]
                copies.append(pltpu.make_async_copy(source, target, sems.at[len(copies)]))
        for copy in copies:
            copy.start()
        for copy in copies:
            copy.wait()

    def pair_columns(start, stop):
        picked = wdo_blocks_ref[:, :, :, start:stop]
        return picked.reshape(-1, stop - start)

    shard = wgu_ref.shape[2] // 2
    units = 2 * wgu_ref.shape[0] * shard
    group = chunk // shard

    def gate_up_rows(start, which):
        first = start // shard // 2
        picked = wgu_ref[first : first + group // 2, :, which * shard : (which + 1) * shard, :]
        return picked.reshape(chunk, picked.shape[-1])

    size = dmix_ref.shape[-1]
    part = dmix_ref.shape[2] // heads
    x = x_ref[0].astype(jnp.float32)
    attended = dot_nt(mixed_ref[0], pair_columns(units, units + heads * size))
    hidden = x + attended * inverse_rms(attended) * (1.0 + ga_ref[...])
    pre = (hidden * inverse_rms(hidden) * (1.0 + gp_ref[...])).astype(jnp.bfloat16)
    pre_ref[0] = pre
    down = jnp.zeros(x.shape, jnp.float32)
    root = (2.0 / math.pi) ** 0.5
    for start in range(0, units, chunk):
        span = slice(start, start + chunk)
        gate = dot_nt(pre, gate_up_rows(start, 0))
        up = dot_nt(pre, gate_up_rows(start, 1))
        square = gate * gate
        bend = jnp.tanh(gate * (root + (root * 0.044715) * square))
        half = 0.5 + 0.5 * bend
        act = gate * half
        slope = half + act * (1.0 - bend) * (root + (3.0 * root * 0.044715) * square)
        act_ref[:, span] = act
        slope_ref[:, span] = up * slope
        product = (act * up).astype(jnp.bfloat16)
        product_ref[0, :, span] = product
        down += dot_nt(product, pair_columns(start, start + chunk))
    out_ref[0] = (hidden + down * inverse_rms(down) * (1.0 + gf_ref[...])).astype(jnp.bfloat16)
    dy = cot_ref[0].astype(jnp.float32)
    d_down, dg_ffn = rms_back(down, gf_ref[...], dy)
    d_down = d_down.astype(jnp.bfloat16)
    ddown_ref[0] = d_down
    d_pre = jnp.zeros(x.shape, jnp.float32)
    for start in range(0, units, chunk):
        span = slice(start, start + chunk)
        d_product = dot_nn(d_down, pair_columns(start, start + chunk))
        d_gate = (d_product * slope_ref[:, span]).astype(jnp.bfloat16)
        d_up = (d_product * act_ref[:, span]).astype(jnp.bfloat16)
        dgate_ref[0, :, span] = d_gate
        dup_ref[0, :, span] = d_up
        d_pre += dot_nn(d_gate, gate_up_rows(start, 0)) + dot_nn(
            d_up, gate_up_rows(start, 1)
        )
    d_hidden, dg_pre = rms_back(hidden, gp_ref[...], d_pre)
    d_hidden = dy + d_hidden
    dhid_ref[0] = d_hidden
    d_att, dg_attn = rms_back(attended, ga_ref[...], d_hidden)
    d_att = d_att.astype(jnp.bfloat16)
    datt_ref[0] = d_att
    dg_ref[0] = jnp.concatenate([dg_attn, dg_pre, dg_ffn], axis=0)
    for head in range(heads):
        d_mixed = dot_nn(
            d_att, pair_columns(units + head * size, units + (head + 1) * size)
        ).astype(jnp.bfloat16)
        for t in range(2):
            dmix_ref[0, t, head * part : (head + 1) * part, :] = d_mixed[t * part : (t + 1) * part]


def attend_back_kernel(
    heads, waits, q_ref, qraw_ref, far_ref, near_ref, own_ref, qid_ref, kid_ref, mixed_ref, dmix_ref,
    cos_ref, sin_ref, gq_ref, *refs
):
    dfar_ref, dnear_ref, down_ref, dqraw_ref, dg_ref, win_ref, grad_ref = refs[waits:]
    size = q_ref.shape[-1]
    part = q_ref.shape[2] // heads
    span = part + WINDOW
    far, near = far_ref.shape[1], near_ref.shape[1]
    load_window(far_ref, near_ref, own_ref, win_ref)
    grad_ref[...] = jnp.zeros_like(grad_ref)
    dg = jnp.zeros((1, size), jnp.float32)
    for t in range(2):
        rows = slice(t * part, (t + 1) * part)
        window = slice(t * part, t * part + span)
        bias = mask_bias(qid_ref, kid_ref, t, part, span)
        keys = win_ref[window, :size]
        values = win_ref[window, size:]
        cosine, sine = cos_ref[0, rows, :], sin_ref[0, rows, :]
        query = q_ref[0, t]
        d_out = dmix_ref[0, t]
        scores = dot_nt(query, keys).reshape(heads, part, span)
        weights = jnp.exp(scores + bias[None]).reshape(heads * part, span)
        weights = weights * (1.0 / jnp.sum(weights, axis=-1, keepdims=True))
        mixed = jnp.concatenate(
            [mixed_ref[0, rows, head * size : (head + 1) * size] for head in range(heads)], axis=0
        )
        delta = jnp.sum(
            d_out.astype(jnp.float32) * mixed.astype(jnp.float32), axis=-1, keepdims=True
        )
        d_scores = (weights * (dot_nt(d_out, values) - delta)).astype(jnp.bfloat16)
        weights = weights.astype(jnp.bfloat16)
        grad_ref[window, :size] += dot_tn(d_scores, query)
        grad_ref[window, size:] += dot_tn(weights, d_out)
        d_query = dot_nn(d_scores, keys) * size ** (-0.5)
        d_raw, part_g = rms_back(
            qraw_ref[0, t].astype(jnp.float32),
            gq_ref[...],
            turn(d_query, stack_heads(cosine, heads), -stack_heads(sine, heads)),
        )
        d_raw = d_raw.astype(jnp.bfloat16)
        for head in range(heads):
            dqraw_ref[0, rows, head * size : (head + 1) * size] = d_raw[
                head * part : (head + 1) * part
            ]
        dg += part_g
    dg_ref[0] = dg
    dfar_ref[0] = grad_ref[:far, :].astype(jnp.bfloat16)
    dnear_ref[0] = grad_ref[far : far + near, :]
    down_ref[0] = grad_ref[far + near :, :]


def input_back_kernel(
    waits, own_ref, recv_ref, kraw_ref, cos_ref, sin_ref, wk_ref, wv_ref, dq_ref, wq_ref, x_ref, dhid_ref,
    gi_ref, gk_ref, *refs
):
    grad_ref, dpair_ref, dgi_ref, dgk_ref = refs[waits:]
    size = wk_ref.shape[0]
    total = own_ref[0] + recv_ref[0].astype(jnp.float32)
    d_key = turn(total[:, :size], cos_ref[0], -sin_ref[0])
    d_raw, dg_key = rms_back(kraw_ref[0].astype(jnp.float32), gk_ref[...], d_key)
    d_raw = d_raw.astype(jnp.bfloat16)
    d_value = total[:, size:].astype(jnp.bfloat16)
    dpair_ref[0, :, :size] = d_raw
    dpair_ref[0, :, size:] = d_value
    d_normed = dot_nn(dq_ref[0], wq_ref[...])
    d_normed += dot_nn(d_raw, wk_ref[...]) + dot_nn(d_value, wv_ref[...])
    d_x, dg_input = rms_back(x_ref[0].astype(jnp.float32), gi_ref[...], d_normed)
    grad_ref[0] = dhid_ref[0] + d_x
    dgi_ref[0] = dg_input
    dgk_ref[0] = dg_key


def flips(bit):
    return [(i, i ^ (1 << bit)) for i in range(lax.axis_size("dp"))]


def device_index():
    return lax.axis_index("dp")[None].astype(jnp.int32)


def side(bit):
    return (lax.axis_index("dp") >> bit) & 1


def stack_step(pairs, bits, done, arrived=()):
    axes = [sum(1 for other in before if other > bit) for bit, before in zip(bits, done)]
    anywhere = pl.BlockSpec(memory_space=pl.ANY)
    block = pl.BlockSpec(memory_space=pltpu.VMEM)
    arrived = list(arrived)
    shapes = [
        own.shape[:axis] + (2,) + own.shape[axis:] for (own, _), axis in zip(pairs, axes)
    ]
    return pl.pallas_call(
        functools.partial(stack_kernel, bits, axes, len(arrived)),
        out_shape=[jax.ShapeDtypeStruct(shape, jnp.bfloat16) for shape in shapes],
        in_specs=[pl.BlockSpec(memory_space=pltpu.SMEM)]
        + [block] * (2 * len(pairs))
        + [anywhere] * len(arrived),
        out_specs=[block] * len(pairs),
        compiler_params=pltpu.CompilerParams(vmem_limit_bytes=VMEM_BYTES),
    )(device_index(), *[array for pair in pairs for array in pair], *arrived)


class RowSum:
    def __init__(self, parts, order, axis):
        self.terms = [
            (part.reshape((2,) * len(order) + part.shape[1:]), list(range(len(order) - 1, -1, -1)))
            for part in parts
        ]
        self.join = axis
        self.order = order
        self.chosen = {}
        self.received = []

    @classmethod
    def from_halves(cls, keep, send, order):
        result = cls([], order, -1)
        shape = (2,) * (len(order) - 1) + keep.shape[1:]
        left = list(range(len(order) - 1, 0, -1))
        received = lax.ppermute(send, "dp", flips(0))
        result.terms = [(keep.reshape(shape), left)]
        result.received = [(received.reshape(shape), left)]
        result.chosen = {0: side(0)}
        result.sent = send
        return result

    def total(self, other=None):
        picks = dict(self.chosen)
        if other is not None:
            picks[other] = 1 - side(other)
        pieces = [self.pick(part, bits, picks) for part, bits in self.terms]
        value = jnp.concatenate(pieces, axis=self.join) if len(pieces) > 1 else pieces[0]
        value = value.astype(jnp.float32)
        for part, bits in self.received:
            value += self.pick(part, bits, picks).astype(jnp.float32)
        return value.astype(jnp.bfloat16)

    def ordered_total(self, after, other=None):
        gone = set(self.chosen) | ({other} if other is not None else set())
        left = [b for b in range(len(self.order) - 1, -1, -1) if b not in gone]
        terms = self.terms + self.received
        block = terms[0][0].shape[-2:]
        anywhere = pl.BlockSpec(memory_space=pl.ANY)

        def spec(bits):
            def place(g, index):
                flat = 0
                for bit in bits:
                    if bit in gone:
                        value = (index[0] >> bit) & 1
                        value = 1 - value if bit == other else value
                    else:
                        value = (g >> (len(left) - 1 - left.index(bit))) & 1
                    flat = 2 * flat + value
                return (flat, 0, 0)

            return pl.BlockSpec((1,) + block, place)

        count = 2 ** len(left)
        out = pl.pallas_call(
            functools.partial(sum_kernel, len(terms)),
            out_shape=jax.ShapeDtypeStruct((count,) + block, jnp.bfloat16),
            grid_spec=pltpu.PrefetchScalarGridSpec(
                num_scalar_prefetch=1,
                grid=(count,),
                in_specs=[spec(bits) for _, bits in terms] + [anywhere] * len(after),
                out_specs=pl.BlockSpec((1,) + block, lambda g, index: (g, 0, 0)),
            ),
            compiler_params=kernel_params(),
        )(device_index(), *[part.reshape((-1,) + block) for part, _ in terms], *after)
        return out.reshape((2,) * len(left) + block)

    def ordered_step(self, bit, after):
        self.sent = self.ordered_total(after, bit)
        self.receive(bit)

    def receive(self, bit):
        received = lax.ppermute(self.sent, "dp", flips(bit))
        self.chosen[bit] = side(bit)
        left = [b for b in range(len(self.order) - 1, -1, -1) if b not in self.chosen]
        self.received.append((received, left))
        return received

    def pick(self, part, bits, picks):
        bits = list(bits)
        for bit, where in picks.items():
            if bit in bits:
                part = lax.dynamic_index_in_dim(part, where, bits.index(bit), keepdims=False)
                bits.remove(bit)
        return part

    def send(self, bit):
        self.sent = self.total(bit)
        return self.sent

    def step(self, bit):
        self.send(bit)
        return self.receive(bit)


def seq_sum(part):
    count = lax.axis_size("seq")
    index = lax.axis_index("seq")
    half = count // 2
    terms = [part]

    def total():
        return sum(term.astype(jnp.float32) for term in terms)

    for t in range(half - 1):
        pairs = [(t, t + 1), (count - 1 - t, count - 2 - t)]
        terms.append(lax.ppermute(total().astype(jnp.bfloat16), "seq", pairs))
    middle = [(half - 1, half), (half, half - 1)]
    terms.append(lax.ppermute(total().astype(jnp.bfloat16), "seq", middle))
    result = total()
    for t in range(half - 2, -1, -1):
        pairs = [(t + 1, t), (count - 2 - t, count - 1 - t)]
        received = lax.ppermute(result.astype(jnp.bfloat16), "seq", pairs)
        outer = (index == t) | (index == count - 1 - t)
        result = jnp.where(outer, received.astype(jnp.float32), result)
    return result


def body(
    tokens,
    cotangent,
    segments,
    positions,
    query_weight,
    key_weight,
    value_weight,
    output_weight,
    gate_weight,
    up_weight,
    down_weight,
    norm_gains,
    query_first,
    key_first,
    value_first,
    output_first,
    gate_first,
    up_first,
    down_first,
    gains_first,
    query_second,
    key_second,
    value_second,
    output_second,
    gate_second,
    up_second,
    down_second,
    gains_second,
):
    count = lax.axis_size("dp")
    bits = (count - 1).bit_length()
    order_a = list(range(1, bits)) + [0]
    order_b = list(range(bits - 1, 0, -1)) + [0]
    low = jnp.bfloat16
    f32 = jnp.float32
    width = tokens.shape[2]
    key_rows = key_weight.shape[0]
    gain_rows = norm_gains.shape[0]
    rest_rows = 2 * key_rows + 16

    def array(shape, kind):
        return jax.ShapeDtypeStruct(shape, kind)

    query_rows = query_weight.shape[0]
    first_shard = pl.pallas_call(
        cast_first_kernel,
        out_shape=array((query_rows + rest_rows, width), low),
    )(query_weight, key_weight, value_weight, norm_gains[None])
    block = pl.BlockSpec(memory_space=pltpu.VMEM)
    anywhere = pl.BlockSpec(memory_space=pl.ANY)
    first_received = lax.ppermute(first_shard, "dp", flips(order_b[0]))
    pair_width = down_weight.shape[1] + output_weight.shape[1]
    pair_half_shape = array((down_weight.shape[0], pair_width // 2), low)
    shards_low = pl.pallas_call(
        functools.partial(cast_rest_kernel, 1),
        out_shape=[
            array(gate_weight.shape, low),
            array(up_weight.shape, low),
            pair_half_shape,
            pair_half_shape,
        ],
        in_specs=[block] * 4 + [anywhere],
    )(gate_weight, up_weight, down_weight, output_weight, first_received)
    rest_orders = [order_a, order_b, order_a, order_b]

    def rest_step(blocks, i):
        return [
            lax.ppermute(own, "dp", flips(order[i])) for own, order in zip(blocks, rest_orders)
        ]

    def rest_stack(blocks, received, i, arrived):
        return stack_step(
            list(zip(blocks, received)),
            [order[i] for order in rest_orders],
            [order[:i] for order in rest_orders],
            arrived,
        )

    (first_all,) = stack_step([(first_shard, first_received)], [order_b[0]], [[]])
    for i in range(1, bits):
        first_received = lax.ppermute(first_all, "dp", flips(order_b[i]))
        (first_all,) = stack_step(
            [(first_all, first_received)], [order_b[i]], [order_b[:i]], shards_low[:1]
        )
    first_all = first_all.reshape((count,) + first_shard.shape)
    rest_received = rest_step(shards_low, 0)
    key_start = query_rows + key_rows
    w_query = first_all[:, :query_rows].reshape(-1, width)
    w_key = first_all[:, query_rows:key_start].reshape(-1, width)
    w_value = first_all[:, key_start : key_start + key_rows].reshape(-1, width)
    gains_all = first_all[:, key_start + key_rows, :gain_rows].reshape(-1)
    seqs, rows, _ = tokens.shape
    size = w_key.shape[0]
    heads = w_query.shape[0] // size
    units = down_weight.shape[1]
    shards = lax.axis_size("seq")
    far = WINDOW - rows
    part = rows // 2
    span = part + WINDOW
    gains_float = gains_all.astype(jnp.float32)[None]
    g_input, g_attn, g_pre, g_ffn = (
        gains_float[:, i * width : (i + 1) * width] for i in range(4)
    )
    g_query = gains_float[:, 4 * width : 4 * width + size]
    g_key = gains_float[:, 4 * width + size : 4 * width + 2 * size]
    angles = positions.astype(jnp.float32)[..., None] * frequencies(size)
    cosine, sine = jnp.cos(angles), jnp.sin(angles)
    core_side = side(0)[None].astype(jnp.int32)
    first_row = lax.axis_index("seq") * rows
    padded = jnp.concatenate([jnp.full((seqs, WINDOW), -1, jnp.int32), segments], axis=1)
    window_ids = lax.dynamic_slice_in_dim(padded, first_row, WINDOW + rows, 1)
    query_ids = window_ids[:, WINDOW:, None]
    key_ids = jnp.stack([window_ids[:, :span], window_ids[:, part:]], axis=1)[:, :, None, :]

    def call(kernel, outs, out_specs, in_specs, scratch, flops, moved):
        return pl.pallas_call(
            kernel,
            grid=(seqs,),
            out_shape=outs,
            in_specs=in_specs,
            out_specs=out_specs,
            scratch_shapes=scratch,
            compiler_params=kernel_params(),
            cost_estimate=pl.CostEstimate(flops=flops, bytes_accessed=moved, transcendentals=0),
        )

    tokens_all = seqs * rows
    head_block = per_seq(2, heads * part, size)
    q_shape = (seqs, 2, heads * part, size)
    normed, pair_own, key_raw = call(
        functools.partial(project_pair_kernel, 6),
        [
            array((seqs, rows, width), low),
            array((seqs, rows, 2 * size), low),
            array((seqs, rows, size), low),
        ],
        [per_seq(rows, width), per_seq(rows, 2 * size), per_seq(rows, size)],
        [
            per_seq(rows, width),
            per_seq(rows, size // 2),
            per_seq(rows, size // 2),
            whole(*w_key.shape),
            whole(*w_value.shape),
            whole(1, width),
            whole(1, size),
        ]
        + [anywhere] * 6,
        [],
        4 * tokens_all * width * size,
        6_000_000,
    )(
        tokens, cosine, sine, w_key, w_value, g_input, g_key, query_ids, key_ids, *rest_received
    )
    upward = [(i, i + 1) for i in range(shards - 1)]
    pair_near = lax.ppermute(pair_own, "seq", upward)
    rest_blocks = rest_stack(shards_low, rest_received, 0, [pair_own])
    query, query_raw = call(
        functools.partial(project_query_kernel, heads, 1),
        [array(q_shape, low), array(q_shape, low)],
        [head_block, head_block],
        [
            per_seq(rows, width),
            per_seq(rows, size // 2),
            per_seq(rows, size // 2),
            whole(*w_query.shape),
            whole(1, size),
            anywhere,
        ],
        [],
        2 * tokens_all * width * heads * size,
        8_000_000,
    )(normed, cosine, sine, w_query, g_query, rest_blocks[0])

    far_send = pl.pallas_call(
        functools.partial(tail_rows_kernel, 1),
        out_shape=array((seqs, far, 2 * size), low),
        in_specs=[block, anywhere],
        out_specs=block,
        compiler_params=pltpu.CompilerParams(vmem_limit_bytes=VMEM_BYTES),
    )(pair_near, query)
    pair_far = lax.ppermute(far_send, "seq", upward[1:])
    for i in range(1, bits - 1):
        rest_blocks = rest_stack(rest_blocks, rest_step(rest_blocks, i), i, [pair_far])
    rest_blocks = [
        blocks.reshape((count // 2,) + blocks.shape[-2:]) for blocks in rest_blocks
    ]
    rest_received = [lax.ppermute(blocks, "dp", flips(0)) for blocks in rest_blocks]
    rest_operands = [array for pair in zip(rest_blocks, rest_received) for array in pair]

    window_specs = [
        per_seq(far, 2 * size),
        per_seq(rows, 2 * size),
        per_seq(rows, 2 * size),
        per_seq(rows, 1),
        per_seq(2, 1, span),
    ]
    attend_flops = 8 * tokens_all * heads * span * size
    mixed = call(
        functools.partial(attend_kernel, heads),
        array((seqs, rows, heads * size), low),
        per_seq(rows, heads * size),
        [head_block] + window_specs,
        [pltpu.VMEM((WINDOW + rows, 2 * size), low)],
        attend_flops,
        16_000_000,
    )(query, pair_far, pair_near, pair_own, query_ids, key_ids)

    (
        layer_output,
        pre_low,
        product_low,
        grad_down_low,
        grad_gate_low,
        grad_up_low,
        grad_attended_low,
        grad_hidden,
        grad_mixed,
        grad_gains_middle,
    ) = call(
        functools.partial(middle_kernel, heads, 512),
        [
            array((seqs, rows, width), low),
            array((seqs, rows, width), low),
            array((seqs, rows, units), low),
            array((seqs, rows, width), low),
            array((seqs, rows, units), low),
            array((seqs, rows, units), low),
            array((seqs, rows, width), low),
            array((seqs, rows, width), f32),
            array(q_shape, low),
            array((seqs, 3, width), f32),
        ],
        [
            per_seq(rows, width),
            per_seq(rows, width),
            per_seq(rows, units),
            per_seq(rows, width),
            per_seq(rows, units),
            per_seq(rows, units),
            per_seq(rows, width),
            per_seq(rows, width),
            head_block,
            per_seq(3, width),
        ],
        [
            pl.BlockSpec(memory_space=pltpu.SMEM),
            per_seq(rows, heads * size),
            per_seq(rows, width),
            per_seq(rows, width),
            anywhere,
            anywhere,
            anywhere,
            anywhere,
            anywhere,
            anywhere,
            anywhere,
            anywhere,
            whole(1, width),
            whole(1, width),
            whole(1, width),
        ],
        [
            pltpu.VMEM((rows, units), f32),
            pltpu.VMEM((rows, units), f32),
            pltpu.VMEM((count // 2, 2, 2 * gate_weight.shape[0], width), low),
            pltpu.VMEM((count // 2, 2, down_weight.shape[0], pair_width), low),
            pltpu.SemaphoreType.DMA((8,)),
        ],
        4 * tokens_all * width * (heads * size + 3 * units),
        40_000_000,
    )(
        core_side, mixed, tokens, cotangent, *rest_operands, g_attn, g_pre, g_ffn,
    )

    def flat(values):
        return values.reshape(tokens_all, values.shape[-1])

    def grad_blocks(gradient, inputs):
        product = weight_grad(flat(gradient), flat(inputs)).astype(low)
        return product.reshape(count, -1, product.shape[1])

    back_a = [0] + order_a[:-1]
    back_b = [0] + order_b[:-1]
    shard_units = gate_weight.shape[0]
    shard_rows = down_weight.shape[0]
    half = count // 2
    direct = shard_units % 128 == 0 and shard_rows % 16 == 0
    if direct:
        columns = 512
        first = units // columns
        last = heads * size // columns
        pair_block = pl.BlockSpec((half, shard_rows, columns), lambda k, side: (0, 0, k))
        pair_shape = array((half, shard_rows, units + heads * size), low)
        fixed = pl.BlockSpec(
            (tokens_all, width), lambda k, side: (0, 0), pipeline_mode=pl.Buffered(1)
        )
        pair_send, pair_keep = pl.pallas_call(
            functools.partial(pair_grad_kernel, first),
            out_shape=[pair_shape, pair_shape],
            grid_spec=pltpu.PrefetchScalarGridSpec(
                num_scalar_prefetch=1,
                grid=(first + last,),
                in_specs=[
                    pl.BlockSpec(
                        (tokens_all, columns), lambda k, side: (0, jnp.minimum(k, first - 1))
                    ),
                    pl.BlockSpec(
                        (tokens_all, columns), lambda k, side: (0, jnp.maximum(k - first, 0))
                    ),
                    fixed,
                    fixed,
                ],
                out_specs=[pair_block, pair_block],
                scratch_shapes=[
                    pltpu.VMEM((width, tokens_all), low),
                    pltpu.VMEM((width, columns), f32),
                ],
            ),
            compiler_params=kernel_params(),
            cost_estimate=pl.CostEstimate(
                flops=2 * tokens_all * width * (units + heads * size),
                bytes_accessed=13_000_000,
                transcendentals=0,
            ),
        )(core_side, flat(product_low), flat(mixed), flat(grad_down_low), flat(grad_attended_low))
        down_out_sum = RowSum.from_halves(pair_keep, pair_send, back_b)

        def shard_of(g, side):
            return (0, 2 * (g % half) + jnp.where(g < half, 1 - side[0], side[0]))

        block_shape = (1, 2 * shard_units, width)
        half_shape = array((half, 2 * shard_units, width), low)
        gate_up_send, gate_up_keep = pl.pallas_call(
            gate_up_grad_kernel,
            out_shape=[half_shape, half_shape],
            grid_spec=pltpu.PrefetchScalarGridSpec(
                num_scalar_prefetch=1,
                grid=(count,),
                in_specs=[
                    pl.BlockSpec((tokens_all, shard_units), shard_of),
                    pl.BlockSpec((tokens_all, shard_units), shard_of),
                    fixed,
                    anywhere,
                ],
                out_specs=[
                    pl.BlockSpec(block_shape, lambda g, side: (jnp.minimum(g, half - 1), 0, 0)),
                    pl.BlockSpec(block_shape, lambda g, side: (jnp.maximum(g - half, 0), 0, 0)),
                ],
            ),
            compiler_params=kernel_params(),
            cost_estimate=pl.CostEstimate(
                flops=4 * tokens_all * width * units, bytes_accessed=14_000_000, transcendentals=0
            ),
        )(core_side, flat(grad_gate_low), flat(grad_up_low), flat(pre_low), pair_send)
        gate_up_sum = RowSum.from_halves(gate_up_keep, gate_up_send, back_a)
    else:
        pair_blocks = jnp.concatenate(
            [grad_blocks(grad_down_low, product_low), grad_blocks(grad_attended_low, mixed)], axis=-1
        )
        down_out_sum = RowSum([pair_blocks], back_b, -1)
        down_out_sum.step(0)
        gate_up_blocks = jnp.concatenate(
            [grad_blocks(grad_gate_low, pre_low), grad_blocks(grad_up_low, pre_low)], axis=-2
        )
        gate_up_sum = RowSum([gate_up_blocks], back_a, -2)
        gate_up_sum.step(0)

    def at_seq(s, *tail):
        return pl.BlockSpec((1,) + tail, lambda g: (s,) + (0,) * len(tail))

    def seq_call(kernel, outs, out_specs, in_specs, operands, scratch, alias, flops):
        return pl.pallas_call(
            kernel,
            grid=(1,),
            out_shape=outs,
            in_specs=in_specs,
            out_specs=out_specs,
            scratch_shapes=scratch,
            input_output_aliases=alias,
            compiler_params=kernel_params(),
            cost_estimate=pl.CostEstimate(
                flops=flops, bytes_accessed=8_000_000, transcendentals=0
            ),
        )(*operands)

    def attend_back(s, buffer, arrived):
        kinds = [
            array((1, far, 2 * size), low),
            array((1, rows, 2 * size), f32),
            array((1, rows, 2 * size), f32),
            array((seqs, rows, heads * size), low),
            array((1, 1, size), f32),
        ]
        specs = [
            at_seq(0, far, 2 * size),
            at_seq(0, rows, 2 * size),
            at_seq(0, rows, 2 * size),
            at_seq(s, rows, heads * size),
            at_seq(0, 1, size),
        ]
        in_specs = [
            at_seq(s, 2, heads * part, size),
            at_seq(s, 2, heads * part, size),
            at_seq(s, far, 2 * size),
            at_seq(s, rows, 2 * size),
            at_seq(s, rows, 2 * size),
            at_seq(s, rows, 1),
            at_seq(s, 2, 1, span),
            at_seq(s, rows, heads * size),
            at_seq(s, 2, heads * part, size),
            at_seq(s, rows, size // 2),
            at_seq(s, rows, size // 2),
            whole(1, size),
        ]
        operands = [
            query, query_raw, pair_far, pair_near, pair_own, query_ids, key_ids, mixed, grad_mixed,
            cosine, sine, g_query,
        ]
        alias = {}
        extra = list(arrived)
        if buffer is not None:
            alias = {len(operands): 3}
            extra = [buffer] + extra
        return seq_call(
            functools.partial(attend_back_kernel, heads, len(extra)),
            kinds,
            specs,
            in_specs + [anywhere] * len(extra),
            operands + extra,
            [
                pltpu.VMEM((WINDOW + rows, 2 * size), low),
                pltpu.VMEM((WINDOW + rows, 2 * size), f32),
            ],
            alias,
            attend_flops * 3 // seqs,
        )

    downward = [(i + 1, i) for i in range(shards - 1)]
    grad_query_low = None
    arrived = [gate_up_sum.sent]

    def near_total(grad_near, from_far, after):
        return pl.pallas_call(
            functools.partial(near_sum_kernel, len(after)),
            out_shape=array(grad_near.shape, low),
            in_specs=[block] * 2 + [anywhere] * len(after),
            out_specs=block,
        )(grad_near, from_far, *after)

    own_parts, query_gains, near_sums, far_parts, near_parts = [], [], [], [], []
    for s in range(seqs):
        grad_far, grad_near, grad_own, grad_query_low, g_part = attend_back(
            s, grad_query_low, arrived
        )
        from_far = lax.ppermute(grad_far, "seq", downward[1:])
        own_parts.append(grad_own)
        query_gains.append(g_part)
        far_parts.append(from_far)
        near_parts.append(grad_near)
        if s == 0:
            down_out_sum.ordered_step(back_b[1], [grad_own])
            gate_up_sum.ordered_step(back_a[1], [down_out_sum.sent])
            arrived = [gate_up_sum.sent]
        elif s == 1:
            near_sums.append(near_total(near_parts[0], far_parts[0], [grad_own]))
            arrived = [near_sums[0]]
    for bit in back_b[2:]:
        down_out_sum.ordered_step(bit, [own_parts[-1]])
    near_sums.append(near_total(near_parts[1], far_parts[1], [down_out_sum.sent]))
    query_columns = heads * size
    grad_w_query = pl.pallas_call(
        functools.partial(query_grad_kernel, 2),
        grid=(heads,),
        out_shape=array((query_columns, width), low),
        in_specs=[
            pl.BlockSpec((tokens_all, size), lambda i: (0, i)),
            whole(tokens_all, width),
            anywhere,
            anywhere,
        ],
        out_specs=pl.BlockSpec((size, width), lambda i: (i, 0)),
        compiler_params=kernel_params(),
        cost_estimate=pl.CostEstimate(
            flops=2 * tokens_all * width * query_columns, bytes_accessed=5_000_000, transcendentals=0
        ),
    )(flat(grad_query_low), flat(normed), near_sums[1], down_out_sum.sent)
    near_sums.append(near_total(near_parts[2], far_parts[2], [grad_w_query]))
    from_near = [lax.ppermute(near_sum, "seq", downward) for near_sum in near_sums]
    for bit in back_a[2:]:
        gate_up_sum.ordered_step(bit, [near_sums[2]])

    def input_back(s, buffers, arrived):
        kinds = [
            array((seqs, rows, width), f32),
            array((seqs, rows, 2 * size), low),
            array((1, 1, width), f32),
            array((1, 1, size), f32),
        ]
        specs = [
            at_seq(s, rows, width),
            at_seq(s, rows, 2 * size),
            at_seq(0, 1, width),
            at_seq(0, 1, size),
        ]
        in_specs = [
            at_seq(0, rows, 2 * size),
            at_seq(0, rows, 2 * size),
            at_seq(s, rows, size),
            at_seq(s, rows, size // 2),
            at_seq(s, rows, size // 2),
            whole(*w_key.shape),
            whole(*w_value.shape),
            at_seq(s, rows, heads * size),
            whole(*w_query.shape),
            at_seq(s, rows, width),
            at_seq(s, rows, width),
            whole(1, width),
            whole(1, size),
        ]
        operands = [
            own_parts[s], from_near[s], key_raw, cosine, sine, w_key, w_value, grad_query_low,
            w_query, tokens, grad_hidden, g_input, g_key,
        ]
        alias = {}
        extra = list(arrived)
        if buffers:
            alias = {len(operands): 0, len(operands) + 1: 1}
            extra = list(buffers) + extra
        return seq_call(
            functools.partial(input_back_kernel, len(extra)),
            kinds,
            specs,
            in_specs + [anywhere] * len(extra),
            operands + extra,
            [],
            alias,
            2 * rows * width * size * (heads + 2),
        )

    buffers = []
    input_gains, key_gains = [], []
    for s in range(seqs):
        waits = [gate_up_sum.sent]
        if s == seqs - 1:
            down_out_part = down_out_sum.ordered_total([buffers[0]])
            waits = [down_out_part]
        *buffers, g_part, g_key_part = input_back(s, buffers, waits)
        input_gains.append(g_part)
        key_gains.append(g_key_part)
    input_grad, grad_pair_low = buffers
    key_value_blocks = grad_blocks(grad_pair_low, normed).reshape(2, count, key_rows, width)
    grad_gains = jnp.concatenate(
        [
            sum(input_gains).reshape(-1),
            jnp.sum(grad_gains_middle, axis=0).reshape(-1),
            sum(query_gains).reshape(-1),
            sum(key_gains).reshape(-1),
        ]
    )
    gain_block = jnp.pad(
        grad_gains.astype(low).reshape(count, 1, gain_rows),
        ((0, 0), (0, 15), (0, width - gain_rows)),
    )
    rest_sum = RowSum(
        [
            grad_w_query.reshape(count, query_rows, width),
            key_value_blocks[0],
            key_value_blocks[1],
            gain_block,
        ],
        back_b,
        -2,
    )
    rest_sum.step(back_b[0])
    gate_up_part = gate_up_sum.ordered_total([rest_sum.sent])
    for bit in back_b[1:]:
        rest_sum.step(bit)
    down_out_total = seq_sum(down_out_part)
    gate_total = seq_sum(gate_up_part[:shard_units])
    up_total = seq_sum(gate_up_part[shard_units:])
    rest_total = seq_sum(rest_sum.total())
    query_total = rest_total[:query_rows]
    rest_total = rest_total[query_rows:]
    down_total = down_out_total[:, :units]
    output_total = down_out_total[:, units:]
    key_total = rest_total[:key_rows]
    value_total = rest_total[key_rows : 2 * key_rows]
    gains_total = rest_total[2 * key_rows, :gain_rows]
    query_momentum, query_variance, query_updated = adam_step(
        query_weight, query_first, query_second, query_total, WEIGHT_DECAY
    )
    key_momentum, key_variance, key_updated = adam_step(
        key_weight, key_first, key_second, key_total, WEIGHT_DECAY
    )
    value_momentum, value_variance, value_updated = adam_step(
        value_weight, value_first, value_second, value_total, WEIGHT_DECAY
    )
    output_momentum, output_variance, output_updated = adam_step(
        output_weight, output_first, output_second, output_total, WEIGHT_DECAY
    )
    gate_momentum, gate_variance, gate_updated = adam_step(
        gate_weight, gate_first, gate_second, gate_total, WEIGHT_DECAY
    )
    up_momentum, up_variance, up_updated = adam_step(
        up_weight, up_first, up_second, up_total, WEIGHT_DECAY
    )
    down_momentum, down_variance, down_updated = adam_step(
        down_weight, down_first, down_second, down_total, WEIGHT_DECAY
    )
    gains_momentum, gains_variance, gains_updated = adam_step(
        norm_gains, gains_first, gains_second, gains_total, 0.0
    )
    return (
        layer_output,
        input_grad,
        query_momentum,
        key_momentum,
        value_momentum,
        output_momentum,
        gate_momentum,
        up_momentum,
        down_momentum,
        gains_momentum,
        query_variance,
        key_variance,
        value_variance,
        output_variance,
        gate_variance,
        up_variance,
        down_variance,
        gains_variance,
        query_updated,
        key_updated,
        value_updated,
        output_updated,
        gate_updated,
        up_updated,
        down_updated,
        gains_updated,
    )


def solution(mesh):
    return jax.shard_map(
        body,
        mesh=mesh,
        in_specs=(
            P("dp", "seq", None),
            P("dp", "seq", None),
            P("dp", None),
            P("dp", "seq"),
            P("dp", None),
            P("dp", None),
            P("dp", None),
            P("dp", None),
            P("dp", None),
            P("dp", None),
            P("dp", None),
            P("dp"),
            P("dp", None),
            P("dp", None),
            P("dp", None),
            P("dp", None),
            P("dp", None),
            P("dp", None),
            P("dp", None),
            P("dp"),
            P("dp", None),
            P("dp", None),
            P("dp", None),
            P("dp", None),
            P("dp", None),
            P("dp", None),
            P("dp", None),
            P("dp"),
        ),
        out_specs=(
            P("dp", "seq", None),
            P("dp", "seq", None),
            P("dp", None),
            P("dp", None),
            P("dp", None),
            P("dp", None),
            P("dp", None),
            P("dp", None),
            P("dp", None),
            P("dp"),
            P("dp", None),
            P("dp", None),
            P("dp", None),
            P("dp", None),
            P("dp", None),
            P("dp", None),
            P("dp", None),
            P("dp"),
            P("dp", None),
            P("dp", None),
            P("dp", None),
            P("dp", None),
            P("dp", None),
            P("dp", None),
            P("dp", None),
            P("dp"),
        ),
        check_vma=False,
    )
```
